32 devices in a mesh: seq: 8 (over y, x, core), head: 4 (over z).
Axes of the slice: x: 2, y: 2, z: 4, core: 2. Of those that a mesh axis runs over, the one named last changes fastest.
Arguments:
- tokens: bfloat16 [16, 512, 1024], P('seq', 'head'), may hold values from -6 to 6
- doc_lengths: int32 [16, 3], P('seq'), may hold values from 1 to 128, as said below
- pad_counts: int32 [16], P('seq'), may hold values from 0 to 64
- w_query: bfloat16 [1024, 1024], replicated, may hold values from -0.1875 to 0.1875
- w_key: bfloat16 [1024, 1024], replicated, may hold values from -0.1875 to 0.1875
- w_value: bfloat16 [1024, 1024], replicated, may hold values from -0.1875 to 0.1875
- w_out: bfloat16 [1024, 1024], replicated, may hold values from -2 to 2
- w_inner: bfloat16 [1024, 4096], replicated, may hold values from -0.1875 to 0.1875
- w_outer: bfloat16 [4096, 1024], replicated, may hold values from -0.09375 to 0.09375
- bias_query: float32 [1024], replicated, may hold values from -3 to 3
- bias_value: float32 [1024], replicated, may hold values from -3 to 3
- bias_out: float32 [1024], replicated, may hold values from -3 to 3
- bias_inner: float32 [4096], replicated, may hold values from -3 to 3
- bias_outer: float32 [1024], replicated, may hold values from -3 to 3
- gain_attn: float32 [1024], replicated, may hold values from 0.5 to 1.5
- beta_attn: float32 [1024], replicated, may hold values from -3 to 3
- gain_final: float32 [1024], replicated, may hold values from 0.5 to 1.5
- beta_final: float32 [1024], replicated, may hold values from -3 to 3
- cotangent: bfloat16 [16, 512, 1024], P('seq', 'head'), may hold values from -6 to 6
Outputs:
- layer_out: bfloat16 [16, 512, 1024], P('seq', 'head')
- input_grad: float32 [16, 512, 1024], P('seq', 'head')
- grad_bias_query: float32 [1024], replicated
- grad_bias_value: float32 [1024], replicated
- grad_bias_out: float32 [1024], replicated
- grad_bias_inner: float32 [4096], replicated
- grad_bias_outer: float32 [1024], replicated
- grad_beta_attn: float32 [1024], replicated
- grad_beta_final: float32 [1024], replicated
The draws below stay inside these ranges and needn't reach their ends.
Inputs may be any that keep to these rules, and one draw needn't show every extreme that they name: `doc_lengths`: lengths of the first 3 documents of a row, in order; the row's last document takes the remaining slots before its padding.
All inputs are finite; a program needn't handle non-finite values.
Results may differ from the reference program's by a relative error of at most 0.012.
Values may be sent and summed in bfloat16 or wider, within the bound.
A program may use at most 128 MiB of HBM per device.

```python
import math
import jax
import jax.numpy as jnp
from jax import lax

D = 1024
HEADS = 16
FF = 4096
SLOTS = 512
DOCS = 4
DOC_MAX = 128
PAD_MAX = 64
ROWS_DEV = 2
ROWS = 16


def chosen_rows(key):
    group_count = ROWS // ROWS_DEV
    chosen = jax.random.randint(key, (group_count,), 0, ROWS_DEV)
    inside = jnp.arange(ROWS_DEV, dtype=jnp.int32)
    spanning = (inside[None, :] == chosen[:, None]).reshape(ROWS)
    fullest = (inside[None, :] == (chosen[:, None] + 1) % ROWS_DEV).reshape(ROWS)
    return (spanning, fullest)


def draw_doc_lengths(key, part):
    spanning, fullest = chosen_rows(key)
    key = jax.random.fold_in(key, 11)
    lengths = jax.random.randint(key, (ROWS, DOCS - 1), 1, DOC_MAX + 1)
    lengths = jnp.where(spanning[:, None], 1, lengths)
    first_column = jnp.arange(DOCS - 1)[None, :] == 0
    lengths = jnp.where(fullest[:, None] & first_column, DOC_MAX, lengths)
    return lengths.astype(jnp.int32)


def draw_pad_counts(key, part):
    spanning, fullest = chosen_rows(key)
    key = jax.random.fold_in(key, 23)
    padding = jax.random.randint(key, (ROWS,), 0, PAD_MAX + 1)
    padding = jnp.where(spanning, 0, padding)
    padding = jnp.where(fullest, PAD_MAX, padding)
    return padding.astype(jnp.int32)


def block_scale(rng, extent, cuts, low, largest):
    def one(axis_at, shards_of):
        steps = jax.random.uniform(jax.random.fold_in(jax.random.fold_in(rng, 6), axis_at), (shards_of,), jnp.float32, low / len(cuts), largest / len(cuts))
        return jnp.repeat(jnp.exp(steps), extent[axis_at] // shards_of).reshape((-1,) + (1,) * (len(extent) - axis_at - 1))

    loudness = one(*cuts[0])
    for cut in cuts[1:]:
        loudness = loudness * one(*cut)
    return loudness


def gaussian(stream_key, dims, width, bound, cuts=(), kind=jnp.bfloat16):
    entries = jax.random.normal(stream_key, dims, jnp.float32) * width
    if len(cuts) > 0:
        entries = block_scale(stream_key, dims, cuts, -0.22, 0.18) * entries
    return jnp.clip(entries, min=-bound, max=bound).astype(kind)


def setup_inputs(seed: int = 0) -> dict:
    key_of = jax.random.split(jax.random.key(seed), 20)
    tokens = gaussian(key_of[0], (ROWS, SLOTS, D), 1.0, 6.0, ((0, 8), (1, 4)))
    doc_lengths = draw_doc_lengths(jax.random.fold_in(key_of[19], 71), 0)
    pad_counts = draw_pad_counts(jax.random.fold_in(key_of[19], 71), 0)
    w_query = gaussian(key_of[3], (D, D), D ** -0.5, 0.1875)
    w_key = gaussian(key_of[4], (D, D), D ** -0.5, 0.1875)
    w_value = gaussian(key_of[5], (D, D), D ** -0.5, 0.1875)
    w_out = gaussian(key_of[6], (D, D), (max(D // 96, 1)) ** -0.5, 2.0)
    w_inner = gaussian(key_of[7], (D, FF), D ** -0.5, 0.1875)
    w_outer = gaussian(key_of[8], (FF, D), FF ** -0.5, 0.09375)
    bias_query = gaussian(key_of[9], (D,), 0.5, 3.0, (), jnp.float32)
    bias_value = gaussian(key_of[10], (D,), 0.5, 3.0, (), jnp.float32)
    bias_out = gaussian(key_of[11], (D,), 0.5, 3.0, (), jnp.float32)
    bias_inner = gaussian(key_of[12], (FF,), 0.5, 3.0, (), jnp.float32)
    bias_outer = gaussian(key_of[13], (D,), 0.5, 3.0, (), jnp.float32)
    gain_attn = jnp.clip(1.0 + 0.1 * jax.random.normal(key_of[14], (D,), jnp.float32), 0.5, 1.5)
    beta_attn = gaussian(key_of[15], (D,), 0.5, 3.0, (), jnp.float32)
    gain_final = jnp.clip(1.0 + 0.1 * jax.random.normal(key_of[16], (D,), jnp.float32), 0.5, 1.5)
    beta_final = gaussian(key_of[17], (D,), 0.5, 3.0, (), jnp.float32)
    cotangent = gaussian(key_of[18], (ROWS, SLOTS, D), 1.0, 6.0, ((0, 8), (1, 4)))
    return {"tokens": tokens, "doc_lengths": doc_lengths, "pad_counts": pad_counts, "w_query": w_query, "w_key": w_key, "w_value": w_value, "w_out": w_out, "w_inner": w_inner, "w_outer": w_outer, "bias_query": bias_query, "bias_value": bias_value, "bias_out": bias_out, "bias_inner": bias_inner, "bias_outer": bias_outer, "gain_attn": gain_attn, "beta_attn": beta_attn, "gain_final": gain_final, "beta_final": beta_final, "cotangent": cotangent}


EPS = 1e-06
NEG = -1000000000.0

@jax.custom_vjp
def low(v):
    return lax.optimization_barrier(v.astype(jnp.bfloat16)).astype(jnp.float32)

@jax.custom_vjp
def low_back(v):
    return v

def low_keep(v):
    return (low(v), None)

def low_pass(kept, grad):
    return (grad,)

def back_keep(v):
    return (v, None)

def back_low(kept, grad):
    return (low(grad),)
low.defvjp(low_keep, low_pass)
low_back.defvjp(back_keep, back_low)

def matmul(left, right):
    return jnp.einsum('rsd,de->rse', left, right, precision=lax.Precision.HIGHEST)

def layer_norm(hidden):
    row_mean = lax.optimization_barrier(jnp.mean(hidden, axis=-1, keepdims=True))
    centred = hidden - row_mean
    return centred * lax.rsqrt(lax.optimization_barrier(jnp.mean(centred * centred, axis=-1, keepdims=True)) + EPS)

def document_ids(doc_lengths, pad_counts, slot_count):
    position = jnp.arange(slot_count).astype(jnp.int32)
    doc_ends = jnp.cumsum(doc_lengths, axis=1, dtype=jnp.int32)
    inside = lax.optimization_barrier(jnp.sum((position[None, :, None] >= doc_ends[:, None, :]).astype(jnp.int32), axis=-1, dtype=jnp.int32))
    return inside + (position[None, :] >= slot_count - pad_counts[:, None]).astype(jnp.int32)

def reference(tokens, doc_lengths, pad_counts, w_query, w_key, w_value, w_out, w_inner, w_outer, bias_query, bias_value, bias_out, bias_inner, bias_outer, gain_attn, beta_attn, gain_final, beta_final, cotangent):
    head_width = D // HEADS
    score_scale = head_width ** (-0.5)
    query_matrix = w_query.astype(jnp.float32)
    key_matrix = w_key.astype(jnp.float32)
    value_matrix = w_value.astype(jnp.float32)
    out_matrix = w_out.astype(jnp.float32)
    inner_matrix = w_inner.astype(jnp.float32)
    outer_matrix = w_outer.astype(jnp.float32)
    doc_ids = document_ids(doc_lengths, pad_counts, SLOTS)
    position = jnp.arange(SLOTS).astype(jnp.int32)
    live_mask = (position[None, :] < SLOTS - pad_counts[:, None]).astype(jnp.float32)
    block_rows = math.gcd(ROWS, 4)
    block_count = ROWS // block_rows

    def block_step(carry, pieces):
        token_block, doc_block, live_block, cot_block = pieces
        same_doc = doc_block[:, :, None] == doc_block[:, None, :]

        def heads_of(matrix):
            return matrix.reshape(block_rows, SLOTS, HEADS, head_width)

        def forward(token_float, query_bias, value_bias, out_bias, inner_bias, outer_bias, attn_beta, final_beta):
            queries = low_back(low(matmul(token_float, query_matrix) + query_bias))
            key_rows = low_back(low(matmul(token_float, key_matrix)))
            value_rows = low_back(low(matmul(token_float, value_matrix) + value_bias))
            raw_scores = low_back(jnp.einsum('rqhd,rkhd->rhqk', heads_of(queries), heads_of(key_rows), precision=lax.Precision.HIGHEST) * score_scale)
            masked = jnp.where(same_doc[:, None], raw_scores, NEG)
            exponent = jnp.exp(masked - lax.optimization_barrier(jnp.max(masked, axis=-1, keepdims=True)))
            attn_probs = exponent / lax.optimization_barrier(jnp.sum(exponent, axis=-1, keepdims=True))
            mixed_rows = jnp.einsum('rhqk,rkhd->rqhd', low(attn_probs), heads_of(value_rows), precision=lax.Precision.HIGHEST)
            attended = low_back(low(mixed_rows.reshape(block_rows, SLOTS, D)))
            hidden_attn = token_float + low_back(matmul(attended, out_matrix)) + out_bias
            middle = layer_norm(hidden_attn) * gain_attn + attn_beta
            inner = low_back(matmul(low(middle), inner_matrix) + inner_bias)
            active = low(jax.nn.gelu(inner, approximate=False))
            hidden_final = middle + low_back(matmul(active, outer_matrix)) + outer_bias
            return live_block[..., None] * (layer_norm(hidden_final) * gain_final + final_beta)
        out_block, pullback = jax.vjp(forward, token_block.astype(jnp.float32), bias_query, bias_value, bias_out, bias_inner, bias_outer, beta_attn, beta_final)
        gradients = pullback(cot_block.astype(jnp.float32))
        carry = tuple((running + gradient for running, gradient in zip(carry, gradients[1:])))
        return (carry, (out_block, gradients[0]))
    start = tuple((jnp.zeros_like(vector) for vector in (bias_query, bias_value, bias_out, bias_inner, bias_outer, beta_attn, beta_final)))
    pieces = (tokens.reshape(block_count, block_rows, SLOTS, D), doc_ids.reshape(block_count, block_rows, SLOTS), live_mask.reshape(block_count, block_rows, SLOTS), cotangent.reshape(block_count, block_rows, SLOTS, D))
    sums, (outputs, input_grads) = lax.scan(block_step, start, pieces)
    layer_out = outputs.reshape(ROWS, SLOTS, D).astype(jnp.bfloat16)
    input_grad = input_grads.reshape(ROWS, SLOTS, D)
    return (layer_out, input_grad, sums[0], sums[1], sums[2], sums[3], sums[4], sums[5], sums[6])
```

```python
import functools

import jax
import jax.numpy as jnp
from jax import lax
from jax.experimental import pallas as pl
from jax.experimental.pallas import tpu as pltpu
from jax.sharding import PartitionSpec as P

HEADS = 16
LANES = 128
EPS = 1e-06
BIG = 2.0**30
FF_CHUNK = 512
NORM_ROWS = 32
MESH = pl.DeviceIdType.MESH
F32 = jnp.float32
BF16 = jnp.bfloat16


def dot(left, right):
    return lax.dot_general(left, right, (((1,), (0,)), ((), ())), preferred_element_type=F32)


def dot_nt(left, right):
    return lax.dot_general(left, right, (((1,), (1,)), ((), ())), preferred_element_type=F32)


def dot_tn(left, right):
    return lax.dot_general(left, right, (((0,), (0,)), ((), ())), preferred_element_type=F32)


def normed(hidden):
    row_mean = jnp.mean(hidden, axis=-1, keepdims=True)
    centred = hidden - row_mean
    inv_std = lax.rsqrt(jnp.mean(centred * centred, axis=-1, keepdims=True) + EPS)
    return centred * inv_std, inv_std


def norm_back(gradient, norm, inv_std):
    return inv_std * (
        gradient
        - jnp.mean(gradient, axis=-1, keepdims=True)
        - norm * jnp.mean(gradient * norm, axis=-1, keepdims=True)
    )


def fold_rows(block):
    total = block[0:8]
    for start in range(8, block.shape[0], 8):
        total = total + block[start : start + 8]
    return total


def kernel(
    seq_size,
    group,
    tokens,
    cotangent,
    doc_lengths,
    pad_counts,
    w_query,
    w_key,
    w_value,
    w_out,
    w_inner,
    w_outer,
    bias_query,
    bias_value,
    bias_out,
    bias_inner,
    bias_outer,
    gain_attn,
    beta_attn,
    gain_final,
    beta_final,
    layer_home,
    grad_home,
    sums_a,
    sums_b,
    m_qkv,
    m_out,
    m_inner,
    m_outer,
    row,
    cot,
    info,
    qs,
    ks,
    vs,
    exps,
    recip,
    mixed,
    att,
    att_far,
    norm_a,
    inv_a,
    mid,
    mid_low,
    acc,
    slope,
    grad_h,
    grad_low,
    grad_att,
    grad_far,
    grad_qkv,
    part_out,
    part_in,
    grad_out,
    layer_out,
    pool_a,
    z_a,
    pool_b,
    z_b,
    w_sem,
    in_sem,
    tok_send,
    tok_recv,
    pass_send,
    pass_recv,
    info_sem,
    cot_send,
    cot_recv,
    att_send,
    att_recv,
    gat_send,
    gat_recv,
    lay_send,
    lay_recv,
    part_sem,
    grad_send,
    grad_recv,
    pa_send,
    pa_recv,
    za_send,
    za_recv,
    pb_send,
    pb_recv,
    zb_send,
    zb_recv,
):
    rows, span, width = tokens.shape
    half_blocks = group // 2
    slots = span * group
    half = slots // 2
    head_width = width // HEADS
    side = width // 2
    pairs = side // LANES
    chunks = m_inner.shape[0]
    score_scale = head_width**-0.5

    seq = lax.axis_index("seq")
    z = lax.axis_index("head")
    core = lax.rem(seq, 2)
    base = seq - core
    partner = base + 1 - core
    z_half = z // half_blocks
    far = 1 - core

    def rows_of(block):
        return pl.ds(pl.multiple_of(block * span, span), span)

    def remote(src, dst, send_sem, recv_sem, at_seq, at_head):
        return pltpu.make_async_remote_copy(
            src_ref=src,
            dst_ref=dst,
            send_sem=send_sem,
            recv_sem=recv_sem,
            device_id=(at_seq, at_head),
            device_id_type=MESH,
        )

    barrier = pltpu.get_barrier_semaphore()

    def greet_z(step, carry):
        pl.semaphore_signal(
            barrier, inc=1, device_id=(seq, lax.rem(z + step, group)), device_id_type=MESH
        )
        return carry

    def greet_seq(step, carry):
        pl.semaphore_signal(
            barrier, inc=1, device_id=(lax.rem(seq + step, seq_size), z), device_id_type=MESH
        )
        return carry

    for r in range(rows):
        target = core * rows + r

        @pl.when(target != z)
        def _():
            pl.semaphore_signal(
                barrier, inc=1, device_id=(base + z_half, target), device_id_type=MESH
            )

    lax.fori_loop(1, seq_size, greet_seq, 0)
    lax.fori_loop(1, group, greet_z, 0)

    mine = pl.ds(pl.multiple_of(core * side, side), side)
    theirs = pl.ds(pl.multiple_of(far * side, side), side)
    qkv_copies = [
        pltpu.make_async_copy(
            weight.at[:, mine], m_qkv.at[:, i * side : (i + 1) * side], w_sem.at[i]
        )
        for i, weight in enumerate((w_query, w_key, w_value))
    ]
    for copy in qkv_copies:
        copy.start()
    out_copies = [
        pltpu.make_async_copy(w_out.at[mine], m_out.at[0:side], w_sem.at[3]),
        pltpu.make_async_copy(w_out.at[theirs], m_out.at[side:width], w_sem.at[4]),
    ]

    def inner_copy(f):
        columns = pl.ds(pl.multiple_of(f * FF_CHUNK, FF_CHUNK), FF_CHUNK)
        return pltpu.make_async_copy(w_inner.at[:, columns], m_inner.at[f], w_sem.at[5 + f])

    def outer_copy(f):
        lines = pl.ds(pl.multiple_of(f * FF_CHUNK, FF_CHUNK), FF_CHUNK)
        return pltpu.make_async_copy(w_outer.at[lines], m_outer.at[f], w_sem.at[5 + chunks + f])

    line = lax.broadcasted_iota(jnp.int32, (8, LANES), 0)
    for r in range(rows):
        first = doc_lengths[r, 0]
        second = first + doc_lengths[r, 1]
        third = second + doc_lengths[r, 2]
        ends = jnp.where(line == 0, first, jnp.where(line == 1, second, third))
        info[core, r] = jnp.where(line == 3, slots - pad_counts[r], ends)

    peers = jnp.where(z_half == core, rows - 1, rows)
    pl.semaphore_wait(barrier, peers + seq_size - 1 + group - 1)

    def spread(source, target_ref, at, send_sem, recv_sem, local_sem):
        for r in range(rows):
            target = core * rows + r

            @pl.when(target != z)
            def _():
                remote(
                    source.at[r],
                    target_ref.at[at],
                    send_sem.at[r],
                    recv_sem.at[z - z_half * half_blocks],
                    base + z_half,
                    target,
                ).start()

            @pl.when(target == z)
            def _():
                pltpu.make_async_copy(source.at[r], target_ref.at[at], local_sem).start()

    def spread_done(source, target_ref, at, send_sem, recv_sem):
        for r in range(rows):
            target = core * rows + r

            @pl.when(target != z)
            def _():
                remote(
                    source.at[r],
                    target_ref.at[at],
                    send_sem.at[r],
                    recv_sem.at[z - z_half * half_blocks],
                    base + z_half,
                    target,
                ).wait_send()

    def arrived(source, target_ref, at, block, send_sem, recv_sem, local_sem):
        j = block - core * half_blocks

        @pl.when(block != z)
        def _():
            remote(
                source.at[0],
                target_ref.at[at],
                send_sem.at[0],
                recv_sem.at[j],
                base + z_half,
                block,
            ).wait_recv()

        @pl.when(block == z)
        def _():
            pltpu.make_async_copy(source.at[0], target_ref.at[at], local_sem).wait()

    info_copy = remote(info.at[core], info.at[core], info_sem.at[0], info_sem.at[1], partner, z)
    info_copy.start()
    spread(tokens, row, rows_of(z), tok_send, tok_recv, in_sem.at[0])
    for copy in out_copies:
        copy.start()

    def start_inner(f, carry):
        inner_copy(f).start()
        outer_copy(f).start()
        return carry

    lax.fori_loop(0, chunks, start_inner, 0)

    info_copy.wait_send()
    remote(info.at[far], info.at[far], info_sem.at[0], info_sem.at[1], partner, z).wait_recv()
    for copy in qkv_copies:
        copy.wait()

    lane = lax.broadcasted_iota(jnp.int32, (slots, LANES), 1)
    slot = lax.broadcasted_iota(jnp.int32, (slots, LANES), 0)
    ends = info[z_half, z - z_half * rows]
    doc = (slot >= ends[0:1]).astype(jnp.int32)
    for i in range(1, 4):
        doc = doc + (slot >= ends[i : i + 1]).astype(jnp.int32)
    doc_query = jnp.where(doc == lane, BIG, 0.0).astype(BF16)
    doc_key = jnp.where((doc != lane) & (lane < 5), -1.0, 0.0).astype(BF16)
    ones = jnp.ones((slots, LANES), BF16)

    def pass_on(block):
        j = block - core * half_blocks
        at = rows_of(block)
        return remote(row.at[at], row.at[at], pass_send.at[j], pass_recv.at[j], partner, z)

    def project(step, carry):
        near = step < half_blocks
        within = lax.rem(z - z_half * half_blocks + step, half_blocks)
        other = step - half_blocks
        beyond = jnp.where(z_half == 0, half_blocks + other, half_blocks - 1 - other)
        block = jnp.where(near, z_half * half_blocks + within, beyond)
        block_half = block // half_blocks
        at = rows_of(block)

        @pl.when(block_half == core)
        def _():
            arrived(tokens, row, at, block, tok_send, tok_recv, in_sem.at[0])
            pass_on(block).start()

        @pl.when(block_half != core)
        def _():
            j = block - far * half_blocks
            remote(
                row.at[at], row.at[at], pass_send.at[j], pass_recv.at[j], partner, z
            ).wait_recv()

        x = row[at, :]
        q = (dot(x, m_qkv[:, 0:side]) + bias_query[:, mine]) * score_scale
        k = dot(x, m_qkv[:, side : 2 * side])
        v = dot(x, m_qkv[:, 2 * side : 3 * side]) + bias_value[:, mine]
        for p in range(pairs):
            cut = slice(p * LANES, (p + 1) * LANES)
            qs[p, at, :] = q[:, cut].astype(BF16)
            ks[p, at, :] = k[:, cut].astype(BF16)
            vs[p, at, :] = v[:, cut].astype(BF16)
        return carry

    lax.fori_loop(0, group, project, 0)
    spread_done(tokens, row, rows_of(z), tok_send, tok_recv)

    cot_at = pl.ds(pl.multiple_of((z - z_half * half_blocks) * span, span), span)
    spread(cotangent, cot, cot_at, cot_send, cot_recv, in_sem.at[1])

    def pass_wait(j, carry):
        pass_on(core * half_blocks + j).wait_send()
        return carry

    lax.fori_loop(0, half_blocks, pass_wait, 0)

    lane_row = lax.broadcasted_iota(jnp.int32, (1, LANES), 1)
    head_mask = [
        (lane_row < head_width).astype(F32),
        (lane_row >= head_width).astype(F32),
    ]
    low_mask = [mask.astype(BF16) for mask in head_mask]
    near_rows = pl.ds(pl.multiple_of(core * half, half), half)
    far_rows = pl.ds(pl.multiple_of(far * half, half), half)

    def att_copy(p):
        return remote(
            att.at[p, far_rows], att_far.at[p], att_send.at[p], att_recv.at[p], partner, z
        )

    def attend(p, carry):
        queries, keys = qs[p], jnp.concatenate([ks[p], doc_key], axis=1)
        values = jnp.concatenate([vs[p], ones], axis=1)
        total = None
        shares = None
        for i in range(2):
            left = jnp.concatenate([queries * low_mask[i], doc_query], axis=1)
            scores = dot_nt(left, keys)
            exponent = jnp.exp(scores - jnp.max(scores, axis=-1, keepdims=True)).astype(BF16)
            exps[2 * p + i] = exponent
            both = dot(exponent, values)
            share = 1.0 / both[:, LANES:]
            part = both[:, :LANES] * share * head_mask[i]
            share = share * head_mask[i]
            total = part if total is None else total + part
            shares = share if shares is None else shares + share
        mixed[p] = total
        recip[p] = shares
        att[p] = total.astype(BF16)
        att_copy(p).start()
        return carry

    lax.fori_loop(0, pairs, attend, 0)

    for copy in out_copies:
        copy.wait()

    def att_wait(p, carry):
        att_copy(p).wait()
        return carry

    lax.fori_loop(0, pairs, att_wait, 0)
    left = jnp.concatenate(
        [att[p, near_rows, :] for p in range(pairs)] + [att_far[p] for p in range(pairs)], axis=1
    )
    acc[...] = dot(left, m_out[...])

    norm_steps = half // NORM_ROWS

    def lines_of(step):
        return pl.ds(pl.multiple_of(step * NORM_ROWS, NORM_ROWS), NORM_ROWS)

    def norm_first(step, carry):
        at = lines_of(step)
        near = pl.ds(pl.multiple_of(core * half + step * NORM_ROWS, NORM_ROWS), NORM_ROWS)
        hidden = row[near, :].astype(F32) + acc[at, :] + bias_out[...]
        norm, inv_std = normed(hidden)
        norm_a[at, :] = norm
        inv_a[at, :] = jnp.broadcast_to(inv_std, (NORM_ROWS, LANES))
        middle = norm * gain_attn[...] + beta_attn[...]
        mid[at, :] = middle
        mid_low[at, :] = middle.astype(BF16)
        return carry

    lax.fori_loop(0, norm_steps, norm_first, 0)

    def forward(f, carry):
        inner_copy(f).wait()
        outer_copy(f).wait()
        columns = pl.ds(pl.multiple_of(f * FF_CHUNK, FF_CHUNK), FF_CHUNK)
        inner = dot(mid_low[...], m_inner[f]) + bias_inner[:, columns]
        cdf = 0.5 * (1.0 + lax.erf(inner * 0.7071067811865476))
        slope[f] = cdf + inner * jnp.exp(-0.5 * inner * inner) * 0.3989422804014327
        active = (inner * cdf).astype(BF16)
        more = dot(active, m_outer[f])

        @pl.when(f == 0)
        def _():
            acc[...] = more

        @pl.when(f > 0)
        def _():
            acc[...] += more

        return carry

    lax.fori_loop(0, chunks, forward, 0)

    def cot_wait(j, carry):
        at = pl.ds(pl.multiple_of(j * span, span), span)
        arrived(cotangent, cot, at, core * half_blocks + j, cot_send, cot_recv, in_sem.at[1])
        return carry

    lax.fori_loop(0, half_blocks, cot_wait, 0)
    spread_done(cotangent, cot, cot_at, cot_send, cot_recv)

    live_end = ends[3:4, 0:1]
    zero_sum = jnp.zeros((8, width), F32)

    def norm_last(step, carry):
        beta_sum, outer_sum = carry
        at = lines_of(step)
        hidden = mid[at, :] + acc[at, :] + bias_outer[...]
        norm, inv_std = normed(hidden)
        place = lax.broadcasted_iota(jnp.int32, (NORM_ROWS, 1), 0) + core * half + step * NORM_ROWS
        live = (place < live_end).astype(F32)
        layer_out[at, :] = (live * (norm * gain_final[...] + beta_final[...])).astype(BF16)
        grad_final = live * cot[at, :].astype(F32)
        grad_hidden = norm_back(grad_final * gain_final[...], norm, inv_std)
        grad_h[at, :] = grad_hidden
        grad_low[at, :] = grad_hidden.astype(BF16)
        return beta_sum + fold_rows(grad_final), outer_sum + fold_rows(grad_hidden)

    beta_final_sum, outer_sum = lax.fori_loop(0, norm_steps, norm_last, (zero_sum, zero_sum))
    pool_a[seq, 3:4, :] = jnp.sum(beta_final_sum, axis=0, keepdims=True)
    pool_a[seq, 1:2, :] = jnp.sum(outer_sum, axis=0, keepdims=True)

    def home(source, target_ref, send_sem, recv_sem, local_sem):
        for j in range(half_blocks):
            block = core * half_blocks + j
            src = source.at[j * span : (j + 1) * span]
            line_at = z - z_half * rows

            @pl.when(block != z)
            def _():
                remote(
                    src,
                    target_ref.at[line_at],
                    send_sem.at[j],
                    recv_sem.at[line_at],
                    base + z_half,
                    block,
                ).start()

            @pl.when(block == z)
            def _():
                pltpu.make_async_copy(src, target_ref.at[line_at], local_sem).start()

    def home_done(source, target_ref, send_sem, recv_sem, local_sem):
        for j in range(half_blocks):
            block = core * half_blocks + j
            src = source.at[j * span : (j + 1) * span]
            line_at = z - z_half * rows

            @pl.when(block != z)
            def _():
                remote(
                    src,
                    target_ref.at[line_at],
                    send_sem.at[j],
                    recv_sem.at[line_at],
                    base + z_half,
                    block,
                ).wait_send()

            @pl.when(block == z)
            def _():
                pltpu.make_async_copy(src, target_ref.at[line_at], local_sem).wait()

        for r in range(rows):
            target = core * rows + r

            @pl.when(target != z)
            def _():
                remote(
                    source.at[0:span],
                    target_ref.at[r],
                    send_sem.at[0],
                    recv_sem.at[r],
                    base + z_half,
                    target,
                ).wait_recv()

    home(layer_out, layer_home, lay_send, lay_recv, in_sem.at[2])

    def backward(f, carry):
        grad_active = dot_nt(grad_low[...], m_outer[f])
        grad_inner = (grad_active * slope[f]).astype(BF16)
        total = jnp.sum(fold_rows(grad_inner.astype(F32)), axis=0, keepdims=True)
        per_line = width // FF_CHUNK
        for i in range(per_line):

            @pl.when(lax.rem(f, per_line) == i)
            def _():
                for t in range(chunks // per_line):

                    @pl.when(f // per_line == t)
                    def _():
                        pool_a[seq, 4 + t : 5 + t, i * FF_CHUNK : (i + 1) * FF_CHUNK] = total

        more = dot_nt(grad_inner, m_inner[f])

        @pl.when(f == 0)
        def _():
            acc[...] = more

        @pl.when(f > 0)
        def _():
            acc[...] += more

        return carry

    lax.fori_loop(0, chunks, backward, 0)

    def norm_first_back(step, carry):
        beta_sum, out_sum = carry
        at = lines_of(step)
        grad_middle = grad_h[at, :] + acc[at, :]
        grad_hidden = norm_back(grad_middle * gain_attn[...], norm_a[at, :], inv_a[at, 0:1])
        grad_h[at, :] = grad_hidden
        grad_low[at, :] = grad_hidden.astype(BF16)
        return beta_sum + fold_rows(grad_middle), out_sum + fold_rows(grad_hidden)

    beta_attn_sum, out_sum = lax.fori_loop(0, norm_steps, norm_first_back, (zero_sum, zero_sum))
    pool_a[seq, 2:3, :] = jnp.sum(beta_attn_sum, axis=0, keepdims=True)
    pool_a[seq, 0:1, :] = jnp.sum(out_sum, axis=0, keepdims=True)

    def plane_copy(pool, send_sem, recv_sem, step):
        return remote(
            pool.at[seq],
            pool.at[seq],
            send_sem.at[step],
            recv_sem.at[seq],
            lax.rem(seq + step, seq_size),
            z,
        )

    def plane_start(pool, send_sem, recv_sem):
        def go(step, carry):
            plane_copy(pool, send_sem, recv_sem, step).start()
            return carry

        lax.fori_loop(1, seq_size, go, 0)

    def plane_wait(pool, send_sem, recv_sem):
        def go(step, carry):
            source = lax.rem(seq + step, seq_size)
            plane_copy(pool, send_sem, recv_sem, step).wait_send()
            remote(
                pool.at[source],
                pool.at[source],
                send_sem.at[step],
                recv_sem.at[source],
                source,
                z,
            ).wait_recv()
            return carry

        lax.fori_loop(1, seq_size, go, 0)

    def column_copy(pool, send_sem, recv_sem, step):
        return remote(
            pool.at[z],
            pool.at[z],
            send_sem.at[step],
            recv_sem.at[z],
            seq,
            lax.rem(z + step, group),
        )

    def column_start(pool, send_sem, recv_sem):
        def go(step, carry):
            column_copy(pool, send_sem, recv_sem, step).start()
            return carry

        lax.fori_loop(1, group, go, 0)

    def column_wait(pool, send_sem, recv_sem):
        def go(step, carry):
            source = lax.rem(z + step, group)
            column_copy(pool, send_sem, recv_sem, step).wait_send()
            remote(
                pool.at[source],
                pool.at[source],
                send_sem.at[step],
                recv_sem.at[source],
                seq,
                source,
            ).wait_recv()
            return carry

        lax.fori_loop(1, group, go, 0)

    plane_start(pool_a, pa_send, pa_recv)

    lines = dot_nt(grad_low[...], m_out[...])
    for p in range(pairs):
        grad_att[p, near_rows, :] = lines[:, p * LANES : (p + 1) * LANES].astype(BF16)
        grad_far[p] = lines[:, side + p * LANES : side + (p + 1) * LANES].astype(BF16)

    def gat_copy(p):
        return remote(
            grad_far.at[p], grad_att.at[p, near_rows], gat_send.at[p], gat_recv.at[p], partner, z
        )

    def gat_start(p, carry):
        gat_copy(p).start()
        return carry

    lax.fori_loop(0, pairs, gat_start, 0)

    def attend_back(p, carry):
        gat_copy(p).wait_send()
        remote(
            grad_far.at[p], grad_att.at[p, far_rows], gat_send.at[p], gat_recv.at[p], partner, z
        ).wait_recv()
        queries, keys = qs[p], ks[p]
        values = jnp.concatenate([vs[p], ones], axis=1)
        share = recip[p]
        scaled = (grad_att[p].astype(F32) * share).astype(BF16)
        product = scaled.astype(F32) * mixed[p]
        dq = dk = dv = None
        for i in range(2):
            delta = jnp.sum(product * head_mask[i], axis=-1, keepdims=True)
            high = delta.astype(BF16).astype(F32)
            extra = jnp.where(lane == 0, -high, jnp.where(lane == 1, high - delta, 0.0))
            grads = scaled * low_mask[i]
            left = jnp.concatenate([grads, extra.astype(BF16)], axis=1)
            exponent = exps[2 * p + i]
            grad_scores = (exponent.astype(F32) * dot_nt(left, values)).astype(BF16)
            dq_part = dot(grad_scores, keys * low_mask[i])
            dk_part = dot_tn(grad_scores, queries * low_mask[i])
            dv_part = dot_tn(exponent, grads)
            dq = dq_part if dq is None else dq + dq_part
            dk = dk_part if dk is None else dk + dk_part
            dv = dv_part if dv is None else dv + dv_part
        dq = (dq * score_scale).astype(BF16)
        dv = dv.astype(BF16)
        for i, block in enumerate((dq, dk.astype(BF16), dv)):
            at = pl.ds(pl.multiple_of(i * side + p * LANES, LANES), LANES)
            grad_qkv[:, at] = block
        for t in range(pairs):

            @pl.when(p == t)
            def _():
                pool_b[seq, t : t + 1, :] = jnp.sum(
                    fold_rows(dq.astype(F32)), axis=0, keepdims=True
                )
                pool_b[seq, pairs + t : pairs + t + 1, :] = jnp.sum(
                    fold_rows(dv.astype(F32)), axis=0, keepdims=True
                )

        return carry

    lax.fori_loop(0, pairs, attend_back, 0)
    plane_start(pool_b, pb_send, pb_recv)

    plane_wait(pool_a, pa_send, pa_recv)
    total = pool_a[0]
    for s in range(1, seq_size):
        total = total + pool_a[s]
    z_a[z] = total
    column_start(z_a, za_send, za_recv)

    part_out[...] = dot_nt(grad_qkv[far_rows, :], m_qkv[...]).astype(BF16)
    part_copy = remote(part_out, part_in, part_sem.at[0], part_sem.at[1], partner, z)
    part_copy.start()
    acc[...] = dot_nt(grad_qkv[near_rows, :], m_qkv[...])
    part_copy.wait()

    def finish(step, carry):
        at = lines_of(step)
        total = grad_h[at, :] + acc[at, :] + part_in[at, :].astype(F32)
        grad_out[at, :] = total.astype(BF16)
        return carry

    lax.fori_loop(0, norm_steps, finish, 0)
    home(grad_out, grad_home, grad_send, grad_recv, in_sem.at[3])

    plane_wait(pool_b, pb_send, pb_recv)
    for i in range(2):
        total = pool_b[i]
        for s in range(2 + i, seq_size, 2):
            total = total + pool_b[s]
        z_b[z, i] = total
    column_start(z_b, zb_send, zb_recv)

    column_wait(z_a, za_send, za_recv)
    total = z_a[0]
    for s in range(1, group):
        total = total + z_a[s]
    sums_a[...] = total

    column_wait(z_b, zb_send, zb_recv)
    total = z_b[0]
    for s in range(1, group):
        total = total + z_b[s]
    sums_b[...] = total

    home_done(layer_out, layer_home, lay_send, lay_recv, in_sem.at[2])
    home_done(grad_out, grad_home, grad_send, grad_recv, in_sem.at[3])


def per_device(
    seq_size,
    group,
    tokens,
    doc_lengths,
    pad_counts,
    w_query,
    w_key,
    w_value,
    w_out,
    w_inner,
    w_outer,
    bias_query,
    bias_value,
    bias_out,
    bias_inner,
    bias_outer,
    gain_attn,
    beta_attn,
    gain_final,
    beta_final,
    cotangent,
):
    rows, span, width = tokens.shape
    hidden = w_inner.shape[1]
    slots = span * group
    half = slots // 2
    half_blocks = group // 2
    side = width // 2
    pairs = side // LANES
    chunks = hidden // FF_CHUNK
    if rows * 2 != group or pairs * 2 != 8 or hidden != 4 * width:
        raise ValueError("unsupported sizes")

    any_space = pl.BlockSpec(memory_space=pl.ANY)
    vmem = pl.BlockSpec(memory_space=pltpu.VMEM)
    smem = pl.BlockSpec(memory_space=pltpu.SMEM)
    dma = pltpu.SemaphoreType.DMA
    scratch = [
        pltpu.VMEM((width, 3 * side), BF16),
        pltpu.VMEM((width, width), BF16),
        pltpu.VMEM((chunks, width, FF_CHUNK), BF16),
        pltpu.VMEM((chunks, FF_CHUNK, width), BF16),
        pltpu.VMEM((slots, width), BF16),
        pltpu.VMEM((half, width), BF16),
        pltpu.VMEM((2, rows, 8, LANES), jnp.int32),
        pltpu.VMEM((pairs, slots, LANES), BF16),
        pltpu.VMEM((pairs, slots, LANES), BF16),
        pltpu.VMEM((pairs, slots, LANES), BF16),
        pltpu.VMEM((2 * pairs, slots, slots), BF16),
        pltpu.VMEM((pairs, slots, LANES), F32),
        pltpu.VMEM((pairs, slots, LANES), F32),
        pltpu.VMEM((pairs, slots, LANES), BF16),
        pltpu.VMEM((pairs, half, LANES), BF16),
        pltpu.VMEM((half, width), F32),
        pltpu.VMEM((half, LANES), F32),
        pltpu.VMEM((half, width), F32),
        pltpu.VMEM((half, width), BF16),
        pltpu.VMEM((half, width), F32),
        pltpu.VMEM((chunks, half, FF_CHUNK), F32),
        pltpu.VMEM((half, width), F32),
        pltpu.VMEM((half, width), BF16),
        pltpu.VMEM((pairs, slots, LANES), BF16),
        pltpu.VMEM((pairs, half, LANES), BF16),
        pltpu.VMEM((slots, 3 * side), BF16),
        pltpu.VMEM((half, width), BF16),
        pltpu.VMEM((half, width), BF16),
        pltpu.VMEM((half, width), BF16),
        pltpu.VMEM((half, width), BF16),
        pltpu.VMEM((seq_size, 8, width), F32),
        pltpu.VMEM((group, 8, width), F32),
        pltpu.VMEM((seq_size, 8, LANES), F32),
        pltpu.VMEM((group, 2, 8, LANES), F32),
        dma((5 + 2 * chunks,)),
        dma((4,)),
        dma((rows,)),
        dma((half_blocks,)),
        dma((half_blocks,)),
        dma((half_blocks,)),
        dma((2,)),
        dma((rows,)),
        dma((half_blocks,)),
        dma((pairs,)),
        dma((pairs,)),
        dma((pairs,)),
        dma((pairs,)),
        dma((half_blocks,)),
        dma((rows,)),
        dma((2,)),
        dma((half_blocks,)),
        dma((rows,)),
        dma((seq_size,)),
        dma((seq_size,)),
        dma((group,)),
        dma((group,)),
        dma((seq_size,)),
        dma((seq_size,)),
        dma((group,)),
        dma((group,)),
    ]
    vectors = (
        bias_query,
        bias_value,
        bias_out,
        bias_inner,
        bias_outer,
        gain_attn,
        beta_attn,
        gain_final,
        beta_final,
    )
    layer_home, grad_home, sums_a, sums_b = pl.pallas_call(
        functools.partial(kernel, seq_size, group),
        out_shape=(
            jax.ShapeDtypeStruct(tokens.shape, BF16),
            jax.ShapeDtypeStruct(tokens.shape, BF16),
            jax.ShapeDtypeStruct((8, width), F32),
            jax.ShapeDtypeStruct((2, 8, LANES), F32),
        ),
        in_specs=[any_space] * 2 + [smem] * 2 + [any_space] * 6 + [vmem] * len(vectors),
        out_specs=(any_space, any_space, vmem, vmem),
        scratch_shapes=scratch,
        compiler_params=pltpu.CompilerParams(
            collective_id=0, has_side_effects=True, vmem_limit_bytes=60 * 2**20
        ),
    )(
        tokens,
        cotangent,
        doc_lengths,
        pad_counts,
        w_query,
        w_key,
        w_value,
        w_out,
        w_inner,
        w_outer,
        *[vector.reshape(1, -1) for vector in vectors],
    )
    grad_bias_query = sums_b[:, :pairs].reshape(width)
    grad_bias_value = sums_b[:, pairs:].reshape(width)
    return (
        layer_home,
        grad_home.astype(F32),
        grad_bias_query,
        grad_bias_value,
        sums_a[0],
        sums_a[4:8].reshape(hidden),
        sums_a[1],
        sums_a[2],
        sums_a[3],
    )


def solution(mesh):
    split = P("seq", "head", None)
    placed = (split, P("seq", None), P("seq")) + (P(),) * 15 + (split,)
    return jax.shard_map(
        functools.partial(per_device, mesh.shape["seq"], mesh.shape["head"]),
        mesh=mesh,
        in_specs=placed,
        out_specs=(split, split) + (P(),) * 7,
        check_vma=False,
    )
```

```python
import functools

import jax
import jax.numpy as jnp
from jax import lax
from jax.experimental import pallas as pl
from jax.experimental.pallas import tpu as pltpu
from jax.sharding import PartitionSpec as P

HEADS = 16
LANES = 128
EPS = 1e-06
BIG = 2.0**30
FF_CHUNK = 512
FEATURE_CHUNK = 256
NORM_ROWS = 32
MESH = pl.DeviceIdType.MESH
F32 = jnp.float32
BF16 = jnp.bfloat16


def dot(left, right):
    return lax.dot_general(left, right, (((1,), (0,)), ((), ())), preferred_element_type=F32)


def dot_nt(left, right):
    return lax.dot_general(left, right, (((1,), (1,)), ((), ())), preferred_element_type=F32)


def dot_tn(left, right):
    return lax.dot_general(left, right, (((0,), (0,)), ((), ())), preferred_element_type=F32)


def normed(hidden):
    row_mean = jnp.mean(hidden, axis=-1, keepdims=True)
    centred = hidden - row_mean
    inv_std = lax.rsqrt(jnp.mean(centred * centred, axis=-1, keepdims=True) + EPS)
    return centred * inv_std, inv_std


def norm_back(gradient, norm, inv_std):
    return inv_std * (
        gradient
        - jnp.mean(gradient, axis=-1, keepdims=True)
        - norm * jnp.mean(gradient * norm, axis=-1, keepdims=True)
    )


def fold_rows(block):
    total = block[0:8]
    for start in range(8, block.shape[0], 8):
        total = total + block[start : start + 8]
    return total


def kernel(
    seq_size,
    group,
    tokens,
    cotangent,
    doc_lengths,
    pad_counts,
    w_query,
    w_key,
    w_value,
    w_out,
    w_inner,
    w_outer,
    in_bias_query,
    in_bias_value,
    in_bias_out,
    in_bias_inner,
    in_bias_outer,
    in_gain_attn,
    in_beta_attn,
    in_gain_final,
    in_beta_final,
    layer_home,
    grad_home,
    sums_a,
    sums_b,
    m_qkv,
    m_out,
    m_inner,
    m_outer,
    bias_query,
    bias_value,
    bias_out,
    bias_inner,
    bias_outer,
    gain_attn,
    beta_attn,
    gain_final,
    beta_final,
    row,
    cot,
    info,
    qs,
    ks,
    vs,
    exps,
    recip,
    mixed,
    att,
    att_far,
    norm_a,
    inv_a,
    mid,
    mid_low,
    acc,
    slope,
    raw,
    active,
    inner_sum,
    grad_h,
    grad_low,
    grad_att,
    grad_far,
    grad_qkv,
    part,
    part_out,
    part_in,
    grad_out,
    layer_out,
    pool_a,
    z_a,
    pool_b,
    z_b,
    w_sem,
    vec_sem,
    in_sem,
    tok_send,
    tok_recv,
    pass_send,
    pass_recv,
    info_sem,
    cot_send,
    cot_recv,
    att_send,
    att_recv,
    gat_send,
    gat_recv,
    lay_send,
    lay_recv,
    part_send,
    part_recv,
    grad_send,
    grad_recv,
    pa_send,
    pa_recv,
    za_send,
    za_recv,
    pb_send,
    pb_recv,
    zb_send,
    zb_recv,
):
    rows, span, width = tokens.shape
    half_blocks = group // 2
    slots = span * group
    half = slots // 2
    head_width = width // HEADS
    side = width // 2
    pairs = side // LANES
    chunks = m_inner.shape[0]
    norm_steps = half // NORM_ROWS
    score_scale = head_width**-0.5

    seq = lax.axis_index("seq")
    z = lax.axis_index("head")
    core = lax.rem(seq, 2)
    base = seq - core
    partner = base + 1 - core
    z_half = z // half_blocks
    far = 1 - core

    def rows_of(block):
        return pl.ds(pl.multiple_of(block * span, span), span)

    def remote(src, dst, send_sem, recv_sem, at_seq, at_head):
        return pltpu.make_async_remote_copy(
            src_ref=src,
            dst_ref=dst,
            send_sem=send_sem,
            recv_sem=recv_sem,
            device_id=(at_seq, at_head),
            device_id_type=MESH,
        )

    barrier = pltpu.get_barrier_semaphore()

    def greet_z(step, carry):
        pl.semaphore_signal(
            barrier, inc=1, device_id=(seq, lax.rem(z + step, group)), device_id_type=MESH
        )
        return carry

    def greet_seq(step, carry):
        pl.semaphore_signal(
            barrier, inc=1, device_id=(lax.rem(seq + step, seq_size), z), device_id_type=MESH
        )
        return carry

    for r in range(rows):
        target = core * rows + r

        @pl.when(target != z)
        def _():
            pl.semaphore_signal(
                barrier, inc=1, device_id=(base + z_half, target), device_id_type=MESH
            )

    lax.fori_loop(1, seq_size, greet_seq, 0)
    lax.fori_loop(1, group, greet_z, 0)

    mine = pl.ds(pl.multiple_of(core * side, side), side)
    theirs = pl.ds(pl.multiple_of(far * side, side), side)
    qkv_copies = [
        pltpu.make_async_copy(
            weight.at[:, mine], m_qkv.at[:, i * side : (i + 1) * side], w_sem.at[i]
        )
        for i, weight in enumerate((w_query, w_key, w_value))
    ]
    for copy in qkv_copies:
        copy.start()
    vector_copies = [
        pltpu.make_async_copy(source, target, vec_sem.at[i])
        for i, (source, target) in enumerate(
            (
                (in_bias_query, bias_query),
                (in_bias_value, bias_value),
                (in_bias_out, bias_out),
                (in_bias_inner, bias_inner),
                (in_bias_outer, bias_outer),
                (in_gain_attn, gain_attn),
                (in_beta_attn, beta_attn),
                (in_gain_final, gain_final),
                (in_beta_final, beta_final),
            )
        )
    ]
    for copy in vector_copies:
        copy.start()
    out_copies = [
        pltpu.make_async_copy(w_out.at[mine], m_out.at[0:side], w_sem.at[3]),
        pltpu.make_async_copy(w_out.at[theirs], m_out.at[side:width], w_sem.at[4]),
    ]

    def inner_copy(f):
        columns = pl.ds(pl.multiple_of(f * FF_CHUNK, FF_CHUNK), FF_CHUNK)
        return pltpu.make_async_copy(w_inner.at[:, columns], m_inner.at[f], w_sem.at[5 + f])

    def outer_copy(f):
        lines = pl.ds(pl.multiple_of(f * FF_CHUNK, FF_CHUNK), FF_CHUNK)
        return pltpu.make_async_copy(w_outer.at[lines], m_outer.at[lines], w_sem.at[5 + chunks + f])

    line = lax.broadcasted_iota(jnp.int32, (8, LANES), 0)
    for r in range(rows):
        first = doc_lengths[r, 0]
        second = first + doc_lengths[r, 1]
        third = second + doc_lengths[r, 2]
        ends = jnp.where(line == 0, first, jnp.where(line == 1, second, third))
        info[core, r] = jnp.where(line == 3, slots - pad_counts[r], ends)

    peers = jnp.where(z_half == core, rows - 1, rows)
    pl.semaphore_wait(barrier, peers + seq_size - 1 + group - 1)

    def spread(source, target_ref, at, send_sem, recv_sem, local_sem):
        for r in range(rows):
            target = core * rows + r

            @pl.when(target != z)
            def _():
                remote(
                    source.at[r],
                    target_ref.at[at],
                    send_sem.at[r],
                    recv_sem.at[z - z_half * half_blocks],
                    base + z_half,
                    target,
                ).start()

            @pl.when(target == z)
            def _():
                pltpu.make_async_copy(source.at[r], target_ref.at[at], local_sem).start()

    def spread_done(source, target_ref, at, send_sem, recv_sem):
        for r in range(rows):
            target = core * rows + r

            @pl.when(target != z)
            def _():
                remote(
                    source.at[r],
                    target_ref.at[at],
                    send_sem.at[r],
                    recv_sem.at[z - z_half * half_blocks],
                    base + z_half,
                    target,
                ).wait_send()

    def arrived(source, target_ref, at, block, send_sem, recv_sem, local_sem):
        j = block - core * half_blocks

        @pl.when(block != z)
        def _():
            remote(
                source.at[0],
                target_ref.at[at],
                send_sem.at[0],
                recv_sem.at[j],
                base + z_half,
                block,
            ).wait_recv()

        @pl.when(block == z)
        def _():
            pltpu.make_async_copy(source.at[0], target_ref.at[at], local_sem).wait()

    info_copy = remote(info.at[core], info.at[core], info_sem.at[0], info_sem.at[1], partner, z)
    info_copy.start()
    spread(tokens, row, rows_of(z), tok_send, tok_recv, in_sem.at[0])
    for copy in out_copies:
        copy.start()

    def start_inner(f, carry):
        inner_copy(f).start()
        outer_copy(f).start()
        return carry

    lax.fori_loop(0, chunks, start_inner, 0)

    info_copy.wait_send()
    remote(info.at[far], info.at[far], info_sem.at[0], info_sem.at[1], partner, z).wait_recv()
    for copy in qkv_copies + vector_copies:
        copy.wait()

    lane = lax.broadcasted_iota(jnp.int32, (slots, LANES), 1)
    slot = lax.broadcasted_iota(jnp.int32, (slots, LANES), 0)
    ends = info[z_half, z - z_half * rows]
    doc = (slot >= ends[0:1]).astype(jnp.int32)
    for i in range(1, 4):
        doc = doc + (slot >= ends[i : i + 1]).astype(jnp.int32)
    doc_query = jnp.where(doc == lane, BIG, 0.0).astype(BF16)
    doc_key = jnp.where((doc != lane) & (lane < 5), -1.0, 0.0).astype(BF16)
    ones = jnp.ones((slots, LANES), BF16)

    def pass_on(block):
        j = block - core * half_blocks
        at = rows_of(block)
        return remote(row.at[at], row.at[at], pass_send.at[j], pass_recv.at[j], partner, z)

    def project(step, carry):
        near = step < half_blocks
        within = lax.rem(z - z_half * half_blocks + step, half_blocks)
        other = step - half_blocks
        beyond = jnp.where(z_half == 0, half_blocks + other, half_blocks - 1 - other)
        block = jnp.where(near, z_half * half_blocks + within, beyond)
        block_half = block // half_blocks
        at = rows_of(block)

        @pl.when(block_half == core)
        def _():
            arrived(tokens, row, at, block, tok_send, tok_recv, in_sem.at[0])
            pass_on(block).start()

        @pl.when(block_half != core)
        def _():
            j = block - far * half_blocks
            remote(
                row.at[at], row.at[at], pass_send.at[j], pass_recv.at[j], partner, z
            ).wait_recv()

        x = row[at, :]
        q = (dot(x, m_qkv[:, 0:side]) + bias_query[:, mine]) * score_scale
        k = dot(x, m_qkv[:, side : 2 * side])
        v = dot(x, m_qkv[:, 2 * side : 3 * side]) + bias_value[:, mine]
        for p in range(pairs):
            cut = slice(p * LANES, (p + 1) * LANES)
            qs[p, at, :] = q[:, cut].astype(BF16)
            ks[p, at, :] = k[:, cut].astype(BF16)
            vs[p, at, :] = v[:, cut].astype(BF16)
        return carry

    lax.fori_loop(0, group, project, 0)
    spread_done(tokens, row, rows_of(z), tok_send, tok_recv)

    cot_at = pl.ds(pl.multiple_of((z - z_half * half_blocks) * span, span), span)
    spread(cotangent, cot, cot_at, cot_send, cot_recv, in_sem.at[1])

    def pass_wait(j, carry):
        pass_on(core * half_blocks + j).wait_send()
        return carry

    lax.fori_loop(0, half_blocks, pass_wait, 0)

    lane_row = lax.broadcasted_iota(jnp.int32, (1, LANES), 1)
    head_mask = [
        (lane_row < head_width).astype(F32),
        (lane_row >= head_width).astype(F32),
    ]
    low_mask = [mask.astype(BF16) for mask in head_mask]
    near_rows = pl.ds(pl.multiple_of(core * half, half), half)
    far_rows = pl.ds(pl.multiple_of(far * half, half), half)

    def att_copy(p):
        return remote(
            att.at[p, far_rows], att_far.at[p], att_send.at[p], att_recv.at[p], partner, z
        )

    def score(p):
        keys = jnp.concatenate([ks[p], doc_key], axis=1)
        for i in range(2):
            left = jnp.concatenate([qs[p] * low_mask[i], doc_query], axis=1)
            slope[2 * lax.rem(p, 2) + i] = dot_nt(left, keys)

    def attend(p):
        values = jnp.concatenate([vs[p], ones], axis=1)
        total = None
        shares = None
        for i in range(2):
            scores = slope[2 * lax.rem(p, 2) + i]
            exponent = jnp.exp(scores - jnp.max(scores, axis=-1, keepdims=True)).astype(BF16)
            exps[2 * p + i] = exponent
            both = dot(exponent, values)
            share = 1.0 / both[:, LANES:]
            spread_out = both[:, :LANES] * share * head_mask[i]
            share = share * head_mask[i]
            total = spread_out if total is None else total + spread_out
            shares = share if shares is None else shares + share
        mixed[p] = total
        recip[p] = shares
        att[p] = total.astype(BF16)
        att_copy(p).start()

    def attend_step(p, carry):
        score(p + 1)
        attend(p)
        return carry

    score(0)
    lax.fori_loop(0, pairs - 1, attend_step, 0, unroll=True)
    attend(pairs - 1)

    for copy in out_copies:
        copy.wait()
    left = jnp.concatenate([att[p, near_rows, :] for p in range(pairs)], axis=1)
    acc[...] = dot(left, m_out[0:side, :])

    def att_wait(p, carry):
        att_copy(p).wait()
        return carry

    lax.fori_loop(0, pairs, att_wait, 0)
    left = jnp.concatenate([att_far[p] for p in range(pairs)], axis=1)
    acc[...] += dot(left, m_out[side:width, :])

    def lines_of(step):
        return pl.ds(pl.multiple_of(step * NORM_ROWS, NORM_ROWS), NORM_ROWS)

    def norm_first(step, carry):
        at = lines_of(step)
        near = pl.ds(pl.multiple_of(core * half + step * NORM_ROWS, NORM_ROWS), NORM_ROWS)
        hidden = row[near, :].astype(F32) + acc[at, :] + bias_out[...]
        norm, inv_std = normed(hidden)
        norm_a[at, :] = norm
        inv_a[at, :] = jnp.broadcast_to(inv_std, (NORM_ROWS, LANES))
        middle = norm * gain_attn[...] + beta_attn[...]
        mid[at, :] = middle
        mid_low[at, :] = middle.astype(BF16)
        return carry

    lax.fori_loop(0, norm_steps, norm_first, 0, unroll=True)

    def weights_wait(f, carry):
        inner_copy(f).wait()
        outer_copy(f).wait()
        return carry

    lax.fori_loop(0, chunks, weights_wait, 0)

    def columns_of(f):
        return pl.ds(pl.multiple_of(f * FF_CHUNK, FF_CHUNK), FF_CHUNK)

    def slope_at(f):
        return f // 2, pl.ds(pl.multiple_of(lax.rem(f, 2) * half, half), half)

    def activate(f):
        inner = raw[lax.rem(f, 2)] + bias_inner[:, columns_of(f)]
        cdf = 0.5 * (1.0 + lax.erf(inner * 0.7071067811865476))
        which, lines = slope_at(f)
        slope[which, lines, :] = cdf + inner * jnp.exp(-0.5 * inner * inner) * 0.3989422804014327
        active[:, columns_of(f)] = (inner * cdf).astype(BF16)

    def forward(f, carry):
        raw[lax.rem(f + 1, 2)] = dot(mid_low[...], m_inner[f + 1])
        activate(f)
        return carry

    raw[0] = dot(mid_low[...], m_inner[0])
    lax.fori_loop(0, chunks - 1, forward, 0, unroll=True)
    activate(chunks - 1)
    for n in range(0, width, FEATURE_CHUNK):
        acc[:, n : n + FEATURE_CHUNK] = dot(active[...], m_outer[:, n : n + FEATURE_CHUNK])

    def cot_wait(j, carry):
        at = pl.ds(pl.multiple_of(j * span, span), span)
        arrived(cotangent, cot, at, core * half_blocks + j, cot_send, cot_recv, in_sem.at[1])
        return carry

    lax.fori_loop(0, half_blocks, cot_wait, 0)
    spread_done(cotangent, cot, cot_at, cot_send, cot_recv)

    live_end = ends[3:4, 0:1]
    zero_sum = jnp.zeros((8, width), F32)

    def norm_last(step, carry):
        beta_sum, outer_sum = carry
        at = lines_of(step)
        hidden = mid[at, :] + acc[at, :] + bias_outer[...]
        norm, inv_std = normed(hidden)
        place = lax.broadcasted_iota(jnp.int32, (NORM_ROWS, 1), 0) + core * half + step * NORM_ROWS
        live = (place < live_end).astype(F32)
        layer_out[at, :] = (live * (norm * gain_final[...] + beta_final[...])).astype(BF16)
        grad_final = live * cot[at, :].astype(F32)
        grad_hidden = norm_back(grad_final * gain_final[...], norm, inv_std)
        grad_h[at, :] = grad_hidden
        grad_low[at, :] = grad_hidden.astype(BF16)
        return beta_sum + fold_rows(grad_final), outer_sum + fold_rows(grad_hidden)

    beta_final_sum, outer_sum = lax.fori_loop(
        0, norm_steps, norm_last, (zero_sum, zero_sum), unroll=True
    )
    pool_a[seq, 3:4, :] = jnp.sum(beta_final_sum, axis=0, keepdims=True)
    pool_a[seq, 1:2, :] = jnp.sum(outer_sum, axis=0, keepdims=True)

    def home_block(block, source, target_ref, send_sem, recv_sem, local_sem):
        j = block - core * half_blocks
        src = source.at[pl.ds(pl.multiple_of(j * span, span), span)]
        line_at = z - z_half * rows

        @pl.when(block != z)
        def _():
            remote(
                src,
                target_ref.at[line_at],
                send_sem.at[j],
                recv_sem.at[line_at],
                base + z_half,
                block,
            ).start()

        @pl.when(block == z)
        def _():
            pltpu.make_async_copy(src, target_ref.at[line_at], local_sem).start()

    def home_done(source, target_ref, send_sem, recv_sem, local_sem):
        for j in range(half_blocks):
            block = core * half_blocks + j
            src = source.at[j * span : (j + 1) * span]
            line_at = z - z_half * rows

            @pl.when(block != z)
            def _():
                remote(
                    src,
                    target_ref.at[line_at],
                    send_sem.at[j],
                    recv_sem.at[line_at],
                    base + z_half,
                    block,
                ).wait_send()

            @pl.when(block == z)
            def _():
                pltpu.make_async_copy(src, target_ref.at[line_at], local_sem).wait()

        for r in range(rows):
            target = core * rows + r

            @pl.when(target != z)
            def _():
                remote(
                    source.at[0:span],
                    target_ref.at[r],
                    send_sem.at[0],
                    recv_sem.at[r],
                    base + z_half,
                    target,
                ).wait_recv()

    for j in range(half_blocks):
        home_block(
            core * half_blocks + j, layer_out, layer_home, lay_send, lay_recv, in_sem.at[2]
        )

    def backward(f, carry):
        which, lines = slope_at(f)
        grad_active = dot_nt(grad_low[...], m_outer[columns_of(f), :])
        grad_inner = (grad_active * slope[which, lines, :]).astype(BF16)
        active[:, columns_of(f)] = grad_inner
        inner_sum[f] = fold_rows(grad_inner.astype(F32))
        return carry

    lax.fori_loop(0, chunks, backward, 0, unroll=True)
    for n in range(0, width, FEATURE_CHUNK):
        total = None
        for f in range(chunks):
            term = dot_nt(
                active[:, f * FF_CHUNK : (f + 1) * FF_CHUNK], m_inner[f, n : n + FEATURE_CHUNK, :]
            )
            total = term if total is None else total + term
        acc[:, n : n + FEATURE_CHUNK] = total
    per_line = width // FF_CHUNK
    for f in range(chunks):
        line_at = 4 + f // per_line
        column = f % per_line * FF_CHUNK
        pool_a[seq, line_at : line_at + 1, column : column + FF_CHUNK] = jnp.sum(
            inner_sum[f], axis=0, keepdims=True
        )

    def norm_first_back(step, carry):
        beta_sum, out_sum = carry
        at = lines_of(step)
        grad_middle = grad_h[at, :] + acc[at, :]
        grad_hidden = norm_back(grad_middle * gain_attn[...], norm_a[at, :], inv_a[at, 0:1])
        grad_h[at, :] = grad_hidden
        grad_low[at, :] = grad_hidden.astype(BF16)
        return beta_sum + fold_rows(grad_middle), out_sum + fold_rows(grad_hidden)

    beta_attn_sum, out_sum = lax.fori_loop(
        0, norm_steps, norm_first_back, (zero_sum, zero_sum), unroll=True
    )
    pool_a[seq, 2:3, :] = jnp.sum(beta_attn_sum, axis=0, keepdims=True)
    pool_a[seq, 0:1, :] = jnp.sum(out_sum, axis=0, keepdims=True)

    def plane_copy(pool, send_sem, recv_sem, step):
        return remote(
            pool.at[seq],
            pool.at[seq],
            send_sem.at[step],
            recv_sem.at[seq],
            lax.rem(seq + step, seq_size),
            z,
        )

    def plane_start(pool, send_sem, recv_sem):
        def go(step, carry):
            plane_copy(pool, send_sem, recv_sem, step).start()
            return carry

        lax.fori_loop(1, seq_size, go, 0)

    def plane_wait(pool, send_sem, recv_sem):
        def go(step, carry):
            source = lax.rem(seq + step, seq_size)
            plane_copy(pool, send_sem, recv_sem, step).wait_send()
            remote(
                pool.at[source],
                pool.at[source],
                send_sem.at[step],
                recv_sem.at[source],
                source,
                z,
            ).wait_recv()
            return carry

        lax.fori_loop(1, seq_size, go, 0)

    def column_copy(pool, send_sem, recv_sem, step):
        return remote(
            pool.at[z],
            pool.at[z],
            send_sem.at[step],
            recv_sem.at[z],
            seq,
            lax.rem(z + step, group),
        )

    def column_start(pool, send_sem, recv_sem):
        def go(step, carry):
            column_copy(pool, send_sem, recv_sem, step).start()
            return carry

        lax.fori_loop(1, group, go, 0)

    def column_wait(pool, send_sem, recv_sem):
        def go(step, carry):
            source = lax.rem(z + step, group)
            column_copy(pool, send_sem, recv_sem, step).wait_send()
            remote(
                pool.at[source],
                pool.at[source],
                send_sem.at[step],
                recv_sem.at[source],
                seq,
                source,
            ).wait_recv()
            return carry

        lax.fori_loop(1, group, go, 0)

    plane_start(pool_a, pa_send, pa_recv)

    def gat_copy(p):
        return remote(
            grad_far.at[p], grad_att.at[p, near_rows], gat_send.at[p], gat_recv.at[p], partner, z
        )

    lines = dot_nt(grad_low[...], m_out[side:width, :])
    for p in range(pairs):
        grad_far[p] = lines[:, p * LANES : (p + 1) * LANES].astype(BF16)
        gat_copy(p).start()
    lines = dot_nt(grad_low[...], m_out[0:side, :])
    for p in range(pairs):
        grad_att[p, near_rows, :] = lines[:, p * LANES : (p + 1) * LANES].astype(BF16)

    def gat_wait(p, carry):
        gat_copy(p).wait_send()
        remote(
            grad_far.at[p], grad_att.at[p, far_rows], gat_send.at[p], gat_recv.at[p], partner, z
        ).wait_recv()
        return carry

    lax.fori_loop(0, pairs, gat_wait, 0)

    def attend_back(p, carry):
        keys = ks[p]
        turned = qs[p].T
        values = jnp.concatenate([vs[p], ones], axis=1)
        scaled = (grad_att[p].astype(F32) * recip[p]).astype(BF16)
        product = scaled.astype(F32) * mixed[p]
        dq = None
        dk = []
        dv = []
        for i in range(2):
            cut = slice(i * head_width, (i + 1) * head_width)
            delta = jnp.sum(product * head_mask[i], axis=-1, keepdims=True)
            high = delta.astype(BF16).astype(F32)
            extra = jnp.where(lane == 0, -high, jnp.where(lane == 1, high - delta, 0.0))
            grads = scaled * low_mask[i]
            left = jnp.concatenate([grads, extra.astype(BF16)], axis=1)
            exponent = exps[2 * p + i]
            grad_scores = (exponent.astype(F32) * dot_nt(left, values)).astype(BF16)
            term = dot(grad_scores, keys * low_mask[i])
            dq = term if dq is None else dq + term
            dk.append(dot(turned[cut], grad_scores))
            dv.append(dot(grads.T[cut], exponent))
        dq = (dq * score_scale).astype(BF16)
        dk = jnp.concatenate(dk, axis=0).astype(BF16).T
        dv = jnp.concatenate(dv, axis=0).astype(BF16).T
        for i, block in enumerate((dq, dk, dv)):
            at = pl.ds(pl.multiple_of(i * side + p * LANES, LANES), LANES)
            grad_qkv[:, at] = block
        pool_b[seq, pl.ds(p, 1), :] = jnp.sum(fold_rows(dq.astype(F32)), axis=0, keepdims=True)
        pool_b[seq, pl.ds(pairs + p, 1), :] = jnp.sum(
            fold_rows(dv.astype(F32)), axis=0, keepdims=True
        )
        return carry

    lax.fori_loop(0, pairs, attend_back, 0, unroll=True)
    plane_start(pool_b, pb_send, pb_recv)

    plane_wait(pool_a, pa_send, pa_recv)
    total = pool_a[0]
    for s in range(1, seq_size):
        total = total + pool_a[s]
    z_a[z] = total
    column_start(z_a, za_send, za_recv)

    def block_at(step):
        first = step < half_blocks
        near = jnp.where(first, 1 - z_half, z_half)
        return near * half_blocks + lax.rem(step, half_blocks)

    def slice_of(block):
        start = (block - block // half_blocks * half_blocks) * span
        return pl.ds(pl.multiple_of(start, span), span)

    def part_copy(block):
        j = block - block // half_blocks * half_blocks
        at = slice_of(block)
        return remote(
            part_out.at[at], part_in.at[at], part_send.at[j], part_recv.at[j], partner, z
        )

    def finish(step):
        block = block_at(step)

        @pl.when(block // half_blocks == core)
        def _():
            at = slice_of(block)
            part_copy(block).wait_recv()
            total = grad_h[at, :] + part[lax.rem(step, 2)] + part_in[at, :].astype(F32)
            grad_out[at, :] = total.astype(BF16)
            home_block(block, grad_out, grad_home, grad_send, grad_recv, in_sem.at[3])

    def token_grad(step, carry):
        block = block_at(step)
        term = dot_nt(grad_qkv[rows_of(block), :], m_qkv[...])
        mine_now = block // half_blocks == core

        @pl.when(mine_now)
        def _():
            part[lax.rem(step, 2)] = term

        @pl.when(jnp.logical_not(mine_now))
        def _():
            part_out[slice_of(block), :] = term.astype(BF16)
            part_copy(block).start()

        @pl.when(step > 0)
        def _():
            finish(step - 1)

        return carry

    lax.fori_loop(0, group, token_grad, 0)
    finish(group - 1)

    def part_wait(j, carry):
        part_copy(far * half_blocks + j).wait_send()
        return carry

    lax.fori_loop(0, half_blocks, part_wait, 0)

    plane_wait(pool_b, pb_send, pb_recv)
    for i in range(2):
        total = pool_b[i]
        for s in range(2 + i, seq_size, 2):
            total = total + pool_b[s]
        z_b[z, i] = total
    column_start(z_b, zb_send, zb_recv)

    column_wait(z_a, za_send, za_recv)
    total = z_a[0]
    for s in range(1, group):
        total = total + z_a[s]
    sums_a[...] = total

    column_wait(z_b, zb_send, zb_recv)
    total = z_b[0]
    for s in range(1, group):
        total = total + z_b[s]
    sums_b[...] = total

    home_done(layer_out, layer_home, lay_send, lay_recv, in_sem.at[2])
    home_done(grad_out, grad_home, grad_send, grad_recv, in_sem.at[3])


def finish_kernel(
    layer,
    grad,
    sums_a,
    sums_b,
    layer_out,
    input_grad,
    grad_bias_query,
    grad_bias_value,
    grad_bias_out,
    grad_bias_inner,
    grad_bias_outer,
    grad_beta_attn,
    grad_beta_final,
    wide,
    lines,
    inner_line,
    sems,
):
    rows = layer.shape[0]
    width = layer.shape[2]
    copies = [pltpu.make_async_copy(layer, layer_out, sems.at[0])]
    copies[0].start()
    for r in range(rows):
        wide[r] = grad[r].astype(F32)
        copies.append(pltpu.make_async_copy(wide.at[r], input_grad.at[r], sems.at[1 + r]))
        copies[-1].start()
    pairs = sums_b.shape[1] // 2
    for i in range(2):
        for p in range(pairs):
            column = (i * pairs + p) * LANES
            lines[0, :, column : column + LANES] = sums_b[i, p : p + 1, :]
            lines[1, :, column : column + LANES] = sums_b[i, pairs + p : pairs + p + 1, :]
    for i in range(4):
        lines[2 + i] = sums_a[i : i + 1, :]
        inner_line[:, i * width : (i + 1) * width] = sums_a[4 + i : 5 + i, :]
    targets = (
        grad_bias_query,
        grad_bias_value,
        grad_bias_out,
        grad_bias_outer,
        grad_beta_attn,
        grad_beta_final,
    )
    for i, target in enumerate(targets):
        copies.append(pltpu.make_async_copy(lines.at[i], target, sems.at[1 + rows + i]))
        copies[-1].start()
    copies.append(pltpu.make_async_copy(inner_line, grad_bias_inner, sems.at[7 + rows]))
    copies[-1].start()
    for copy in copies:
        copy.wait()


def per_device(
    seq_size,
    group,
    tokens,
    doc_lengths,
    pad_counts,
    w_query,
    w_key,
    w_value,
    w_out,
    w_inner,
    w_outer,
    bias_query,
    bias_value,
    bias_out,
    bias_inner,
    bias_outer,
    gain_attn,
    beta_attn,
    gain_final,
    beta_final,
    cotangent,
):
    rows, span, width = tokens.shape
    hidden = w_inner.shape[1]
    slots = span * group
    half = slots // 2
    half_blocks = group // 2
    side = width // 2
    pairs = side // LANES
    chunks = hidden // FF_CHUNK
    if rows * 2 != group or pairs != 4 or hidden != 4 * width or slots != FF_CHUNK:
        raise ValueError("unsupported sizes")

    any_space = pl.BlockSpec(memory_space=pl.ANY)
    vmem = pl.BlockSpec(memory_space=pltpu.VMEM)
    smem = pl.BlockSpec(memory_space=pltpu.SMEM)
    dma = pltpu.SemaphoreType.DMA
    scratch = [
        pltpu.VMEM((width, 3 * side), BF16),
        pltpu.VMEM((width, width), BF16),
        pltpu.VMEM((chunks, width, FF_CHUNK), BF16),
        pltpu.VMEM((hidden, width), BF16),
        pltpu.VMEM((1, width), F32),
        pltpu.VMEM((1, width), F32),
        pltpu.VMEM((1, width), F32),
        pltpu.VMEM((1, hidden), F32),
        pltpu.VMEM((1, width), F32),
        pltpu.VMEM((1, width), F32),
        pltpu.VMEM((1, width), F32),
        pltpu.VMEM((1, width), F32),
        pltpu.VMEM((1, width), F32),
        pltpu.VMEM((slots, width), BF16),
        pltpu.VMEM((half, width), BF16),
        pltpu.VMEM((2, rows, 8, LANES), jnp.int32),
        pltpu.VMEM((pairs, slots, LANES), BF16),
        pltpu.VMEM((pairs, slots, LANES), BF16),
        pltpu.VMEM((pairs, slots, LANES), BF16),
        pltpu.VMEM((2 * pairs, slots, slots), BF16),
        pltpu.VMEM((pairs, slots, LANES), F32),
        pltpu.VMEM((pairs, slots, LANES), F32),
        pltpu.VMEM((pairs, slots, LANES), BF16),
        pltpu.VMEM((pairs, half, LANES), BF16),
        pltpu.VMEM((half, width), F32),
        pltpu.VMEM((half, LANES), F32),
        pltpu.VMEM((half, width), F32),
        pltpu.VMEM((half, width), BF16),
        pltpu.VMEM((half, width), F32),
        pltpu.VMEM((chunks // 2, slots, slots), F32),
        pltpu.VMEM((2, half, FF_CHUNK), F32),
        pltpu.VMEM((half, hidden), BF16),
        pltpu.VMEM((chunks, 8, FF_CHUNK), F32),
        pltpu.VMEM((half, width), F32),
        pltpu.VMEM((half, width), BF16),
        pltpu.VMEM((pairs, slots, LANES), BF16),
        pltpu.VMEM((pairs, half, LANES), BF16),
        pltpu.VMEM((slots, 3 * side), BF16),
        pltpu.VMEM((2, span, width), F32),
        pltpu.VMEM((half, width), BF16),
        pltpu.VMEM((half, width), BF16),
        pltpu.VMEM((half, width), BF16),
        pltpu.VMEM((half, width), BF16),
        pltpu.VMEM((seq_size, 8, width), F32),
        pltpu.VMEM((group, 8, width), F32),
        pltpu.VMEM((seq_size, 8, LANES), F32),
        pltpu.VMEM((group, 2, 8, LANES), F32),
        dma((5 + 2 * chunks,)),
        dma((9,)),
        dma((4,)),
        dma((rows,)),
        dma((half_blocks,)),
        dma((half_blocks,)),
        dma((half_blocks,)),
        dma((2,)),
        dma((rows,)),
        dma((half_blocks,)),
        dma((pairs,)),
        dma((pairs,)),
        dma((pairs,)),
        dma((pairs,)),
        dma((half_blocks,)),
        dma((rows,)),
        dma((half_blocks,)),
        dma((half_blocks,)),
        dma((half_blocks,)),
        dma((rows,)),
        dma((seq_size,)),
        dma((seq_size,)),
        dma((group,)),
        dma((group,)),
        dma((seq_size,)),
        dma((seq_size,)),
        dma((group,)),
        dma((group,)),
    ]
    vectors = (
        bias_query,
        bias_value,
        bias_out,
        bias_inner,
        bias_outer,
        gain_attn,
        beta_attn,
        gain_final,
        beta_final,
    )
    layer_home, grad_home, sums_a, sums_b = pl.pallas_call(
        functools.partial(kernel, seq_size, group),
        out_shape=(
            pltpu.VMEM(tokens.shape, BF16),
            pltpu.VMEM(tokens.shape, BF16),
            pltpu.VMEM((8, width), F32),
            pltpu.VMEM((2, 8, LANES), F32),
        ),
        in_specs=[any_space] * 2 + [smem] * 2 + [any_space] * (6 + len(vectors)),
        out_specs=(vmem,) * 4,
        scratch_shapes=scratch,
        compiler_params=pltpu.CompilerParams(
            collective_id=0, has_side_effects=True, vmem_limit_bytes=58 * 2**20
        ),
    )(
        tokens,
        cotangent,
        doc_lengths,
        pad_counts,
        w_query,
        w_key,
        w_value,
        w_out,
        w_inner,
        w_outer,
        *[vector.reshape(1, -1) for vector in vectors],
    )
    line = jax.ShapeDtypeStruct((1, width), F32)
    results = pl.pallas_call(
        finish_kernel,
        out_shape=(
            jax.ShapeDtypeStruct(tokens.shape, BF16),
            jax.ShapeDtypeStruct(tokens.shape, F32),
            line,
            line,
            line,
            jax.ShapeDtypeStruct((1, hidden), F32),
            line,
            line,
            line,
        ),
        in_specs=[vmem] * 4,
        out_specs=(any_space,) * 9,
        scratch_shapes=[
            pltpu.VMEM(tokens.shape, F32),
            pltpu.VMEM((6, 1, width), F32),
            pltpu.VMEM((1, hidden), F32),
            dma((8 + rows,)),
        ],
        compiler_params=pltpu.CompilerParams(vmem_limit_bytes=32 * 2**20),
    )(layer_home, grad_home, sums_a, sums_b)
    return tuple(results[:2]) + tuple(vector.reshape(-1) for vector in results[2:])


def solution(mesh):
    split = P("seq", "head", None)
    placed = (split, P("seq", None), P("seq")) + (P(),) * 15 + (split,)
    return jax.shard_map(
        functools.partial(per_device, mesh.shape["seq"], mesh.shape["head"]),
        mesh=mesh,
        in_specs=placed,
        out_specs=(split, split) + (P(),) * 7,
        check_vma=False,
    )
```

```python
import functools

import jax
import jax.numpy as jnp
from jax import lax
from jax.experimental import pallas as pl
from jax.experimental.pallas import tpu as pltpu
from jax.sharding import PartitionSpec as P

HEADS = 16
LANES = 128
EPS = 1e-06
BIG = 2.0**30
FF_CHUNK = 512
FEATURE_CHUNK = 256
NORM_ROWS = 32
MESH = pl.DeviceIdType.MESH
F32 = jnp.float32
BF16 = jnp.bfloat16


def dot(left, right):
    return lax.dot_general(left, right, (((1,), (0,)), ((), ())), preferred_element_type=F32)


def dot_nt(left, right):
    return lax.dot_general(left, right, (((1,), (1,)), ((), ())), preferred_element_type=F32)


def dot_tn(left, right):
    return lax.dot_general(left, right, (((0,), (0,)), ((), ())), preferred_element_type=F32)


def normed(hidden):
    row_mean = jnp.mean(hidden, axis=-1, keepdims=True)
    centred = hidden - row_mean
    inv_std = lax.rsqrt(jnp.mean(centred * centred, axis=-1, keepdims=True) + EPS)
    return centred * inv_std, inv_std


def norm_back(gradient, norm, inv_std):
    return inv_std * (
        gradient
        - jnp.mean(gradient, axis=-1, keepdims=True)
        - norm * jnp.mean(gradient * norm, axis=-1, keepdims=True)
    )


def fold_rows(block):
    total = block[0:8]
    for start in range(8, block.shape[0], 8):
        total = total + block[start : start + 8]
    return total


def kernel(
    seq_size,
    group,
    tokens,
    cotangent,
    doc_lengths,
    pad_counts,
    w_query,
    w_key,
    w_value,
    w_out,
    w_inner,
    w_outer,
    in_bias_query,
    in_bias_value,
    in_bias_out,
    in_bias_inner,
    in_bias_outer,
    in_gain_attn,
    in_beta_attn,
    in_gain_final,
    in_beta_final,
    layer_home,
    grad_home,
    sums_a,
    sums_b,
    m_qkv,
    m_out,
    m_inner,
    m_outer,
    bias_query,
    bias_value,
    bias_out,
    bias_inner,
    bias_outer,
    gain_attn,
    beta_attn,
    gain_final,
    beta_final,
    row,
    cot,
    info,
    qs,
    ks,
    vs,
    exps,
    recip,
    mixed,
    att,
    att_far,
    norm_a,
    inv_a,
    mid,
    mid_low,
    acc,
    slope,
    raw,
    active,
    inner_sum,
    grad_h,
    grad_low,
    grad_att,
    grad_far,
    grad_qkv,
    key_part,
    value_part,
    docs,
    part,
    part_out,
    part_in,
    grad_out,
    layer_out,
    vec_a,
    pool_a,
    z_a,
    pool_b,
    z_b,
    w_sem,
    vec_sem,
    in_sem,
    tok_send,
    tok_recv,
    pass_send,
    pass_recv,
    info_sem,
    cot_send,
    cot_recv,
    att_send,
    att_recv,
    gat_send,
    gat_recv,
    lay_send,
    lay_recv,
    part_send,
    part_recv,
    grad_send,
    grad_recv,
    pa_send,
    pa_recv,
    za_send,
    za_recv,
    ga_send,
    ga_recv,
    pb_send,
    pb_recv,
    zb_send,
    zb_recv,
):
    rows, span, width = tokens.shape
    half_blocks = group // 2
    slots = span * group
    half = slots // 2
    head_width = width // HEADS
    side = width // 2
    pairs = side // LANES
    chunks = m_inner.shape[0]
    norm_steps = half // NORM_ROWS
    score_scale = head_width**-0.5
    slices = sums_a.shape[0]
    slice_width = width // slices

    seq = lax.axis_index("seq")
    z = lax.axis_index("head")
    core = lax.rem(seq, 2)
    base = seq - core
    partner = base + 1 - core
    z_half = z // half_blocks
    far = 1 - core

    def rows_of(block):
        return pl.ds(pl.multiple_of(block * span, span), span)

    def remote(src, dst, send_sem, recv_sem, at_seq, at_head):
        return pltpu.make_async_remote_copy(
            src_ref=src,
            dst_ref=dst,
            send_sem=send_sem,
            recv_sem=recv_sem,
            device_id=(at_seq, at_head),
            device_id_type=MESH,
        )

    barrier = pltpu.get_barrier_semaphore()

    def greet_z(step, carry):
        pl.semaphore_signal(
            barrier, inc=1, device_id=(seq, lax.rem(z + step, group)), device_id_type=MESH
        )
        return carry

    def greet_seq(step, carry):
        pl.semaphore_signal(
            barrier, inc=1, device_id=(lax.rem(seq + step, seq_size), z), device_id_type=MESH
        )
        return carry

    for r in range(rows):
        target = core * rows + r

        @pl.when(target != z)
        def _():
            pl.semaphore_signal(
                barrier, inc=1, device_id=(base + z_half, target), device_id_type=MESH
            )

    lax.fori_loop(1, seq_size, greet_seq, 0)
    lax.fori_loop(1, group, greet_z, 0)

    mine = pl.ds(pl.multiple_of(core * side, side), side)
    theirs = pl.ds(pl.multiple_of(far * side, side), side)
    qkv_copies = [
        pltpu.make_async_copy(
            weight.at[:, mine], m_qkv.at[:, i * side : (i + 1) * side], w_sem.at[i]
        )
        for i, weight in enumerate((w_query, w_key, w_value))
    ]
    for copy in qkv_copies:
        copy.start()
    vector_copies = [
        pltpu.make_async_copy(source, target, vec_sem.at[i])
        for i, (source, target) in enumerate(
            (
                (in_bias_query, bias_query),
                (in_bias_value, bias_value),
                (in_bias_out, bias_out),
                (in_bias_inner, bias_inner),
                (in_bias_outer, bias_outer),
                (in_gain_attn, gain_attn),
                (in_beta_attn, beta_attn),
                (in_gain_final, gain_final),
                (in_beta_final, beta_final),
            )
        )
    ]
    for copy in vector_copies:
        copy.start()
    out_copies = [
        pltpu.make_async_copy(w_out.at[mine], m_out.at[0:side], w_sem.at[3]),
        pltpu.make_async_copy(w_out.at[theirs], m_out.at[side:width], w_sem.at[4]),
    ]

    def inner_copy(f):
        columns = pl.ds(pl.multiple_of(f * FF_CHUNK, FF_CHUNK), FF_CHUNK)
        return pltpu.make_async_copy(w_inner.at[:, columns], m_inner.at[f], w_sem.at[5 + f])

    def outer_copy(f):
        lines = pl.ds(pl.multiple_of(f * FF_CHUNK, FF_CHUNK), FF_CHUNK)
        return pltpu.make_async_copy(w_outer.at[lines], m_outer.at[lines], w_sem.at[5 + chunks + f])

    line = lax.broadcasted_iota(jnp.int32, (8, LANES), 0)
    for r in range(rows):
        first = doc_lengths[r, 0]
        second = first + doc_lengths[r, 1]
        third = second + doc_lengths[r, 2]
        ends = jnp.where(line == 0, first, jnp.where(line == 1, second, third))
        info[core, r] = jnp.where(line == 3, slots - pad_counts[r], ends)

    peers = jnp.where(z_half == core, rows - 1, rows)
    pl.semaphore_wait(barrier, peers + seq_size - 1 + group - 1)

    def spread(source, target_ref, at, send_sem, recv_sem, local_sem):
        for r in range(rows):
            target = core * rows + r

            @pl.when(target != z)
            def _():
                remote(
                    source.at[r],
                    target_ref.at[at],
                    send_sem.at[r],
                    recv_sem.at[z - z_half * half_blocks],
                    base + z_half,
                    target,
                ).start()

            @pl.when(target == z)
            def _():
                pltpu.make_async_copy(source.at[r], target_ref.at[at], local_sem).start()

    def spread_done(source, target_ref, at, send_sem, recv_sem):
        for r in range(rows):
            target = core * rows + r

            @pl.when(target != z)
            def _():
                remote(
                    source.at[r],
                    target_ref.at[at],
                    send_sem.at[r],
                    recv_sem.at[z - z_half * half_blocks],
                    base + z_half,
                    target,
                ).wait_send()

    def arrived(source, target_ref, at, block, send_sem, recv_sem, local_sem):
        j = block - core * half_blocks

        @pl.when(block != z)
        def _():
            remote(
                source.at[0],
                target_ref.at[at],
                send_sem.at[0],
                recv_sem.at[j],
                base + z_half,
                block,
            ).wait_recv()

        @pl.when(block == z)
        def _():
            pltpu.make_async_copy(source.at[0], target_ref.at[at], local_sem).wait()

    info_copy = remote(info.at[core], info.at[core], info_sem.at[0], info_sem.at[1], partner, z)
    info_copy.start()
    spread(tokens, row, rows_of(z), tok_send, tok_recv, in_sem.at[0])
    for copy in out_copies:
        copy.start()

    def start_inner(f, carry):
        inner_copy(f).start()
        outer_copy(f).start()
        return carry

    lax.fori_loop(0, chunks, start_inner, 0)

    info_copy.wait_send()
    remote(info.at[far], info.at[far], info_sem.at[0], info_sem.at[1], partner, z).wait_recv()
    for copy in qkv_copies + vector_copies:
        copy.wait()

    lane = lax.broadcasted_iota(jnp.int32, (slots, LANES), 1)
    slot = lax.broadcasted_iota(jnp.int32, (slots, LANES), 0)
    ends = info[z_half, z - z_half * rows]
    doc = (slot >= ends[0:1]).astype(jnp.int32)
    for i in range(1, 4):
        doc = doc + (slot >= ends[i : i + 1]).astype(jnp.int32)
    doc_query = jnp.where(doc == lane, BIG, 0.0).astype(BF16)
    doc_key = jnp.where((doc != lane) & (lane < 5), -1.0, 0.0).astype(BF16)
    ones = jnp.ones((slots, LANES), BF16)

    def pass_on(block):
        j = block - core * half_blocks
        at = rows_of(block)
        return remote(row.at[at], row.at[at], pass_send.at[j], pass_recv.at[j], partner, z)

    def project(step, carry):
        near = step < half_blocks
        within = lax.rem(z - z_half * half_blocks + step, half_blocks)
        other = step - half_blocks
        beyond = jnp.where(z_half == 0, half_blocks + other, half_blocks - 1 - other)
        block = jnp.where(near, z_half * half_blocks + within, beyond)
        block_half = block // half_blocks
        at = rows_of(block)

        @pl.when(block_half == core)
        def _():
            arrived(tokens, row, at, block, tok_send, tok_recv, in_sem.at[0])
            pass_on(block).start()

        @pl.when(block_half != core)
        def _():
            j = block - far * half_blocks
            remote(
                row.at[at], row.at[at], pass_send.at[j], pass_recv.at[j], partner, z
            ).wait_recv()

        x = row[at, :]
        q = (dot(x, m_qkv[:, 0:side]) + bias_query[:, mine]) * score_scale
        k = dot(x, m_qkv[:, side : 2 * side])
        v = dot(x, m_qkv[:, 2 * side : 3 * side]) + bias_value[:, mine]
        for p in range(pairs):
            cut = slice(p * LANES, (p + 1) * LANES)
            qs[p, at, :] = q[:, cut].astype(BF16)
            ks[p, at, :] = k[:, cut].astype(BF16)
            vs[p, at, :] = v[:, cut].astype(BF16)
        return carry

    lax.fori_loop(0, group, project, 0)
    spread_done(tokens, row, rows_of(z), tok_send, tok_recv)

    cot_at = pl.ds(pl.multiple_of((z - z_half * half_blocks) * span, span), span)
    spread(cotangent, cot, cot_at, cot_send, cot_recv, in_sem.at[1])

    def pass_wait(j, carry):
        pass_on(core * half_blocks + j).wait_send()
        return carry

    lax.fori_loop(0, half_blocks, pass_wait, 0)

    lane_row = lax.broadcasted_iota(jnp.int32, (1, LANES), 1)
    head_mask = [
        (lane_row < head_width).astype(F32),
        (lane_row >= head_width).astype(F32),
    ]
    low_mask = [mask.astype(BF16) for mask in head_mask]
    near_rows = pl.ds(pl.multiple_of(core * half, half), half)
    far_rows = pl.ds(pl.multiple_of(far * half, half), half)

    def att_copy(p):
        return remote(
            att.at[p, far_rows], att_far.at[p], att_send.at[p], att_recv.at[p], partner, z
        )

    def score(unit):
        at, p, spot = unit
        keys = jnp.concatenate([ks[p], doc_key], axis=1)
        for i in range(2):
            left = jnp.concatenate([qs[p, at, :] * low_mask[i], docs[at, :]], axis=1)
            slope[2 * spot + i, 0:half, :] = dot_nt(left, keys)

    def attend(unit):
        at, p, spot = unit
        values = jnp.concatenate([vs[p], ones], axis=1)
        total = None
        shares = None
        for i in range(2):
            scores = slope[2 * spot + i, 0:half, :]
            exponent = jnp.exp(scores - jnp.max(scores, axis=-1, keepdims=True)).astype(BF16)
            exps[2 * p + i, at, :] = exponent
            both = dot(exponent, values)
            share = 1.0 / both[:, LANES:]
            spread_out = both[:, :LANES] * share * head_mask[i]
            share = share * head_mask[i]
            total = spread_out if total is None else total + spread_out
            shares = share if shares is None else shares + share
        mixed[p, at, :] = total
        recip[p, at, :] = shares
        att[p, at, :] = total.astype(BF16)

    docs[...] = doc_query
    units = [(at, p, p % 2) for at in (far_rows, near_rows) for p in range(pairs)]
    score(units[0])
    for i, unit in enumerate(units):
        if i + 1 < len(units):
            score(units[i + 1])
        attend(unit)
        if i < pairs:
            att_copy(i).start()

    for copy in out_copies:
        copy.wait()
    left = jnp.concatenate([att[p, near_rows, :] for p in range(pairs)], axis=1)
    acc[...] = dot(left, m_out[0:side, :])

    def att_wait(p, carry):
        att_copy(p).wait()
        return carry

    lax.fori_loop(0, pairs, att_wait, 0)
    left = jnp.concatenate([att_far[p] for p in range(pairs)], axis=1)
    acc[...] += dot(left, m_out[side:width, :])

    def lines_of(step):
        return pl.ds(pl.multiple_of(step * NORM_ROWS, NORM_ROWS), NORM_ROWS)

    def norm_first(step, carry):
        at = lines_of(step)
        near = pl.ds(pl.multiple_of(core * half + step * NORM_ROWS, NORM_ROWS), NORM_ROWS)
        hidden = row[near, :].astype(F32) + acc[at, :] + bias_out[...]
        norm, inv_std = normed(hidden)
        norm_a[at, :] = norm
        inv_a[at, :] = jnp.broadcast_to(inv_std, (NORM_ROWS, LANES))
        middle = norm * gain_attn[...] + beta_attn[...]
        mid[at, :] = middle
        mid_low[at, :] = middle.astype(BF16)
        return carry

    lax.fori_loop(0, norm_steps, norm_first, 0, unroll=True)

    def weights_wait(f, carry):
        inner_copy(f).wait()
        outer_copy(f).wait()
        return carry

    lax.fori_loop(0, chunks, weights_wait, 0)

    def slope_at(f):
        return f // 2, slice(f % 2 * half, (f % 2 + 1) * half)

    def activate(f):
        columns = slice(f * FF_CHUNK, (f + 1) * FF_CHUNK)
        inner = raw[f % 2] + bias_inner[:, columns]
        cdf = 0.5 * (1.0 + lax.erf(inner * 0.7071067811865476))
        which, lines = slope_at(f)
        slope[which, lines, :] = cdf + inner * jnp.exp(-0.5 * inner * inner) * 0.3989422804014327
        active[:, columns] = (inner * cdf).astype(BF16)

    raw[0] = dot(mid_low[...], m_inner[0])
    for f in range(chunks):
        if f + 1 < chunks:
            raw[(f + 1) % 2] = dot(mid_low[...], m_inner[f + 1])
        activate(f)
    for n in range(0, width, FEATURE_CHUNK):
        acc[:, n : n + FEATURE_CHUNK] = dot(active[...], m_outer[:, n : n + FEATURE_CHUNK])

    def cot_wait(j, carry):
        at = pl.ds(pl.multiple_of(j * span, span), span)
        arrived(cotangent, cot, at, core * half_blocks + j, cot_send, cot_recv, in_sem.at[1])
        return carry

    lax.fori_loop(0, half_blocks, cot_wait, 0)

    live_end = ends[3:4, 0:1]
    zero_sum = jnp.zeros((8, width), F32)

    def norm_last(step, carry):
        beta_sum, outer_sum = carry
        at = lines_of(step)
        hidden = mid[at, :] + acc[at, :] + bias_outer[...]
        norm, inv_std = normed(hidden)
        place = lax.broadcasted_iota(jnp.int32, (NORM_ROWS, 1), 0) + core * half + step * NORM_ROWS
        live = (place < live_end).astype(F32)
        layer_out[at, :] = (live * (norm * gain_final[...] + beta_final[...])).astype(BF16)
        grad_final = live * cot[at, :].astype(F32)
        grad_hidden = norm_back(grad_final * gain_final[...], norm, inv_std)
        grad_h[at, :] = grad_hidden
        grad_low[at, :] = grad_hidden.astype(BF16)
        return beta_sum + fold_rows(grad_final), outer_sum + fold_rows(grad_hidden)

    def home_block(block, source, target_ref, send_sem, recv_sem, local_sem):
        j = block - core * half_blocks
        src = source.at[pl.ds(pl.multiple_of(j * span, span), span)]
        line_at = z - z_half * rows

        @pl.when(block != z)
        def _():
            remote(
                src,
                target_ref.at[line_at],
                send_sem.at[j],
                recv_sem.at[line_at],
                base + z_half,
                block,
            ).start()

        @pl.when(block == z)
        def _():
            pltpu.make_async_copy(src, target_ref.at[line_at], local_sem).start()

    def home_done(source, target_ref, send_sem, recv_sem, local_sem):
        for j in range(half_blocks):
            block = core * half_blocks + j
            src = source.at[j * span : (j + 1) * span]
            line_at = z - z_half * rows

            @pl.when(block != z)
            def _():
                remote(
                    src,
                    target_ref.at[line_at],
                    send_sem.at[j],
                    recv_sem.at[line_at],
                    base + z_half,
                    block,
                ).wait_send()

            @pl.when(block == z)
            def _():
                pltpu.make_async_copy(src, target_ref.at[line_at], local_sem).wait()

        for r in range(rows):
            target = core * rows + r

            @pl.when(target != z)
            def _():
                remote(
                    source.at[0:span],
                    target_ref.at[r],
                    send_sem.at[0],
                    recv_sem.at[r],
                    base + z_half,
                    target,
                ).wait_recv()

    block_steps = span // NORM_ROWS
    sums = (zero_sum, zero_sum)
    for j in range(half_blocks):
        sums = lax.fori_loop(
            j * block_steps, (j + 1) * block_steps, norm_last, sums, unroll=True
        )
        home_block(
            core * half_blocks + j, layer_out, layer_home, lay_send, lay_recv, in_sem.at[2]
        )
    vec_a[3:4, :] = jnp.sum(sums[0], axis=0, keepdims=True)
    vec_a[1:2, :] = jnp.sum(sums[1], axis=0, keepdims=True)

    for f in range(chunks):
        which, lines = slope_at(f)
        columns = slice(f * FF_CHUNK, (f + 1) * FF_CHUNK)
        grad_active = dot_nt(grad_low[...], m_outer[columns, :])
        grad_inner = (grad_active * slope[which, lines, :]).astype(BF16)
        active[:, columns] = grad_inner
        inner_sum[f] = fold_rows(grad_inner.astype(F32))
    for n in range(0, width, FEATURE_CHUNK):
        total = None
        for f in range(chunks):
            term = dot_nt(
                active[:, f * FF_CHUNK : (f + 1) * FF_CHUNK], m_inner[f, n : n + FEATURE_CHUNK, :]
            )
            total = term if total is None else total + term
        acc[:, n : n + FEATURE_CHUNK] = total
    per_line = width // FF_CHUNK
    for f in range(chunks):
        line_at = 4 + f // per_line
        column = f % per_line * FF_CHUNK
        vec_a[line_at : line_at + 1, column : column + FF_CHUNK] = jnp.sum(
            inner_sum[f], axis=0, keepdims=True
        )

    def norm_first_back(step, carry):
        beta_sum, out_sum = carry
        at = lines_of(step)
        grad_middle = grad_h[at, :] + acc[at, :]
        grad_hidden = norm_back(grad_middle * gain_attn[...], norm_a[at, :], inv_a[at, 0:1])
        grad_h[at, :] = grad_hidden
        grad_low[at, :] = grad_hidden.astype(BF16)
        return beta_sum + fold_rows(grad_middle), out_sum + fold_rows(grad_hidden)

    beta_attn_sum, out_sum = lax.fori_loop(
        0, norm_steps, norm_first_back, (zero_sum, zero_sum), unroll=True
    )
    vec_a[2:3, :] = jnp.sum(beta_attn_sum, axis=0, keepdims=True)
    vec_a[0:1, :] = jnp.sum(out_sum, axis=0, keepdims=True)

    def all_peers(start, size, here, make, wait):
        def go(step, carry):
            peer = start + lax.rem(here - start + step, size)
            send, receive = make(step, peer)
            if wait:
                remote(*send).wait_send()
                remote(*receive).wait_recv()
            else:
                remote(*send).start()
            return carry

        lax.fori_loop(1, size, go, 0)

    def plane_a(step, peer):
        piece = pl.ds(pl.multiple_of(lax.rem(peer, slices) * slice_width, LANES), slice_width)
        return (
            (vec_a.at[:, piece], pool_a.at[seq], pa_send.at[step], pa_recv.at[seq], peer, z),
            (vec_a.at[:, piece], pool_a.at[peer], pa_send.at[step], pa_recv.at[peer], peer, z),
        )

    def column_a(step, peer):
        return (
            (z_a.at[z], z_a.at[z], za_send.at[step], za_recv.at[z], seq, peer),
            (z_a.at[peer], z_a.at[peer], za_send.at[step], za_recv.at[peer], seq, peer),
        )

    own_slice = lax.rem(seq, slices)

    def gather_a(step, peer):
        there = lax.rem(peer, slices)
        return (
            (
                sums_a.at[own_slice],
                sums_a.at[own_slice],
                ga_send.at[step],
                ga_recv.at[own_slice],
                peer,
                z,
            ),
            (
                sums_a.at[there], sums_a.at[there], ga_send.at[step], ga_recv.at[there], peer, z
            ),
        )

    def column_b(step, peer):
        return (
            (z_b.at[z], z_b.at[z], zb_send.at[step], zb_recv.at[z], seq, peer),
            (z_b.at[peer], z_b.at[peer], zb_send.at[step], zb_recv.at[peer], seq, peer),
        )

    def plane_b(step, peer):
        return (
            (pool_b.at[seq], pool_b.at[seq], pb_send.at[step], pb_recv.at[seq], peer, z),
            (pool_b.at[peer], pool_b.at[peer], pb_send.at[step], pb_recv.at[peer], peer, z),
        )

    def total_of(pool, places):
        total = pool[places[0]]
        for place in places[1:]:
            total = total + pool[place]
        return total

    all_peers(0, seq_size, seq, plane_a, False)
    pool_a[seq] = vec_a[:, pl.ds(pl.multiple_of(own_slice * slice_width, LANES), slice_width)]

    def gat_copy(p):
        return remote(
            grad_far.at[p], grad_att.at[p, near_rows], gat_send.at[p], gat_recv.at[p], partner, z
        )

    lines = dot_nt(grad_low[...], m_out[side:width, :])
    for p in range(pairs):
        grad_far[p] = lines[:, p * LANES : (p + 1) * LANES].astype(BF16)
        gat_copy(p).start()
    lines = dot_nt(grad_low[...], m_out[0:side, :])
    for p in range(pairs):
        grad_att[p, near_rows, :] = lines[:, p * LANES : (p + 1) * LANES].astype(BF16)

    def gat_wait(p, carry):
        gat_copy(p).wait_send()
        remote(
            grad_far.at[p], grad_att.at[p, far_rows], gat_send.at[p], gat_recv.at[p], partner, z
        ).wait_recv()
        return carry

    def attend_back(at, p, first):
        keys = ks[p]
        turned = qs[p, at, :].T
        values = jnp.concatenate([vs[p], ones], axis=1)
        scaled = (grad_att[p, at, :].astype(F32) * recip[p, at, :]).astype(BF16)
        product = scaled.astype(F32) * mixed[p, at, :]
        dq = None
        dk = []
        dv = []
        for i in range(2):
            cut = slice(i * head_width, (i + 1) * head_width)
            delta = jnp.sum(product * head_mask[i], axis=-1, keepdims=True)
            high = delta.astype(BF16).astype(F32)
            extra = jnp.where(half_lane == 0, -high, jnp.where(half_lane == 1, high - delta, 0.0))
            grads = scaled * low_mask[i]
            left = jnp.concatenate([grads, extra.astype(BF16)], axis=1)
            exponent = exps[2 * p + i, at, :]
            grad_scores = (exponent.astype(F32) * dot_nt(left, values)).astype(BF16)
            term = dot(grad_scores, keys * low_mask[i])
            dq = term if dq is None else dq + term
            dk.append(dot(turned[cut], grad_scores))
            dv.append(dot(grads.T[cut], exponent))
        dq = (dq * score_scale).astype(BF16)
        dk = jnp.concatenate(dk, axis=0)
        dv = jnp.concatenate(dv, axis=0)
        grad_qkv[at, p * LANES : (p + 1) * LANES] = dq
        dq_sum = jnp.sum(fold_rows(dq.astype(F32)), axis=0, keepdims=True)
        if first:
            key_part[p] = dk
            value_part[p] = dv
            z_b[z, p : p + 1, :] = dq_sum
        else:
            dk = (dk + key_part[p]).astype(BF16).T
            dv = (dv + value_part[p]).astype(BF16).T
            grad_qkv[:, side + p * LANES : side + (p + 1) * LANES] = dk
            grad_qkv[:, 2 * side + p * LANES : 2 * side + (p + 1) * LANES] = dv
            z_b[z, p : p + 1, :] += dq_sum
            z_b[z, pairs + p : pairs + p + 1, :] = jnp.sum(
                fold_rows(dv.astype(F32)), axis=0, keepdims=True
            )

    half_lane = lax.broadcasted_iota(jnp.int32, (half, LANES), 1)
    for p in range(pairs):
        attend_back(near_rows, p, True)
    all_peers(0, seq_size, seq, plane_a, True)
    z_a[z] = total_of(pool_a, range(seq_size))
    all_peers(0, group, z, column_a, False)
    lax.fori_loop(0, pairs, gat_wait, 0)
    for p in range(pairs):
        attend_back(far_rows, p, False)
    all_peers(0, group, z, column_b, False)

    def half_of(step):
        return 1 - z_half if step < 2 else z_half

    def part_copy(c):
        return remote(part_out.at[c], part_in.at[c], part_send.at[c], part_recv.at[c], partner, z)

    def grad_block(j, c):
        return (
            core * half_blocks + j,
            grad_out.at[c],
            grad_home.at[:, c],
            grad_send.at[c],
            grad_recv.at[c],
            in_sem.at[3 + c],
        )

    def token_grad(step):
        c = step % 2
        own = half_of(step)
        at = pl.ds(pl.multiple_of(own * half, half), half)
        columns = slice(c * side, (c + 1) * side)
        term = dot_nt(grad_qkv[at, :], m_qkv[columns, :])

        @pl.when(own == core)
        def _():
            part[c] = term

        @pl.when(own != core)
        def _():
            part_out[c] = term.astype(BF16)
            part_copy(c).start()

    def finish(step):
        c = step % 2
        columns = slice(c * side, (c + 1) * side)

        @pl.when(half_of(step) == core)
        def _():
            part_copy(c).wait_recv()
            total = grad_h[:, columns] + part[c] + part_in[c].astype(F32)
            grad_out[c] = total.astype(BF16)
            for j in range(half_blocks):
                home_block(*grad_block(j, c))

    token_grad(0)
    token_grad(1)
    finish(0)
    all_peers(0, group, z, column_a, True)
    sums_a[own_slice] = total_of(z_a, range(group))
    all_peers(seq - own_slice, slices, seq, gather_a, False)
    finish(1)
    token_grad(2)
    token_grad(3)
    finish(2)
    all_peers(0, group, z, column_b, True)
    pool_b[seq] = total_of(z_b, range(group))
    all_peers(0, seq_size, seq, plane_b, False)
    finish(3)

    for c in range(2):
        part_copy(c).wait_send()
    all_peers(seq - own_slice, slices, seq, gather_a, True)
    all_peers(0, seq_size, seq, plane_b, True)
    for i in range(2):
        sums_b[i] = total_of(pool_b, range(i, seq_size, 2))
    spread_done(cotangent, cot, cot_at, cot_send, cot_recv)
    home_done(layer_out, layer_home, lay_send, lay_recv, in_sem.at[2])
    for c in range(2):
        home_done(*grad_block(0, c)[1:])


def finish_kernel(
    layer,
    grad,
    sums_a,
    sums_b,
    layer_out,
    input_grad,
    grad_bias_query,
    grad_bias_value,
    grad_bias_out,
    grad_bias_inner,
    grad_bias_outer,
    grad_beta_attn,
    grad_beta_final,
    wide,
    lines,
    inner_line,
    sems,
):
    rows, span, width = layer.shape
    slices, _, slice_width = sums_a.shape
    copies = [pltpu.make_async_copy(layer, layer_out, sems.at[0])]
    copies[0].start()
    for r in range(rows):
        for c in range(2):
            wide[r, :, c * width // 2 : (c + 1) * width // 2] = grad[r, c].astype(F32)
        copies.append(pltpu.make_async_copy(wide.at[r], input_grad.at[r], sems.at[1 + r]))
        copies[-1].start()
    pairs = sums_b.shape[1] // 2
    for i in range(2):
        for p in range(pairs):
            column = (i * pairs + p) * LANES
            lines[0, :, column : column + LANES] = sums_b[i, p : p + 1, :]
            lines[1, :, column : column + LANES] = sums_b[i, pairs + p : pairs + p + 1, :]
    for j in range(slices):
        column = j * slice_width
        for i in range(4):
            lines[2 + i, :, column : column + slice_width] = sums_a[j, i : i + 1, :]
            inner_line[:, i * width + column : i * width + column + slice_width] = sums_a[
                j, 4 + i : 5 + i, :
            ]
    targets = (
        grad_bias_query,
        grad_bias_value,
        grad_bias_out,
        grad_bias_outer,
        grad_beta_attn,
        grad_beta_final,
    )
    for i, target in enumerate(targets):
        copies.append(pltpu.make_async_copy(lines.at[i], target, sems.at[1 + rows + i]))
        copies[-1].start()
    copies.append(pltpu.make_async_copy(inner_line, grad_bias_inner, sems.at[7 + rows]))
    copies[-1].start()
    for copy in copies:
        copy.wait()


def per_device(
    seq_size,
    group,
    tokens,
    doc_lengths,
    pad_counts,
    w_query,
    w_key,
    w_value,
    w_out,
    w_inner,
    w_outer,
    bias_query,
    bias_value,
    bias_out,
    bias_inner,
    bias_outer,
    gain_attn,
    beta_attn,
    gain_final,
    beta_final,
    cotangent,
):
    rows, span, width = tokens.shape
    hidden = w_inner.shape[1]
    slots = span * group
    half = slots // 2
    half_blocks = group // 2
    side = width // 2
    pairs = side // LANES
    chunks = hidden // FF_CHUNK
    slices = min(8, seq_size)
    slice_width = width // slices
    if rows * 2 != group or pairs != 4 or hidden != 4 * width or slots != FF_CHUNK:
        raise ValueError("unsupported sizes")

    any_space = pl.BlockSpec(memory_space=pl.ANY)
    vmem = pl.BlockSpec(memory_space=pltpu.VMEM)
    smem = pl.BlockSpec(memory_space=pltpu.SMEM)
    dma = pltpu.SemaphoreType.DMA
    scratch = [
        pltpu.VMEM((width, 3 * side), BF16),
        pltpu.VMEM((width, width), BF16),
        pltpu.VMEM((chunks, width, FF_CHUNK), BF16),
        pltpu.VMEM((hidden, width), BF16),
        pltpu.VMEM((1, width), F32),
        pltpu.VMEM((1, width), F32),
        pltpu.VMEM((1, width), F32),
        pltpu.VMEM((1, hidden), F32),
        pltpu.VMEM((1, width), F32),
        pltpu.VMEM((1, width), F32),
        pltpu.VMEM((1, width), F32),
        pltpu.VMEM((1, width), F32),
        pltpu.VMEM((1, width), F32),
        pltpu.VMEM((slots, width), BF16),
        pltpu.VMEM((half, width), BF16),
        pltpu.VMEM((2, rows, 8, LANES), jnp.int32),
        pltpu.VMEM((pairs, slots, LANES), BF16),
        pltpu.VMEM((pairs, slots, LANES), BF16),
        pltpu.VMEM((pairs, slots, LANES), BF16),
        pltpu.VMEM((2 * pairs, slots, slots), BF16),
        pltpu.VMEM((pairs, slots, LANES), F32),
        pltpu.VMEM((pairs, slots, LANES), F32),
        pltpu.VMEM((pairs, slots, LANES), BF16),
        pltpu.VMEM((pairs, half, LANES), BF16),
        pltpu.VMEM((half, width), F32),
        pltpu.VMEM((half, LANES), F32),
        pltpu.VMEM((half, width), F32),
        pltpu.VMEM((half, width), BF16),
        pltpu.VMEM((half, width), F32),
        pltpu.VMEM((chunks // 2, slots, slots), F32),
        pltpu.VMEM((2, half, FF_CHUNK), F32),
        pltpu.VMEM((half, hidden), BF16),
        pltpu.VMEM((chunks, 8, FF_CHUNK), F32),
        pltpu.VMEM((half, width), F32),
        pltpu.VMEM((half, width), BF16),
        pltpu.VMEM((pairs, slots, LANES), BF16),
        pltpu.VMEM((pairs, half, LANES), BF16),
        pltpu.VMEM((slots, 3 * side), BF16),
        pltpu.VMEM((pairs, LANES, slots), F32),
        pltpu.VMEM((pairs, LANES, slots), F32),
        pltpu.VMEM((slots, LANES), BF16),
        pltpu.VMEM((2, half, side), F32),
        pltpu.VMEM((2, half, side), BF16),
        pltpu.VMEM((2, half, side), BF16),
        pltpu.VMEM((2, half, side), BF16),
        pltpu.VMEM((half, width), BF16),
        pltpu.VMEM((8, width), F32),
        pltpu.VMEM((seq_size, 8, slice_width), F32),
        pltpu.VMEM((group, 8, slice_width), F32),
        pltpu.VMEM((seq_size, 8, LANES), F32),
        pltpu.VMEM((group, 8, LANES), F32),
        dma((5 + 2 * chunks,)),
        dma((9,)),
        dma((5,)),
        dma((rows,)),
        dma((half_blocks,)),
        dma((half_blocks,)),
        dma((half_blocks,)),
        dma((2,)),
        dma((rows,)),
        dma((half_blocks,)),
        dma((pairs,)),
        dma((pairs,)),
        dma((pairs,)),
        dma((pairs,)),
        dma((half_blocks,)),
        dma((rows,)),
        dma((2,)),
        dma((2,)),
        dma((2, half_blocks)),
        dma((2, rows)),
        dma((seq_size,)),
        dma((seq_size,)),
        dma((group,)),
        dma((group,)),
        dma((slices,)),
        dma((slices,)),
        dma((seq_size,)),
        dma((seq_size,)),
        dma((group,)),
        dma((group,)),
    ]
    vectors = (
        bias_query,
        bias_value,
        bias_out,
        bias_inner,
        bias_outer,
        gain_attn,
        beta_attn,
        gain_final,
        beta_final,
    )
    layer_home, grad_home, sums_a, sums_b = pl.pallas_call(
        functools.partial(kernel, seq_size, group),
        out_shape=(
            pltpu.VMEM(tokens.shape, BF16),
            pltpu.VMEM((rows, 2, span, side), BF16),
            pltpu.VMEM((slices, 8, slice_width), F32),
            pltpu.VMEM((2, 8, LANES), F32),
        ),
        in_specs=[any_space] * 2 + [smem] * 2 + [any_space] * (6 + len(vectors)),
        out_specs=(vmem,) * 4,
        scratch_shapes=scratch,
        compiler_params=pltpu.CompilerParams(
            collective_id=0, has_side_effects=True, vmem_limit_bytes=58 * 2**20
        ),
    )(
        tokens,
        cotangent,
        doc_lengths,
        pad_counts,
        w_query,
        w_key,
        w_value,
        w_out,
        w_inner,
        w_outer,
        *[vector.reshape(1, -1) for vector in vectors],
    )
    line = jax.ShapeDtypeStruct((1, width), F32)
    results = pl.pallas_call(
        finish_kernel,
        out_shape=(
            jax.ShapeDtypeStruct(tokens.shape, BF16),
            jax.ShapeDtypeStruct(tokens.shape, F32),
            line,
            line,
            line,
            jax.ShapeDtypeStruct((1, hidden), F32),
            line,
            line,
            line,
        ),
        in_specs=[vmem] * 4,
        out_specs=(any_space,) * 9,
        scratch_shapes=[
            pltpu.VMEM(tokens.shape, F32),
            pltpu.VMEM((6, 1, width), F32),
            pltpu.VMEM((1, hidden), F32),
            dma((8 + rows,)),
        ],
        compiler_params=pltpu.CompilerParams(vmem_limit_bytes=32 * 2**20),
    )(layer_home, grad_home, sums_a, sums_b)
    return tuple(results[:2]) + tuple(vector.reshape(-1) for vector in results[2:])


def solution(mesh):
    split = P("seq", "head", None)
    placed = (split, P("seq", None), P("seq")) + (P(),) * 15 + (split,)
    return jax.shard_map(
        functools.partial(per_device, mesh.shape["seq"], mesh.shape["head"]),
        mesh=mesh,
        in_specs=placed,
        out_specs=(split, split) + (P(),) * 7,
        check_vma=False,
    )
```

```python
import functools

import jax
import jax.numpy as jnp
from jax import lax
from jax.experimental import pallas as pl
from jax.experimental.pallas import tpu as pltpu
from jax.sharding import PartitionSpec as P

HEADS = 16
LANES = 128
EPS = 1e-06
BIG = 2.0**30
FF_CHUNK = 512
FEATURE_CHUNK = 256
NORM_ROWS = 32
GRAD_COLUMNS = 512
GRAD_LAG = 1
MESH = pl.DeviceIdType.MESH
F32 = jnp.float32
BF16 = jnp.bfloat16


def dot(left, right):
    return lax.dot_general(left, right, (((1,), (0,)), ((), ())), preferred_element_type=F32)


def dot_nt(left, right):
    return lax.dot_general(left, right, (((1,), (1,)), ((), ())), preferred_element_type=F32)


def dot_tn(left, right):
    return lax.dot_general(left, right, (((0,), (0,)), ((), ())), preferred_element_type=F32)


def normed(hidden):
    row_mean = jnp.mean(hidden, axis=-1, keepdims=True)
    centred = hidden - row_mean
    inv_std = lax.rsqrt(jnp.mean(centred * centred, axis=-1, keepdims=True) + EPS)
    return centred * inv_std, inv_std


def norm_back(gradient, norm, inv_std):
    return inv_std * (
        gradient
        - jnp.mean(gradient, axis=-1, keepdims=True)
        - norm * jnp.mean(gradient * norm, axis=-1, keepdims=True)
    )


def fold_rows(block):
    total = block[0:8]
    for start in range(8, block.shape[0], 8):
        total = total + block[start : start + 8]
    return total


def kernel(
    seq_size,
    group,
    tokens,
    cotangent,
    doc_lengths,
    pad_counts,
    w_query,
    w_key,
    w_value,
    w_out,
    w_inner,
    w_outer,
    in_bias_query,
    in_bias_value,
    in_bias_out,
    in_bias_inner,
    in_bias_outer,
    in_gain_attn,
    in_beta_attn,
    in_gain_final,
    in_beta_final,
    layer_home,
    grad_home,
    sums_a,
    sums_b,
    m_qkv,
    m_out,
    m_inner,
    m_outer,
    vectors,
    bias_inner,
    row,
    cot,
    info,
    qs,
    ks,
    vs,
    exps,
    recip,
    mixed,
    att,
    att_far,
    norm_a,
    inv_a,
    mid,
    mid_low,
    acc,
    slope,
    raw,
    active,
    inner_sum,
    grad_h,
    grad_low,
    grad_att,
    grad_far,
    grad_qkv,
    turned,
    lefts,
    grads_turned,
    grad_scores,
    part,
    part_out,
    part_in,
    grad_out,
    layer_out,
    vec_a,
    pool_a,
    z_a,
    pool_b,
    z_b,
    w_sem,
    in_sem,
    tok_send,
    tok_recv,
    pass_send,
    pass_recv,
    info_sem,
    cot_send,
    cot_recv,
    att_send,
    att_recv,
    gat_send,
    gat_recv,
    lay_send,
    lay_recv,
    part_send,
    part_recv,
    grad_send,
    grad_recv,
    bias_send,
    bias_recv,
):
    rows, span, width = tokens.shape
    half_blocks = group // 2
    slots = span * group
    half = slots // 2
    head_width = width // HEADS
    side = width // 2
    pairs = side // LANES
    chunks = m_inner.shape[0]
    norm_steps = half // NORM_ROWS
    score_scale = head_width**-0.5
    slices = sums_a.shape[0]
    slice_width = width // slices

    seq = lax.axis_index("seq")
    z = lax.axis_index("head")
    core = lax.rem(seq, 2)
    base = seq - core
    partner = base + 1 - core
    z_half = z // half_blocks
    far = 1 - core

    def near_at(j):
        return pl.ds(pl.multiple_of(half + j * span, span), span)

    def far_at(j):
        return pl.ds(pl.multiple_of(j * span, span), span)

    def remote(src, dst, send_sem, recv_sem, at_seq, at_head):
        return pltpu.make_async_remote_copy(
            src_ref=src,
            dst_ref=dst,
            send_sem=send_sem,
            recv_sem=recv_sem,
            device_id=(at_seq, at_head),
            device_id_type=MESH,
        )

    barrier = pltpu.get_barrier_semaphore()

    def greet_z(step, carry):
        pl.semaphore_signal(
            barrier, inc=1, device_id=(seq, lax.rem(z + step, group)), device_id_type=MESH
        )
        return carry

    def greet_seq(step, carry):
        pl.semaphore_signal(
            barrier, inc=1, device_id=(lax.rem(seq + step, seq_size), z), device_id_type=MESH
        )
        return carry

    for r in range(rows):
        target = core * rows + r

        @pl.when(target != z)
        def _():
            pl.semaphore_signal(
                barrier, inc=1, device_id=(base + z_half, target), device_id_type=MESH
            )

    lax.fori_loop(1, seq_size, greet_seq, 0)
    lax.fori_loop(1, group, greet_z, 0)

    mine = pl.ds(pl.multiple_of(core * side, side), side)
    theirs = pl.ds(pl.multiple_of(far * side, side), side)
    for i, weight in enumerate((w_query, w_key, w_value)):
        pltpu.make_async_copy(
            weight.at[:, mine], m_qkv.at[:, i * side : (i + 1) * side], w_sem.at[0]
        ).start()
    for i, vector in enumerate(
        (
            in_bias_query,
            in_bias_value,
            in_bias_out,
            in_bias_outer,
            in_gain_attn,
            in_beta_attn,
            in_gain_final,
            in_beta_final,
        )
    ):
        pltpu.make_async_copy(vector, vectors.at[i], w_sem.at[4]).start()
    pltpu.make_async_copy(in_bias_inner, bias_inner, w_sem.at[5]).start()

    def loaded(target, i):
        pltpu.make_async_copy(target, target, w_sem.at[i]).wait()

    line = lax.broadcasted_iota(jnp.int32, (8, LANES), 0)
    for r in range(rows):
        first = doc_lengths[r, 0]
        second = first + doc_lengths[r, 1]
        third = second + doc_lengths[r, 2]
        ends = jnp.where(line == 0, first, jnp.where(line == 1, second, third))
        info[core, r] = jnp.where(line == 3, slots - pad_counts[r], ends)

    peers = jnp.where(z_half == core, rows - 1, rows)
    pl.semaphore_wait(barrier, peers + seq_size - 1 + group - 1)

    early = (z >= half_blocks // 2) & (z < group - half_blocks // 2)

    def spread(index, source, target_ref, at, send_sem, recv_sem):
        r = jnp.where(core == 0, rows - 1 - index, index)
        target = core * rows + r

        @pl.when(target != z)
        def _():
            remote(
                source.at[r],
                target_ref.at[at],
                send_sem.at[r],
                recv_sem.at[z - z_half * half_blocks],
                base + z_half,
                target,
            ).start()

    def keep(source, target_ref, at, local_sem):
        @pl.when(core == z_half)
        def _():
            pltpu.make_async_copy(
                source.at[z - z_half * rows], target_ref.at[at], local_sem
            ).start()

    def spread_done(index, source, target_ref, at, send_sem, recv_sem):
        r = jnp.where(core == 0, rows - 1 - index, index)
        target = core * rows + r

        @pl.when(target != z)
        def _():
            remote(
                source.at[r],
                target_ref.at[at],
                send_sem.at[r],
                recv_sem.at[z - z_half * half_blocks],
                base + z_half,
                target,
            ).wait_send()

    def arrived(source, target_ref, at, block, send_sem, recv_sem, local_sem):
        j = block - core * half_blocks

        @pl.when(block != z)
        def _():
            remote(
                source.at[0],
                target_ref.at[at],
                send_sem.at[0],
                recv_sem.at[j],
                base + z_half,
                block,
            ).wait_recv()

        @pl.when(block == z)
        def _():
            pltpu.make_async_copy(source.at[0], target_ref.at[at], local_sem).wait()

    info_copy = remote(info.at[core], info.at[core], info_sem.at[0], info_sem.at[1], partner, z)
    info_copy.start()
    tok_at = near_at(z - z_half * half_blocks)
    cot_at = pl.ds(pl.multiple_of((z - z_half * half_blocks) * span, span), span)

    def send_tokens():
        for index in range(rows):
            spread(index, tokens, row, tok_at, tok_send, tok_recv)

    def tokens_sent():
        for index in range(rows):
            spread_done(index, tokens, row, tok_at, tok_send, tok_recv)

    def send_cotangents():
        for index in range(rows):
            spread(index, cotangent, cot, cot_at, cot_send, cot_recv)

    def cotangents_sent():
        for index in range(rows):
            spread_done(index, cotangent, cot, cot_at, cot_send, cot_recv)

    send_tokens()
    keep(tokens, row, tok_at, in_sem.at[0])
    keep(cotangent, cot, cot_at, in_sem.at[1])
    pltpu.make_async_copy(w_out.at[mine], m_out.at[0:side], w_sem.at[1]).start()
    pltpu.make_async_copy(w_out.at[theirs], m_out.at[side:width], w_sem.at[1]).start()
    for f in range(chunks):
        columns = slice(f * FF_CHUNK, (f + 1) * FF_CHUNK)
        pltpu.make_async_copy(w_inner.at[:, columns], m_inner.at[f], w_sem.at[2]).start()
    pltpu.make_async_copy(w_outer, m_outer, w_sem.at[3]).start()

    info_copy.wait_send()
    remote(info.at[far], info.at[far], info_sem.at[0], info_sem.at[1], partner, z).wait_recv()
    loaded(m_qkv, 0)
    loaded(vectors, 4)
    loaded(bias_inner, 5)
    bias_query = vectors[0, :, mine]
    bias_value = vectors[1, :, mine]

    lane = lax.broadcasted_iota(jnp.int32, (slots, LANES), 1)
    place = lax.broadcasted_iota(jnp.int32, (slots, LANES), 0)
    slot = jnp.where(place < half, far * half + place, core * half + place - half)
    ends = info[z_half, z - z_half * rows]
    doc = (slot >= ends[0:1]).astype(jnp.int32)
    for i in range(1, 4):
        doc = doc + (slot >= ends[i : i + 1]).astype(jnp.int32)
    doc_query = jnp.where(doc == lane, BIG, 0.0).astype(BF16)
    doc_key = jnp.where((doc != lane) & (lane < 5), -1.0, 0.0).astype(BF16)
    ones = jnp.ones((slots, LANES), BF16)

    def pass_on(j):
        return remote(
            row.at[near_at(j)], row.at[far_at(j)], pass_send.at[j], pass_recv.at[j], partner, z
        )

    def taken(which, step):
        local = lax.rem(z - z_half * half_blocks + step, half_blocks)
        beyond = jnp.where(z_half == 0, half_blocks - 1 - step, step)
        return jnp.where(which == z_half, local, beyond)

    def project(at):
        x = row[at, :]
        q = (dot(x, m_qkv[:, 0:side]) + bias_query) * score_scale
        k = dot(x, m_qkv[:, side : 2 * side])
        v = dot(x, m_qkv[:, 2 * side : 3 * side]) + bias_value
        for p in range(pairs):
            cut = slice(p * LANES, (p + 1) * LANES)
            qs[p, at, :] = q[:, cut].astype(BF16)
            ks[p, at, :] = k[:, cut].astype(BF16)
            vs[p, at, :] = v[:, cut].astype(BF16)


    def project_step(i, carry):
        in_turn = core == z_half
        own = jnp.where(in_turn, i < half_blocks, lax.rem(i, 2) == 1)
        step = jnp.where(in_turn, lax.rem(i, half_blocks), i // 2)
        j = taken(jnp.where(own, core, far), step)

        @pl.when(own)
        def _():
            block = core * half_blocks + j
            arrived(tokens, row, near_at(j), block, tok_send, tok_recv, in_sem.at[0])
            pass_on(j).start()

            @pl.when((i == group - 1) & jnp.logical_not(early))
            def _():
                send_cotangents()

        @pl.when(jnp.logical_not(own))
        def _():
            pass_on(j).wait_recv()

        project(pl.ds(pl.multiple_of(jnp.where(own, half, 0) + j * span, span), span))
        return carry

    lax.fori_loop(0, group, project_step, 0)

    @pl.when((core == z_half) & jnp.logical_not(early))
    def _():
        send_cotangents()

    for i, target in enumerate((m_out, m_inner, m_outer)):
        loaded(target, 1 + i)

    lane_row = lax.broadcasted_iota(jnp.int32, (1, LANES), 1)
    head_mask = [
        (lane_row < head_width).astype(F32),
        (lane_row >= head_width).astype(F32),
    ]
    low_mask = [mask.astype(BF16) for mask in head_mask]
    near_rows = slice(half, slots)
    far_rows = slice(0, half)

    def score(unit, spot):
        head, at = unit
        p = head // 2
        left = jnp.concatenate([qs[p, at, :] * low_mask[head % 2], doc_query[at, :]], axis=1)
        keys = jnp.concatenate([ks[p], doc_key], axis=1)
        slope[spot, 0:half, :] = dot_nt(left, keys)

    def soften(unit, spot):
        head, at = unit
        scores = slope[spot, 0:half, :]
        exponent = jnp.exp(scores - jnp.max(scores, axis=-1, keepdims=True))
        exps[head, at, :] = exponent.astype(BF16)

    def mix(unit):
        head, at = unit
        both = dot(exps[head, at, :], jnp.concatenate([vs[head // 2], ones], axis=1))
        share = 1.0 / both[:, LANES:]
        return both[:, :LANES] * share * head_mask[head % 2], share * head_mask[head % 2]

    units = [(head, at) for at in (far_rows, near_rows) for head in range(2 * pairs)]
    spots = slope.shape[0]
    score(units[0], 0)
    for i in range(len(units) + 1):
        if i + 1 < len(units):
            score(units[i + 1], (i + 1) % spots)
        if i > 0:
            head, at = units[i - 1]
            if head % 2 == 0:
                held = mix(units[i - 1])
            else:
                total, shares = (a + b for a, b in zip(held, mix(units[i - 1])))
                p = head // 2
                mixed[p, at, :] = total
                recip[p, at, :] = shares
                att[p, at, :] = total.astype(BF16)
        if i < len(units):
            soften(units[i], i % spots)
        if i == 2 * pairs:
            att_copy = remote(
                att.at[:, far_rows], att_far, att_send.at[0], att_recv.at[0], partner, z
            )
            att_copy.start()

            @pl.when(early)
            def _():
                tokens_sent()
                send_cotangents()


    left = jnp.concatenate([att[p, near_rows, :] for p in range(pairs)], axis=1)
    acc[...] = dot(left, m_out[0:side, :])

    def whole(source, target, send_sem, recv_sem):
        return remote(source, target, send_sem, recv_sem, partner, z)

    att_copy.wait()
    left = jnp.concatenate([att_far[p] for p in range(pairs)], axis=1)
    acc[...] += dot(left, m_out[side:width, :])

    def lines_of(step):
        return pl.ds(pl.multiple_of(step * NORM_ROWS, NORM_ROWS), NORM_ROWS)

    def norm_first(step, carry):
        at = lines_of(step)
        near = pl.ds(pl.multiple_of(half + step * NORM_ROWS, NORM_ROWS), NORM_ROWS)
        hidden = row[near, :].astype(F32) + acc[at, :] + vectors[2]
        norm, inv_std = normed(hidden)
        norm_a[at, :] = norm
        inv_a[at, :] = jnp.broadcast_to(inv_std, (NORM_ROWS, LANES))
        middle = norm * vectors[4] + vectors[5]
        mid[at, :] = middle
        mid_low[at, :] = middle.astype(BF16)
        return carry

    lax.fori_loop(0, norm_steps, norm_first, 0, unroll=True)

    def slope_at(f):
        return f // 2, slice(f % 2 * half, (f % 2 + 1) * half)

    def activate(f):
        columns = slice(f * FF_CHUNK, (f + 1) * FF_CHUNK)
        inner = raw[f % 2] + bias_inner[:, columns]
        cdf = 0.5 * (1.0 + lax.erf(inner * 0.7071067811865476))
        which, lines = slope_at(f)
        slope[which, lines, :] = cdf + inner * jnp.exp(-0.5 * inner * inner) * 0.3989422804014327
        active[:, columns] = (inner * cdf).astype(BF16)

    raw[0] = dot(mid_low[...], m_inner[0])
    for f in range(chunks):
        if f + 1 < chunks:
            raw[(f + 1) % 2] = dot(mid_low[...], m_inner[f + 1])
        activate(f)
    for n in range(0, width, FEATURE_CHUNK):
        acc[:, n : n + FEATURE_CHUNK] = dot(active[...], m_outer[:, n : n + FEATURE_CHUNK])

    def cot_wait(j, carry):
        at = pl.ds(pl.multiple_of(j * span, span), span)
        arrived(cotangent, cot, at, core * half_blocks + j, cot_send, cot_recv, in_sem.at[1])
        return carry

    lax.fori_loop(0, half_blocks, cot_wait, 0)

    live_end = ends[3:4, 0:1]
    zero_sum = jnp.zeros((8, width), F32)

    def norm_last(step, carry):
        beta_sum, outer_sum = carry
        at = lines_of(step)
        hidden = mid[at, :] + acc[at, :] + vectors[3]
        norm, inv_std = normed(hidden)
        place = lax.broadcasted_iota(jnp.int32, (NORM_ROWS, 1), 0) + core * half + step * NORM_ROWS
        live = (place < live_end).astype(F32)
        layer_out[at, :] = (live * (norm * vectors[6] + vectors[7])).astype(BF16)
        grad_final = live * cot[at, :].astype(F32)
        grad_hidden = norm_back(grad_final * vectors[6], norm, inv_std)
        grad_h[at, :] = grad_hidden
        grad_low[at, :] = grad_hidden.astype(BF16)
        return beta_sum + fold_rows(grad_final), outer_sum + fold_rows(grad_hidden)

    def home_block(block, source, target_ref, send_sem, recv_sem, local_sem):
        j = block - core * half_blocks
        src = source.at[pl.ds(pl.multiple_of(j * span, span), span)]
        line_at = z - z_half * rows

        @pl.when(block != z)
        def _():
            remote(
                src,
                target_ref.at[line_at],
                send_sem.at[j],
                recv_sem.at[line_at],
                base + z_half,
                block,
            ).start()

        @pl.when(block == z)
        def _():
            pltpu.make_async_copy(src, target_ref.at[line_at], local_sem).start()

    def home_done(source, target_ref, send_sem, recv_sem, local_sem):
        for j in range(half_blocks):
            block = core * half_blocks + j
            src = source.at[j * span : (j + 1) * span]
            line_at = z - z_half * rows

            @pl.when(block != z)
            def _():
                remote(
                    src,
                    target_ref.at[line_at],
                    send_sem.at[j],
                    recv_sem.at[line_at],
                    base + z_half,
                    block,
                ).wait_send()

            @pl.when(block == z)
            def _():
                pltpu.make_async_copy(src, target_ref.at[line_at], local_sem).wait()

        for r in range(rows):
            target = core * rows + r

            @pl.when(target != z)
            def _():
                remote(
                    source.at[0:span],
                    target_ref.at[r],
                    send_sem.at[0],
                    recv_sem.at[r],
                    base + z_half,
                    target,
                ).wait_recv()

    sums = lax.fori_loop(0, norm_steps, norm_last, (zero_sum, zero_sum), unroll=True)
    for j in range(half_blocks):
        home_block(
            core * half_blocks + j, layer_out, layer_home, lay_send, lay_recv, in_sem.at[2]
        )
    beta_final_sum, outer_sum = sums

    for f in range(chunks):
        which, lines = slope_at(f)
        columns = slice(f * FF_CHUNK, (f + 1) * FF_CHUNK)
        grad_active = dot_nt(grad_low[...], m_outer[columns, :])
        grad_inner = (grad_active * slope[which, lines, :]).astype(BF16)
        active[:, columns] = grad_inner
        inner_sum[f] = fold_rows(grad_inner.astype(F32))
    for n in range(0, width, FEATURE_CHUNK):
        total = None
        for f in range(chunks):
            term = dot_nt(
                active[:, f * FF_CHUNK : (f + 1) * FF_CHUNK], m_inner[f, n : n + FEATURE_CHUNK, :]
            )
            total = term if total is None else total + term
        acc[:, n : n + FEATURE_CHUNK] = total
    def norm_first_back(step, carry):
        beta_sum, out_sum = carry
        at = lines_of(step)
        grad_middle = grad_h[at, :] + acc[at, :]
        grad_hidden = norm_back(grad_middle * vectors[4], norm_a[at, :], inv_a[at, 0:1])
        grad_h[at, :] = grad_hidden
        grad_low[at, :] = grad_hidden.astype(BF16)
        return beta_sum + fold_rows(grad_middle), out_sum + fold_rows(grad_hidden)

    beta_attn_sum, out_sum = lax.fori_loop(
        0, norm_steps, norm_first_back, (zero_sum, zero_sum), unroll=True
    )

    def sum_up():
        per_line = width // FF_CHUNK
        for f in range(chunks):
            line_at = 4 + f // per_line
            column = f % per_line * FF_CHUNK
            vec_a[line_at : line_at + 1, column : column + FF_CHUNK] = jnp.sum(
                inner_sum[f], axis=0, keepdims=True
            )
        for i, lines in enumerate((out_sum, outer_sum, beta_attn_sum, beta_final_sum)):
            vec_a[i : i + 1, :] = jnp.sum(lines, axis=0, keepdims=True)
        pool_a[seq] = vec_a[:, pl.ds(pl.multiple_of(own_slice * slice_width, LANES), slice_width)]

    def send_all(start, size, here, make):
        def go(step, carry):
            make(start + lax.rem(here - start + step, size)).start()
            return carry

        lax.fori_loop(1, size, go, 0)

    def wait_all(pool, size, make):
        everything = pool.at[pl.ds(0, size - 1)]
        copy = make(everything, everything)
        copy.wait()

    def bias_copy(i, peer_seq, peer_z):
        return lambda source, target: remote(
            source, target, bias_send.at[i], bias_recv.at[i], peer_seq, peer_z
        )

    def plane_a(peer):
        piece = pl.ds(pl.multiple_of(lax.rem(peer, slices) * slice_width, LANES), slice_width)
        return bias_copy(0, peer, z)(vec_a.at[:, piece], pool_a.at[seq])

    def column_a(peer):
        return bias_copy(1, seq, peer)(z_a.at[z], z_a.at[z])

    own_slice = lax.rem(seq, slices)

    def gather_a(peer):
        return bias_copy(2, peer, z)(sums_a.at[own_slice], sums_a.at[own_slice])

    def column_b(peer):
        return bias_copy(3, seq, peer)(z_b.at[z], z_b.at[z])

    def plane_b(peer):
        return bias_copy(4, peer, z)(pool_b.at[seq], pool_b.at[seq])

    def total_of(pool, places):
        total = pool[places[0]]
        for place in places[1:]:
            total = total + pool[place]
        return total

    def gat_copy(p):
        return remote(
            grad_far.at[p], grad_att.at[p, far_rows], gat_send.at[0], gat_recv.at[0], partner, z
        )

    lines = dot_nt(grad_low[...], m_out[side:width, :])
    for p in range(pairs):
        grad_far[p] = lines[:, p * LANES : (p + 1) * LANES].astype(BF16)
        gat_copy(p).start()
    lines = dot_nt(grad_low[...], m_out[0:side, :])
    for p in range(pairs):
        grad_att[p, near_rows, :] = lines[:, p * LANES : (p + 1) * LANES].astype(BF16)
        turned[p] = qs[p].T

    def prepare(p, at):
        scaled = (grad_att[p, at, :].astype(F32) * recip[p, at, :]).astype(BF16)
        product = scaled.astype(F32) * mixed[p, at, :]
        half_lane = lane[at, :]
        for i in range(2):
            delta = jnp.sum(product * head_mask[i], axis=-1, keepdims=True)
            high = delta.astype(BF16).astype(F32)
            extra = jnp.where(half_lane == 0, -high, jnp.where(half_lane == 1, high - delta, 0.0))
            grads = scaled * low_mask[i]
            lefts[2 * p + i, at, :] = jnp.concatenate([grads, extra.astype(BF16)], axis=1)
            cut = slice(i * head_width, (i + 1) * head_width)
            grads_turned[p, cut, at] = grads.T[cut]

    def score_grads(p):
        values = jnp.concatenate([vs[p], ones], axis=1)
        for i in range(2):
            head = 2 * p + i
            grad_probs = dot_nt(lefts[head], values)
            grad_scores[head % 4] = (exps[head].astype(F32) * grad_probs).astype(BF16)

    def attend_back(p):
        dq = None
        dk = []
        dv = []
        for i in range(2):
            cut = slice(i * head_width, (i + 1) * head_width)
            head = 2 * p + i
            term = dot(grad_scores[head % 4], ks[p] * low_mask[i])
            dq = term if dq is None else dq + term
            dk.append(dot(turned[p, cut, :], grad_scores[head % 4]))
            dv.append(dot(grads_turned[p, cut, :], exps[head]))
        dq = (dq * score_scale).astype(BF16)
        dk = jnp.concatenate(dk, axis=0).astype(BF16).T
        dv = jnp.concatenate(dv, axis=0).astype(BF16).T
        for i, block in enumerate((dq, dk, dv)):
            grad_qkv[:, i * side + p * LANES : i * side + (p + 1) * LANES] = block
        z_b[z, p : p + 1, :] = jnp.sum(fold_rows(dq.astype(F32)), axis=0, keepdims=True)
        z_b[z, pairs + p : pairs + p + 1, :] = jnp.sum(
            fold_rows(dv.astype(F32)), axis=0, keepdims=True
        )

    sum_up()
    send_all(0, seq_size, seq, plane_a)
    for p in range(pairs):
        prepare(p, near_rows)
    whole(grad_far, grad_far, gat_send.at[0], gat_recv.at[0]).wait()
    for p in range(pairs):
        prepare(p, far_rows)
    score_grads(0)
    for p in range(pairs):
        if p + 1 < pairs:
            score_grads(p + 1)
        attend_back(p)
    send_all(0, group, z, column_b)
    wait_all(pool_a, seq_size, bias_copy(0, partner, z))
    z_a[z] = total_of(pool_a, range(seq_size))
    send_all(0, group, z, column_a)

    def part_copy(c, j):
        at = far_at(j)
        return remote(
            part_out.at[c, at], part_in.at[c, at], part_send.at[c, j], part_recv.at[c, j], partner, z
        )

    def token_grad(first, c):
        mine_now = core == (1 - z_half if first else z_half)
        at = pl.ds(pl.multiple_of(jnp.where(mine_now, half, 0), half), half)
        columns = slice(c * GRAD_COLUMNS, (c + 1) * GRAD_COLUMNS)
        term = dot_nt(grad_qkv[at, :], m_qkv[columns, :])

        @pl.when(mine_now)
        def _():
            part[c] = term

        @pl.when(jnp.logical_not(mine_now))
        def _():
            for j in range(half_blocks):
                at = slice(j * span, (j + 1) * span)
                part_out[c, at, :] = term[at].astype(BF16)
                part_copy(c, j).start()

    home_line = z - z_half * rows

    def finish(first, c):
        columns = slice(c * GRAD_COLUMNS, (c + 1) * GRAD_COLUMNS)

        @pl.when(core == (1 - z_half if first else z_half))
        def _():
            for j in range(half_blocks):
                block = core * half_blocks + j
                at = slice(j * span, (j + 1) * span)
                part_copy(c, j).wait_recv()
                total = grad_h[at, columns] + part[c, at, :] + part_in[c, at, :].astype(F32)
                grad_out[c, at, :] = total.astype(BF16)
                source = grad_out.at[c, at]

                @pl.when(block != z)
                def _():
                    remote(
                        source,
                        grad_home.at[home_line, c],
                        grad_send.at[j],
                        grad_recv.at[home_line],
                        base + z_half,
                        block,
                    ).start()

                @pl.when(block == z)
                def _():
                    pltpu.make_async_copy(source, grad_home.at[home_line, c], in_sem.at[3]).start()

    def grads_done():
        for j in range(half_blocks):
            block = core * half_blocks + j
            everything = grad_home.at[home_line]

            @pl.when(block != z)
            def _():
                whole(everything, everything, grad_send.at[j], grad_recv.at[home_line]).wait_send()

            @pl.when(block == z)
            def _():
                pltpu.make_async_copy(everything, everything, in_sem.at[3]).wait()

        for r in range(rows):

            @pl.when(core * rows + r != z)
            def _():
                everything = grad_home.at[r]
                whole(everything, everything, grad_send.at[0], grad_recv.at[r]).wait_recv()

    pieces = part.shape[0]
    for first in (True, False):
        for c in range(pieces):
            token_grad(first, c)
            if c >= GRAD_LAG:
                finish(first, c - GRAD_LAG)
        for c in range(pieces - GRAD_LAG, pieces):
            finish(first, c)
    wait_all(z_a, group, bias_copy(1, partner, z))
    sums_a[own_slice] = total_of(z_a, range(group))
    send_all(seq - own_slice, slices, seq, gather_a)
    wait_all(z_b, group, bias_copy(3, partner, z))
    pool_b[seq] = total_of(z_b, range(group))
    send_all(0, seq_size, seq, plane_b)

    for c in range(pieces):
        for j in range(half_blocks):
            part_copy(c, j).wait_send()
    wait_all(sums_a, slices, bias_copy(2, partner, z))
    wait_all(pool_b, seq_size, bias_copy(4, partner, z))
    for i in range(2):
        sums_b[i] = total_of(pool_b, range(i, seq_size, 2))

    @pl.when(jnp.logical_not(early))
    def _():
        tokens_sent()

    cotangents_sent()

    def pass_wait(j, carry):
        pass_on(j).wait_send()
        return carry

    lax.fori_loop(0, half_blocks, pass_wait, 0)
    home_done(layer_out, layer_home, lay_send, lay_recv, in_sem.at[2])
    grads_done()


def finish_kernel(
    layer,
    grad,
    sums_a,
    sums_b,
    layer_out,
    input_grad,
    grad_bias_query,
    grad_bias_value,
    grad_bias_out,
    grad_bias_inner,
    grad_bias_outer,
    grad_beta_attn,
    grad_beta_final,
    wide,
    lines,
    inner_line,
    sems,
):
    rows, span, width = layer.shape
    slices, _, slice_width = sums_a.shape
    copies = [pltpu.make_async_copy(layer, layer_out, sems.at[0])]
    copies[0].start()
    for r in range(rows):
        for c in range(grad.shape[1]):
            wide[r, :, c * GRAD_COLUMNS : (c + 1) * GRAD_COLUMNS] = grad[r, c].astype(F32)
        copies.append(pltpu.make_async_copy(wide.at[r], input_grad.at[r], sems.at[1 + r]))
        copies[-1].start()
    pairs = sums_b.shape[1] // 2
    for i in range(2):
        for p in range(pairs):
            column = (i * pairs + p) * LANES
            lines[0, :, column : column + LANES] = sums_b[i, p : p + 1, :]
            lines[1, :, column : column + LANES] = sums_b[i, pairs + p : pairs + p + 1, :]
    for j in range(slices):
        column = j * slice_width
        for i in range(4):
            lines[2 + i, :, column : column + slice_width] = sums_a[j, i : i + 1, :]
            inner_line[:, i * width + column : i * width + column + slice_width] = sums_a[
                j, 4 + i : 5 + i, :
            ]
    targets = (
        grad_bias_query,
        grad_bias_value,
        grad_bias_out,
        grad_bias_outer,
        grad_beta_attn,
        grad_beta_final,
    )
    for i, target in enumerate(targets):
        copies.append(pltpu.make_async_copy(lines.at[i], target, sems.at[1 + rows + i]))
        copies[-1].start()
    copies.append(pltpu.make_async_copy(inner_line, grad_bias_inner, sems.at[7 + rows]))
    copies[-1].start()
    for copy in copies:
        copy.wait()


def per_device(
    seq_size,
    group,
    tokens,
    doc_lengths,
    pad_counts,
    w_query,
    w_key,
    w_value,
    w_out,
    w_inner,
    w_outer,
    bias_query,
    bias_value,
    bias_out,
    bias_inner,
    bias_outer,
    gain_attn,
    beta_attn,
    gain_final,
    beta_final,
    cotangent,
):
    rows, span, width = tokens.shape
    hidden = w_inner.shape[1]
    slots = span * group
    half = slots // 2
    half_blocks = group // 2
    side = width // 2
    pairs = side // LANES
    chunks = hidden // FF_CHUNK
    slices = min(8, seq_size)
    pieces = width // GRAD_COLUMNS
    slice_width = width // slices
    if rows * 2 != group or pairs != 4 or hidden != 4 * width or slots != FF_CHUNK:
        raise ValueError("unsupported sizes")

    any_space = pl.BlockSpec(memory_space=pl.ANY)
    vmem = pl.BlockSpec(memory_space=pltpu.VMEM)
    smem = pl.BlockSpec(memory_space=pltpu.SMEM)
    dma = pltpu.SemaphoreType.DMA
    scratch = [
        pltpu.VMEM((width, 3 * side), BF16),
        pltpu.VMEM((width, width), BF16),
        pltpu.VMEM((chunks, width, FF_CHUNK), BF16),
        pltpu.VMEM((hidden, width), BF16),
        pltpu.VMEM((8, 1, width), F32),
        pltpu.VMEM((1, hidden), F32),
        pltpu.VMEM((slots, width), BF16),
        pltpu.VMEM((half, width), BF16),
        pltpu.VMEM((2, rows, 8, LANES), jnp.int32),
        pltpu.VMEM((pairs, slots, LANES), BF16),
        pltpu.VMEM((pairs, slots, LANES), BF16),
        pltpu.VMEM((pairs, slots, LANES), BF16),
        pltpu.VMEM((2 * pairs, slots, slots), BF16),
        pltpu.VMEM((pairs, slots, LANES), F32),
        pltpu.VMEM((pairs, slots, LANES), F32),
        pltpu.VMEM((pairs, slots, LANES), BF16),
        pltpu.VMEM((pairs, half, LANES), BF16),
        pltpu.VMEM((half, width), F32),
        pltpu.VMEM((half, LANES), F32),
        pltpu.VMEM((half, width), F32),
        pltpu.VMEM((half, width), BF16),
        pltpu.VMEM((half, width), F32),
        pltpu.VMEM((chunks // 2, slots, slots), F32),
        pltpu.VMEM((2, half, FF_CHUNK), F32),
        pltpu.VMEM((half, hidden), BF16),
        pltpu.VMEM((chunks, 8, FF_CHUNK), F32),
        pltpu.VMEM((half, width), F32),
        pltpu.VMEM((half, width), BF16),
        pltpu.VMEM((pairs, slots, LANES), BF16),
        pltpu.VMEM((pairs, half, LANES), BF16),
        pltpu.VMEM((slots, 3 * side), BF16),
        pltpu.VMEM((pairs, LANES, slots), BF16),
        pltpu.VMEM((2 * pairs, slots, 2 * LANES), BF16),
        pltpu.VMEM((pairs, LANES, slots), BF16),
        pltpu.VMEM((4, slots, slots), BF16),
        pltpu.VMEM((pieces, half, GRAD_COLUMNS), F32),
        pltpu.VMEM((pieces, half, GRAD_COLUMNS), BF16),
        pltpu.VMEM((pieces, half, GRAD_COLUMNS), BF16),
        pltpu.VMEM((pieces, half, GRAD_COLUMNS), BF16),
        pltpu.VMEM((half, width), BF16),
        pltpu.VMEM((8, width), F32),
        pltpu.VMEM((seq_size, 8, slice_width), F32),
        pltpu.VMEM((group, 8, slice_width), F32),
        pltpu.VMEM((seq_size, 8, LANES), F32),
        pltpu.VMEM((group, 8, LANES), F32),
        dma((6,)),
        dma((4,)),
        dma((rows,)),
        dma((half_blocks,)),
        dma((half_blocks,)),
        dma((half_blocks,)),
        dma((2,)),
        dma((rows,)),
        dma((half_blocks,)),
        dma((1,)),
        dma((1,)),
        dma((1,)),
        dma((1,)),
        dma((half_blocks,)),
        dma((rows,)),
        dma((pieces, half_blocks)),
        dma((pieces, half_blocks)),
        dma((half_blocks,)),
        dma((rows,)),
        dma((5,)),
        dma((5,)),
    ]
    vectors = (
        bias_query,
        bias_value,
        bias_out,
        bias_inner,
        bias_outer,
        gain_attn,
        beta_attn,
        gain_final,
        beta_final,
    )
    layer_home, grad_home, sums_a, sums_b = pl.pallas_call(
        functools.partial(kernel, seq_size, group),
        out_shape=(
            pltpu.VMEM(tokens.shape, BF16),
            pltpu.VMEM((rows, pieces, span, GRAD_COLUMNS), BF16),
            pltpu.VMEM((slices, 8, slice_width), F32),
            pltpu.VMEM((2, 8, LANES), F32),
        ),
        in_specs=[any_space] * 2 + [smem] * 2 + [any_space] * (6 + len(vectors)),
        out_specs=(vmem,) * 4,
        scratch_shapes=scratch,
        compiler_params=pltpu.CompilerParams(
            collective_id=0, has_side_effects=True, vmem_limit_bytes=58 * 2**20
        ),
    )(
        tokens,
        cotangent,
        doc_lengths,
        pad_counts,
        w_query,
        w_key,
        w_value,
        w_out,
        w_inner,
        w_outer,
        *[vector.reshape(1, -1) for vector in vectors],
    )
    line = jax.ShapeDtypeStruct((1, width), F32)
    results = pl.pallas_call(
        finish_kernel,
        out_shape=(
            jax.ShapeDtypeStruct(tokens.shape, BF16),
            jax.ShapeDtypeStruct(tokens.shape, F32),
            line,
            line,
            line,
            jax.ShapeDtypeStruct((1, hidden), F32),
            line,
            line,
            line,
        ),
        in_specs=[vmem] * 4,
        out_specs=(any_space,) * 9,
        scratch_shapes=[
            pltpu.VMEM(tokens.shape, F32),
            pltpu.VMEM((6, 1, width), F32),
            pltpu.VMEM((1, hidden), F32),
            dma((8 + rows,)),
        ],
        compiler_params=pltpu.CompilerParams(vmem_limit_bytes=32 * 2**20),
    )(layer_home, grad_home, sums_a, sums_b)
    return tuple(results[:2]) + tuple(vector.reshape(-1) for vector in results[2:])


def solution(mesh):
    split = P("seq", "head", None)
    placed = (split, P("seq", None), P("seq")) + (P(),) * 15 + (split,)
    return jax.shard_map(
        functools.partial(per_device, mesh.shape["seq"], mesh.shape["head"]),
        mesh=mesh,
        in_specs=placed,
        out_specs=(split, split) + (P(),) * 7,
        check_vma=False,
    )
```

```python
import functools

import jax
import jax.numpy as jnp
from jax import lax
from jax.experimental import pallas as pl
from jax.experimental.pallas import tpu as pltpu
from jax.sharding import PartitionSpec as P

HEADS = 16
LANES = 128
EPS = 1e-06
BIG = 2.0**30
FF_CHUNK = 512
FEATURE_CHUNK = 512
NORM_ROWS = 32
MESH = pl.DeviceIdType.MESH
F32 = jnp.float32
BF16 = jnp.bfloat16


def dot(left, right):
    return lax.dot_general(left, right, (((1,), (0,)), ((), ())), preferred_element_type=F32)


def dot_nt(left, right):
    return lax.dot_general(left, right, (((1,), (1,)), ((), ())), preferred_element_type=F32)


def dot_tn(left, right):
    return lax.dot_general(left, right, (((0,), (0,)), ((), ())), preferred_element_type=F32)


def normed(hidden):
    row_mean = jnp.mean(hidden, axis=-1, keepdims=True)
    centred = hidden - row_mean
    inv_std = lax.rsqrt(jnp.mean(centred * centred, axis=-1, keepdims=True) + EPS)
    return centred * inv_std, inv_std


def norm_back(gradient, norm, inv_std):
    return inv_std * (
        gradient
        - jnp.mean(gradient, axis=-1, keepdims=True)
        - norm * jnp.mean(gradient * norm, axis=-1, keepdims=True)
    )


def fold_rows(block):
    total = block[0:8]
    for start in range(8, block.shape[0], 8):
        total = total + block[start : start + 8]
    return total


def kernel(
    seq_size,
    group,
    tokens,
    cotangent,
    doc_lengths,
    pad_counts,
    w_query,
    w_key,
    w_value,
    w_out,
    w_inner,
    w_outer,
    in_bias_query,
    in_bias_value,
    in_bias_out,
    in_bias_inner,
    in_bias_outer,
    in_gain_attn,
    in_beta_attn,
    in_gain_final,
    in_beta_final,
    layer_home,
    grad_home,
    sums_a,
    sums_b,
    m_qkv,
    m_out,
    m_inner,
    m_outer,
    vectors,
    bias_inner,
    row,
    cot,
    info,
    qs,
    ks,
    vs,
    exps,
    recip,
    mixed,
    att,
    att_far,
    norm_a,
    inv_a,
    inv_f,
    mid,
    mid_low,
    acc,
    slope,
    raw_even,
    raw_odd,
    active,
    inner_sum,
    grad_h,
    grad_low,
    grad_att,
    grad_far,
    grad_qkv,
    turned,
    lefts,
    grads_turned,
    grad_scores,
    part,
    part_out,
    part_in,
    grad_out,
    layer_out,
    vec_a,
    pool_a,
    z_a,
    pool_b,
    z_b,
    w_sem,
    in_sem,
    tok_send,
    tok_recv,
    pass_send,
    pass_recv,
    info_sem,
    cot_send,
    cot_recv,
    att_send,
    att_recv,
    gat_send,
    gat_recv,
    lay_send,
    lay_recv,
    part_send,
    part_recv,
    grad_send,
    grad_recv,
    bias_send,
    bias_recv,
):
    rows, span, width = tokens.shape
    half_blocks = group // 2
    slots = span * group
    half = slots // 2
    head_width = width // HEADS
    side = width // 2
    pairs = side // LANES
    chunks = m_inner.shape[0]
    norm_steps = half // NORM_ROWS
    score_scale = head_width**-0.5
    slices = sums_a.shape[0]
    slice_width = width // slices

    seq = lax.axis_index("seq")
    z = lax.axis_index("head")
    core = lax.rem(seq, 2)
    base = seq - core
    partner = base + 1 - core
    z_half = z // half_blocks
    far = 1 - core

    def near_at(j):
        return pl.ds(pl.multiple_of(half + j * span, span), span)

    def far_at(j):
        return pl.ds(pl.multiple_of(j * span, span), span)

    def remote(src, dst, send_sem, recv_sem, at_seq, at_head):
        return pltpu.make_async_remote_copy(
            src_ref=src,
            dst_ref=dst,
            send_sem=send_sem,
            recv_sem=recv_sem,
            device_id=(at_seq, at_head),
            device_id_type=MESH,
        )

    barrier = pltpu.get_barrier_semaphore()

    def greet_z(step, carry):
        pl.semaphore_signal(
            barrier, inc=1, device_id=(seq, lax.rem(z + step, group)), device_id_type=MESH
        )
        return carry

    def greet_seq(step, carry):
        pl.semaphore_signal(
            barrier, inc=1, device_id=(lax.rem(seq + step, seq_size), z), device_id_type=MESH
        )
        return carry

    for r in range(half_blocks):
        other = core * half_blocks + r

        @pl.when(other != z)
        def _():
            pl.semaphore_signal(barrier, inc=1, device_id=(partner, other), device_id_type=MESH)

    lax.fori_loop(1, seq_size, greet_seq, 0)
    lax.fori_loop(1, group, greet_z, 0)

    mine = pl.ds(pl.multiple_of(core * side, side), side)
    theirs = pl.ds(pl.multiple_of(far * side, side), side)
    for i, weight in enumerate((w_query, w_key, w_value)):
        pltpu.make_async_copy(
            weight.at[:, mine], m_qkv.at[:, i * side : (i + 1) * side], w_sem.at[0]
        ).start()
    for i, vector in enumerate(
        (
            in_bias_query,
            in_bias_value,
            in_bias_out,
            in_bias_outer,
            in_gain_attn,
            in_beta_attn,
            in_gain_final,
            in_beta_final,
        )
    ):
        pltpu.make_async_copy(vector, vectors.at[i], w_sem.at[4]).start()
    pltpu.make_async_copy(in_bias_inner, bias_inner, w_sem.at[5]).start()

    def loaded(target, i):
        pltpu.make_async_copy(target, target, w_sem.at[i]).wait()

    line = lax.broadcasted_iota(jnp.int32, (8, LANES), 0)
    for r in range(rows):
        first = doc_lengths[r, 0]
        second = first + doc_lengths[r, 1]
        third = second + doc_lengths[r, 2]
        ends = jnp.where(line == 0, first, jnp.where(line == 1, second, third))
        info[core, r] = jnp.where(line == 3, slots - pad_counts[r], ends)

    crossed = jnp.where(z_half == core, 0, group - 1)
    pl.semaphore_wait(barrier, crossed + seq_size - 1 + group - 1)

    early = (z >= half_blocks // 2) & (z < group - half_blocks // 2)

    def spread(index, source, target_ref, at, send_sem, recv_sem):
        r = jnp.where(core == 0, rows - 1 - index, index)
        target = core * rows + r

        @pl.when(target != z)
        def _():
            remote(
                source.at[r],
                target_ref.at[at],
                send_sem.at[r],
                recv_sem.at[z - z_half * half_blocks],
                base + z_half,
                target,
            ).start()

    def keep(source, target_ref, at, local_sem):
        @pl.when(core == z_half)
        def _():
            pltpu.make_async_copy(
                source.at[z - z_half * rows], target_ref.at[at], local_sem
            ).start()

    def spread_done(index, source, target_ref, at, send_sem, recv_sem):
        r = jnp.where(core == 0, rows - 1 - index, index)
        target = core * rows + r

        @pl.when(target != z)
        def _():
            remote(
                source.at[r],
                target_ref.at[at],
                send_sem.at[r],
                recv_sem.at[z - z_half * half_blocks],
                base + z_half,
                target,
            ).wait_send()

    def arrived(source, target_ref, at, block, send_sem, recv_sem, local_sem):
        j = block - core * half_blocks

        @pl.when(block != z)
        def _():
            remote(
                source.at[0],
                target_ref.at[at],
                send_sem.at[0],
                recv_sem.at[j],
                base + z_half,
                block,
            ).wait_recv()

        @pl.when(block == z)
        def _():
            pltpu.make_async_copy(source.at[0], target_ref.at[at], local_sem).wait()

    info_copy = remote(info.at[core], info.at[core], info_sem.at[0], info_sem.at[1], partner, z)
    info_copy.start()
    tok_at = near_at(z - z_half * half_blocks)
    cot_at = pl.ds(pl.multiple_of((z - z_half * half_blocks) * span, span), span)

    def send_tokens():
        for index in range(rows):
            spread(index, tokens, row, tok_at, tok_send, tok_recv)

    def tokens_sent():
        for index in range(rows):
            spread_done(index, tokens, row, tok_at, tok_send, tok_recv)

    def send_cotangents():
        for index in range(rows):
            spread(index, cotangent, cot, cot_at, cot_send, cot_recv)

    def cotangents_sent():
        for index in range(rows):
            spread_done(index, cotangent, cot, cot_at, cot_send, cot_recv)

    send_tokens()
    keep(tokens, row, tok_at, in_sem.at[0])
    keep(cotangent, cot, cot_at, in_sem.at[1])
    pltpu.make_async_copy(w_out.at[mine], m_out.at[0:side], w_sem.at[1]).start()
    pltpu.make_async_copy(w_out.at[theirs], m_out.at[side:width], w_sem.at[1]).start()
    for f in range(chunks):
        columns = slice(f * FF_CHUNK, (f + 1) * FF_CHUNK)
        pltpu.make_async_copy(w_inner.at[:, columns], m_inner.at[f], w_sem.at[2]).start()
    pltpu.make_async_copy(w_outer, m_outer, w_sem.at[3]).start()

    info_copy.wait_send()
    remote(info.at[far], info.at[far], info_sem.at[0], info_sem.at[1], partner, z).wait_recv()
    loaded(m_qkv, 0)
    loaded(vectors, 4)
    loaded(bias_inner, 5)
    bias_query = vectors[0, :, mine]
    bias_value = vectors[1, :, mine]

    lane = lax.broadcasted_iota(jnp.int32, (slots, LANES), 1)
    place = lax.broadcasted_iota(jnp.int32, (slots, LANES), 0)
    slot = jnp.where(place < half, far * half + place, core * half + place - half)
    ends = info[z_half, z - z_half * rows]
    doc = (slot >= ends[0:1]).astype(jnp.int32)
    for i in range(1, 4):
        doc = doc + (slot >= ends[i : i + 1]).astype(jnp.int32)
    doc_query = jnp.where(doc == lane, BIG, 0.0).astype(BF16)
    doc_key = jnp.where((doc != lane) & (lane < 5), -1.0, 0.0).astype(BF16)
    ones = jnp.ones((slots, LANES), BF16)

    def pass_on(j):
        return remote(
            row.at[near_at(j)], row.at[far_at(j)], pass_send.at[j], pass_recv.at[j], partner, z
        )

    def taken(which, step):
        local = lax.rem(z - z_half * half_blocks + step, half_blocks)
        beyond = jnp.where(z_half == 0, half_blocks - 1 - step, step)
        return jnp.where(which == z_half, local, beyond)

    def project(at):
        x = row[at, :]
        q = (dot(x, m_qkv[:, 0:side]) + bias_query) * score_scale
        k = dot(x, m_qkv[:, side : 2 * side])
        v = dot(x, m_qkv[:, 2 * side : 3 * side]) + bias_value
        for p in range(pairs):
            cut = slice(p * LANES, (p + 1) * LANES)
            qs[p, at, :] = q[:, cut].astype(BF16)
            ks[p, at, :] = k[:, cut].astype(BF16)
            vs[p, at, :] = v[:, cut].astype(BF16)


    def project_step(i, carry):
        in_turn = core == z_half
        own = jnp.where(in_turn, i < half_blocks, lax.rem(i, 2) == 1)
        step = jnp.where(in_turn, lax.rem(i, half_blocks), i // 2)
        j = taken(jnp.where(own, core, far), step)

        @pl.when(own)
        def _():
            block = core * half_blocks + j
            arrived(tokens, row, near_at(j), block, tok_send, tok_recv, in_sem.at[0])
            pass_on(j).start()

            @pl.when((i == group - 1) & jnp.logical_not(early))
            def _():
                send_cotangents()

        @pl.when(jnp.logical_not(own))
        def _():
            pass_on(j).wait_recv()

            @pl.when(in_turn & (i == half_blocks) & jnp.logical_not(early))
            def _():
                send_cotangents()

        project(pl.ds(pl.multiple_of(jnp.where(own, half, 0) + j * span, span), span))
        return carry

    lax.fori_loop(0, group, project_step, 0)

    for i, target in enumerate((m_out, m_inner, m_outer)):
        loaded(target, 1 + i)

    lane_row = lax.broadcasted_iota(jnp.int32, (1, LANES), 1)
    head_mask = [
        (lane_row < head_width).astype(F32),
        (lane_row >= head_width).astype(F32),
    ]
    low_mask = [mask.astype(BF16) for mask in head_mask]
    near_rows = slice(half, slots)
    far_rows = slice(0, half)

    def score(unit, spot):
        head, at = unit
        p = head // 2
        left = jnp.concatenate([qs[p, at, :] * low_mask[head % 2], doc_query[at, :]], axis=1)
        keys = jnp.concatenate([ks[p], doc_key], axis=1)
        slope[spot, 0:half, :] = dot_nt(left, keys)

    def soften(unit, spot):
        head, at = unit
        scores = slope[spot, 0:half, :]
        exponent = jnp.exp(scores - jnp.max(scores, axis=-1, keepdims=True))
        exps[head, at, :] = exponent.astype(BF16)

    def mix(unit):
        head, at = unit
        both = dot(exps[head, at, :], jnp.concatenate([vs[head // 2], ones], axis=1))
        share = 1.0 / both[:, LANES:]
        return both[:, :LANES] * share * head_mask[head % 2], share * head_mask[head % 2]

    units = [(head, at) for at in (far_rows, near_rows) for head in range(2 * pairs)]
    spots = slope.shape[0]
    score(units[0], 0)
    for i in range(len(units) + 1):
        if i + 1 < len(units):
            score(units[i + 1], (i + 1) % spots)
        if i > 0:
            head, at = units[i - 1]
            if head % 2 == 0:
                held = mix(units[i - 1])
            else:
                total, shares = (a + b for a, b in zip(held, mix(units[i - 1])))
                p = head // 2
                mixed[p, at, :] = total
                recip[p, at, :] = shares
                att[p, at, :] = total.astype(BF16)
        if i < len(units):
            soften(units[i], i % spots)
        if i == 2 * pairs:
            att_copy = remote(
                att.at[:, far_rows], att_far, att_send.at[0], att_recv.at[0], partner, z
            )
            att_copy.start()

            @pl.when(early)
            def _():
                tokens_sent()
                send_cotangents()


    def whole(source, target, send_sem, recv_sem):
        return remote(source, target, send_sem, recv_sem, partner, z)

    att_copy.wait()
    left = jnp.concatenate(
        [att[p, near_rows, :] for p in range(pairs)] + [att_far[p] for p in range(pairs)], axis=1
    )
    acc[...] = dot(left, m_out[...])
    def lines_of(step):
        return pl.ds(pl.multiple_of(step * NORM_ROWS, NORM_ROWS), NORM_ROWS)

    def norm_first(step, carry):
        at = lines_of(step)
        near = pl.ds(pl.multiple_of(half + step * NORM_ROWS, NORM_ROWS), NORM_ROWS)
        hidden = row[near, :].astype(F32) + acc[at, :] + vectors[2]
        norm, inv_std = normed(hidden)
        norm_a[at, :] = norm
        inv_a[at, :] = jnp.broadcast_to(inv_std, (NORM_ROWS, LANES))
        middle = norm * vectors[4] + vectors[5]
        mid[at, :] = middle
        mid_low[at, :] = middle.astype(BF16)
        return carry

    lax.fori_loop(0, norm_steps, norm_first, 0, unroll=True)

    def slope_at(f):
        return f // 2, slice(f % 2 * half, (f % 2 + 1) * half)

    def activate(f):
        columns = slice(f * FF_CHUNK, (f + 1) * FF_CHUNK)
        inner = raw[f % 2][...] + bias_inner[:, columns]
        cdf = 0.5 * (1.0 + lax.erf(inner * 0.7071067811865476))
        which, lines = slope_at(f)
        slope[which, lines, :] = cdf + inner * jnp.exp(-0.5 * inner * inner) * 0.3989422804014327
        active[:, columns] = (inner * cdf).astype(BF16)

    raw = (raw_even, raw_odd)
    raw_even[...] = dot(mid_low[...], m_inner[0])
    for f in range(chunks):
        if f + 1 < chunks:
            raw[(f + 1) % 2][...] = dot(mid_low[...], m_inner[f + 1])
        activate(f)
    for n in range(0, width, FEATURE_CHUNK):
        acc[:, n : n + FEATURE_CHUNK] = dot(active[...], m_outer[:, n : n + FEATURE_CHUNK])

    live_end = ends[3:4, 0:1]

    def live_at(step):
        place = lax.broadcasted_iota(jnp.int32, (NORM_ROWS, 1), 0) + core * half + step * NORM_ROWS
        return (place < live_end).astype(F32)

    def norm_last(step, carry):
        at = lines_of(step)
        norm, inv_std = normed(mid[at, :] + acc[at, :] + vectors[3])
        acc[at, :] = norm
        inv_f[at, :] = jnp.broadcast_to(inv_std, (NORM_ROWS, LANES))
        layer_out[at, :] = (live_at(step) * (norm * vectors[6] + vectors[7])).astype(BF16)
        return carry

    lax.fori_loop(0, norm_steps, norm_last, 0, unroll=True)

    def home_block(block, source, target_ref, send_sem, recv_sem, local_sem):
        j = block - core * half_blocks
        src = source.at[pl.ds(pl.multiple_of(j * span, span), span)]
        line_at = z - z_half * rows

        @pl.when(block != z)
        def _():
            remote(
                src,
                target_ref.at[line_at],
                send_sem.at[j],
                recv_sem.at[line_at],
                base + z_half,
                block,
            ).start()

        @pl.when(block == z)
        def _():
            pltpu.make_async_copy(src, target_ref.at[line_at], local_sem).start()

    def home_done(source, target_ref, send_sem, recv_sem, local_sem):
        for j in range(half_blocks):
            block = core * half_blocks + j
            src = source.at[j * span : (j + 1) * span]
            line_at = z - z_half * rows

            @pl.when(block != z)
            def _():
                remote(
                    src,
                    target_ref.at[line_at],
                    send_sem.at[j],
                    recv_sem.at[line_at],
                    base + z_half,
                    block,
                ).wait_send()

            @pl.when(block == z)
            def _():
                pltpu.make_async_copy(src, target_ref.at[line_at], local_sem).wait()

        for r in range(rows):
            target = core * rows + r

            @pl.when(target != z)
            def _():
                remote(
                    source.at[0:span],
                    target_ref.at[r],
                    send_sem.at[0],
                    recv_sem.at[r],
                    base + z_half,
                    target,
                ).wait_recv()

    for j in range(half_blocks):
        home_block(
            core * half_blocks + j, layer_out, layer_home, lay_send, lay_recv, in_sem.at[2]
        )
    for p in range(pairs):
        turned[p] = qs[p].T

    def cot_wait(j, carry):
        at = pl.ds(pl.multiple_of(j * span, span), span)
        arrived(cotangent, cot, at, core * half_blocks + j, cot_send, cot_recv, in_sem.at[1])
        return carry

    lax.fori_loop(0, half_blocks, cot_wait, 0)

    zero_sum = jnp.zeros((8, width), F32)

    def norm_last_back(step, carry):
        beta_sum, outer_sum = carry
        at = lines_of(step)
        grad_final = live_at(step) * cot[at, :].astype(F32)
        grad_hidden = norm_back(grad_final * vectors[6], acc[at, :], inv_f[at, 0:1])
        grad_h[at, :] = grad_hidden
        grad_low[at, :] = grad_hidden.astype(BF16)
        return beta_sum + fold_rows(grad_final), outer_sum + fold_rows(grad_hidden)

    sums = lax.fori_loop(0, norm_steps, norm_last_back, (zero_sum, zero_sum), unroll=True)
    beta_final_sum, outer_sum = sums

    for f in range(chunks):
        which, lines = slope_at(f)
        columns = slice(f * FF_CHUNK, (f + 1) * FF_CHUNK)
        grad_active = dot_nt(grad_low[...], m_outer[columns, :])
        grad_inner = (grad_active * slope[which, lines, :]).astype(BF16)
        active[:, columns] = grad_inner
        inner_sum[f] = fold_rows(grad_inner.astype(F32))
    for n in range(0, width, FEATURE_CHUNK):
        total = None
        for f in range(chunks):
            term = dot_nt(
                active[:, f * FF_CHUNK : (f + 1) * FF_CHUNK], m_inner[f, n : n + FEATURE_CHUNK, :]
            )
            total = term if total is None else total + term
        acc[:, n : n + FEATURE_CHUNK] = total
    def norm_first_back(step, carry):
        beta_sum, out_sum = carry
        at = lines_of(step)
        grad_middle = grad_h[at, :] + acc[at, :]
        grad_hidden = norm_back(grad_middle * vectors[4], norm_a[at, :], inv_a[at, 0:1])
        grad_h[at, :] = grad_hidden
        grad_low[at, :] = grad_hidden.astype(BF16)
        return beta_sum + fold_rows(grad_middle), out_sum + fold_rows(grad_hidden)

    beta_attn_sum, out_sum = lax.fori_loop(
        0, norm_steps, norm_first_back, (zero_sum, zero_sum), unroll=True
    )

    def sum_up():
        per_line = width // FF_CHUNK
        for f in range(chunks):
            line_at = 4 + f // per_line
            column = f % per_line * FF_CHUNK
            vec_a[line_at : line_at + 1, column : column + FF_CHUNK] = jnp.sum(
                inner_sum[f], axis=0, keepdims=True
            )
        for i, lines in enumerate((out_sum, outer_sum, beta_attn_sum, beta_final_sum)):
            vec_a[i : i + 1, :] = jnp.sum(lines, axis=0, keepdims=True)
        pool_a[seq] = vec_a[:, pl.ds(pl.multiple_of(own_slice * slice_width, LANES), slice_width)]

    def send_all(start, size, here, make):
        def go(step, carry):
            make(start + lax.rem(here - start + step, size)).start()
            return carry

        lax.fori_loop(1, size, go, 0)

    def wait_all(pool, size, make):
        everything = pool.at[pl.ds(0, size - 1)]
        copy = make(everything, everything)
        copy.wait()

    def bias_copy(i, peer_seq, peer_z):
        return lambda source, target: remote(
            source, target, bias_send.at[i], bias_recv.at[i], peer_seq, peer_z
        )

    def plane_a(peer):
        piece = pl.ds(pl.multiple_of(lax.rem(peer, slices) * slice_width, LANES), slice_width)
        return bias_copy(0, peer, z)(vec_a.at[:, piece], pool_a.at[seq])

    def column_a(peer):
        return bias_copy(1, seq, peer)(z_a.at[z], z_a.at[z])

    own_slice = lax.rem(seq, slices)

    def gather_a(peer):
        return bias_copy(2, peer, z)(sums_a.at[own_slice], sums_a.at[own_slice])

    def column_b(peer):
        return bias_copy(3, seq, peer)(z_b.at[z], z_b.at[z])

    def plane_b(peer):
        return bias_copy(4, peer, z)(pool_b.at[seq], pool_b.at[seq])

    def total_of(pool, places):
        total = pool[places[0]]
        for place in places[1:]:
            total = total + pool[place]
        return total

    def gat_copy(p):
        return remote(
            grad_far.at[p], grad_att.at[p, far_rows], gat_send.at[0], gat_recv.at[0], partner, z
        )

    lines = dot_nt(grad_low[...], m_out[side:width, :])
    for p in range(pairs):
        grad_far[p] = lines[:, p * LANES : (p + 1) * LANES].astype(BF16)
        gat_copy(p).start()
    sum_up()
    send_all(0, seq_size, seq, plane_a)
    lines = dot_nt(grad_low[...], m_out[0:side, :])
    for p in range(pairs):
        grad_att[p, near_rows, :] = lines[:, p * LANES : (p + 1) * LANES].astype(BF16)

    def prepare(p, at):
        scaled = (grad_att[p, at, :].astype(F32) * recip[p, at, :]).astype(BF16)
        product = scaled.astype(F32) * mixed[p, at, :]
        half_lane = lane[at, :]
        for i in range(2):
            delta = jnp.sum(product * head_mask[i], axis=-1, keepdims=True)
            high = delta.astype(BF16).astype(F32)
            extra = jnp.where(half_lane == 0, -high, jnp.where(half_lane == 1, high - delta, 0.0))
            grads = scaled * low_mask[i]
            lefts[2 * p + i, at, :] = jnp.concatenate([grads, extra.astype(BF16)], axis=1)
        grads_turned[p, :, at] = scaled.T

    def score_grads(head, at):
        values = jnp.concatenate([vs[head // 2], ones], axis=1)
        grads = exps[head, at, :].astype(F32) * dot_nt(lefts[head, at, :], values)
        grad_scores[head, at, :] = grads.astype(BF16)
        return fold_rows(grads)

    def attend_back(p, turn):
        start = jnp.where(core == (1 - z_half if turn == 0 else z_half), half, 0)
        part_of = pl.ds(pl.multiple_of(start, half), half)
        dq = None
        dk = []
        dv = []
        for i in range(2):
            cut = slice(i * head_width, (i + 1) * head_width)
            head = 2 * p + i
            term = dot(grad_scores[head, part_of, :], ks[p] * low_mask[i])
            dq = term if dq is None else dq + term
            dk.append(dot(turned[p, cut, :], grad_scores[head, :, part_of]))
            dv.append(dot(grads_turned[p, cut, :], exps[head, :, part_of]))
        dq = (dq * score_scale).astype(BF16)
        dk = jnp.concatenate(dk, axis=0).astype(BF16).T
        dv = jnp.concatenate(dv, axis=0).astype(BF16).T
        for i, block in enumerate((dq, dk, dv)):
            grad_qkv[turn, :, i * side + p * LANES : i * side + (p + 1) * LANES] = block

    def score_grads_of(at):
        sums = []
        prepare(0, at)
        for p in range(pairs):
            if p + 1 < pairs:
                prepare(p + 1, at)
            sums += [score_grads(2 * p, at), score_grads(2 * p + 1, at)]
        return sums

    near_sums = score_grads_of(near_rows)
    whole(grad_far, grad_far, gat_send.at[0], gat_recv.at[0]).wait()
    far_sums = score_grads_of(far_rows)
    for p in range(pairs):
        rows_of_pair = []
        for head in (2 * p, 2 * p + 1):
            sums = near_sums[head] + far_sums[head]
            high = sums.astype(BF16)
            rows_of_pair += [high, (sums - high.astype(F32)).astype(BF16)]
        query_sum = dot(jnp.concatenate(rows_of_pair, axis=0), ks[p])
        query_sum = query_sum[0:16] * head_mask[0] + query_sum[16:32] * head_mask[1]
        z_b[z, p : p + 1, :] = jnp.sum(query_sum, axis=0, keepdims=True) * score_scale
        z_b[z, pairs + p : pairs + p + 1, :] = jnp.sum(
            fold_rows(grad_att[p].astype(F32)), axis=0, keepdims=True
        )
    send_all(0, group, z, column_b)
    for p in range(pairs):
        attend_back(p, 0)
    wait_all(pool_a, seq_size, bias_copy(0, partner, z))
    z_a[z] = total_of(pool_a, range(seq_size))
    send_all(0, group, z, column_a)

    home_line = z - z_half * rows

    def part_copy(turn, j):
        at = far_at(j)
        return remote(
            part_out.at[turn, at],
            part_in.at[turn, at],
            part_send.at[turn, j],
            part_recv.at[turn, j],
            partner,
            z,
        )

    def token_grad(turn, which):
        own = core == (1 - z_half if turn == 0 else z_half)
        columns = pl.ds(pl.multiple_of(which * side, side), side)
        term = dot_nt(grad_qkv[turn], m_qkv[columns, :])
        return term + jnp.where(own, 1.0, 0.0) * grad_h[:, columns]

    def finish(turn):
        for j in range(half_blocks):
            block = (1 - z_half if turn == 0 else z_half) * half_blocks + j
            at = slice(j * span, (j + 1) * span)
            part_copy(turn, j).wait_recv()
            grad_out[turn, at, :] = (part[at, :] + part_in[turn, at, :].astype(F32)).astype(BF16)
            source = grad_out.at[turn, at]
            target_ref = grad_home.at[home_line, core]
            stays = (block == z) & (core == z_half)

            @pl.when(jnp.logical_not(stays))
            def _():
                remote(
                    source,
                    target_ref,
                    grad_send.at[turn],
                    grad_recv.at[home_line],
                    base + z_half,
                    block,
                ).start()

            @pl.when(stays)
            def _():
                pltpu.make_async_copy(source, target_ref, in_sem.at[3]).start()

    def grads_done():
        everything = grad_out.at[0]
        whole(everything, everything, grad_send.at[0], grad_recv.at[0]).wait_send()
        one = everything.at[0:span]

        @pl.when(core == z_half)
        def _():
            pltpu.make_async_copy(one, one, in_sem.at[3]).wait()
            if half_blocks > 1:
                rest = everything.at[span:half]
                whole(rest, rest, grad_send.at[1], grad_recv.at[0]).wait_send()

        @pl.when(core != z_half)
        def _():
            whole(everything, everything, grad_send.at[1], grad_recv.at[0]).wait_send()

        for r in range(rows):
            everything = grad_home.at[r]

            @pl.when(core * rows + r != z)
            def _():
                whole(everything, everything, grad_send.at[0], grad_recv.at[r]).wait_recv()

            @pl.when(core * rows + r == z)
            def _():
                one = everything.at[0]
                whole(one, one, grad_send.at[0], grad_recv.at[r]).wait_recv()

    for turn in range(2):
        if turn == 1:
            for p in range(pairs):
                attend_back(p, 1)
        part_out[turn] = token_grad(turn, far).astype(BF16)
        for j in range(half_blocks):
            part_copy(turn, j).start()
        part[...] = token_grad(turn, core)
        finish(turn)
    wait_all(z_a, group, bias_copy(1, partner, z))
    sums_a[own_slice] = total_of(z_a, range(group))
    send_all(seq - own_slice, slices, seq, gather_a)
    wait_all(z_b, group, bias_copy(3, partner, z))
    pool_b[seq] = total_of(z_b, range(group))
    send_all(0, seq_size, seq, plane_b)

    for turn in range(2):
        for j in range(half_blocks):
            part_copy(turn, j).wait_send()
    wait_all(sums_a, slices, bias_copy(2, partner, z))
    wait_all(pool_b, seq_size, bias_copy(4, partner, z))
    for i in range(2):
        sums_b[i] = total_of(pool_b, range(i, seq_size, 2))

    @pl.when(jnp.logical_not(early))
    def _():
        tokens_sent()

    cotangents_sent()

    def pass_wait(j, carry):
        pass_on(j).wait_send()
        return carry

    lax.fori_loop(0, half_blocks, pass_wait, 0)
    home_done(layer_out, layer_home, lay_send, lay_recv, in_sem.at[2])
    grads_done()


def finish_kernel(
    layer,
    grad,
    sums_a,
    sums_b,
    layer_out,
    input_grad,
    grad_bias_query,
    grad_bias_value,
    grad_bias_out,
    grad_bias_inner,
    grad_bias_outer,
    grad_beta_attn,
    grad_beta_final,
    wide,
    lines,
    inner_line,
    sems,
):
    rows, span, width = layer.shape
    slices, _, slice_width = sums_a.shape
    copies = [pltpu.make_async_copy(layer, layer_out, sems.at[0])]
    copies[0].start()
    for r in range(rows):
        for c in range(2):
            wide[r, :, c * width // 2 : (c + 1) * width // 2] = grad[r, c].astype(F32)
        copies.append(pltpu.make_async_copy(wide.at[r], input_grad.at[r], sems.at[1 + r]))
        copies[-1].start()
    pairs = sums_b.shape[1] // 2
    for i in range(2):
        for p in range(pairs):
            column = (i * pairs + p) * LANES
            lines[0, :, column : column + LANES] = sums_b[i, p : p + 1, :]
            lines[1, :, column : column + LANES] = sums_b[i, pairs + p : pairs + p + 1, :]
    for j in range(slices):
        column = j * slice_width
        for i in range(4):
            lines[2 + i, :, column : column + slice_width] = sums_a[j, i : i + 1, :]
            inner_line[:, i * width + column : i * width + column + slice_width] = sums_a[
                j, 4 + i : 5 + i, :
            ]
    targets = (
        grad_bias_query,
        grad_bias_value,
        grad_bias_out,
        grad_bias_outer,
        grad_beta_attn,
        grad_beta_final,
    )
    for i, target in enumerate(targets):
        copies.append(pltpu.make_async_copy(lines.at[i], target, sems.at[1 + rows + i]))
        copies[-1].start()
    copies.append(pltpu.make_async_copy(inner_line, grad_bias_inner, sems.at[7 + rows]))
    copies[-1].start()
    for copy in copies:
        copy.wait()


def per_device(
    seq_size,
    group,
    tokens,
    doc_lengths,
    pad_counts,
    w_query,
    w_key,
    w_value,
    w_out,
    w_inner,
    w_outer,
    bias_query,
    bias_value,
    bias_out,
    bias_inner,
    bias_outer,
    gain_attn,
    beta_attn,
    gain_final,
    beta_final,
    cotangent,
):
    rows, span, width = tokens.shape
    hidden = w_inner.shape[1]
    slots = span * group
    half = slots // 2
    half_blocks = group // 2
    side = width // 2
    pairs = side // LANES
    chunks = hidden // FF_CHUNK
    slices = min(8, seq_size)
    slice_width = width // slices
    if rows * 2 != group or pairs != 4 or hidden != 4 * width or slots != FF_CHUNK:
        raise ValueError("unsupported sizes")

    any_space = pl.BlockSpec(memory_space=pl.ANY)
    vmem = pl.BlockSpec(memory_space=pltpu.VMEM)
    smem = pl.BlockSpec(memory_space=pltpu.SMEM)
    dma = pltpu.SemaphoreType.DMA
    scratch = [
        pltpu.VMEM((width, 3 * side), BF16),
        pltpu.VMEM((width, width), BF16),
        pltpu.VMEM((chunks, width, FF_CHUNK), BF16),
        pltpu.VMEM((hidden, width), BF16),
        pltpu.VMEM((8, 1, width), F32),
        pltpu.VMEM((1, hidden), F32),
        pltpu.VMEM((slots, width), BF16),
        pltpu.VMEM((half, width), BF16),
        pltpu.VMEM((2, rows, 8, LANES), jnp.int32),
        pltpu.VMEM((pairs, slots, LANES), BF16),
        pltpu.VMEM((pairs, slots, LANES), BF16),
        pltpu.VMEM((pairs, slots, LANES), BF16),
        pltpu.VMEM((2 * pairs, slots, slots), BF16),
        pltpu.VMEM((pairs, slots, LANES), F32),
        pltpu.VMEM((pairs, slots, LANES), F32),
        pltpu.VMEM((pairs, slots, LANES), BF16),
        pltpu.VMEM((pairs, half, LANES), BF16),
        pltpu.VMEM((half, width), F32),
        pltpu.VMEM((half, LANES), F32),
        pltpu.VMEM((half, LANES), F32),
        pltpu.VMEM((half, width), F32),
        pltpu.VMEM((half, width), BF16),
        pltpu.VMEM((half, width), F32),
        pltpu.VMEM((chunks // 2, slots, slots), F32),
        pltpu.VMEM((half, FF_CHUNK), F32),
        pltpu.VMEM((half, FF_CHUNK), F32),
        pltpu.VMEM((half, hidden), BF16),
        pltpu.VMEM((chunks, 8, FF_CHUNK), F32),
        pltpu.VMEM((half, width), F32),
        pltpu.VMEM((half, width), BF16),
        pltpu.VMEM((pairs, slots, LANES), BF16),
        pltpu.VMEM((pairs, half, LANES), BF16),
        pltpu.VMEM((2, half, 3 * side), BF16),
        pltpu.VMEM((pairs, LANES, slots), BF16),
        pltpu.VMEM((2 * pairs, slots, 2 * LANES), BF16),
        pltpu.VMEM((pairs, LANES, slots), BF16),
        pltpu.VMEM((2 * pairs, slots, slots), BF16),
        pltpu.VMEM((half, side), F32),
        pltpu.VMEM((2, half, side), BF16),
        pltpu.VMEM((2, half, side), BF16),
        pltpu.VMEM((2, half, side), BF16),
        pltpu.VMEM((half, width), BF16),
        pltpu.VMEM((8, width), F32),
        pltpu.VMEM((seq_size, 8, slice_width), F32),
        pltpu.VMEM((group, 8, slice_width), F32),
        pltpu.VMEM((seq_size, 8, LANES), F32),
        pltpu.VMEM((group, 8, LANES), F32),
        dma((6,)),
        dma((4,)),
        dma((rows,)),
        dma((half_blocks,)),
        dma((half_blocks,)),
        dma((half_blocks,)),
        dma((2,)),
        dma((rows,)),
        dma((half_blocks,)),
        dma((1,)),
        dma((1,)),
        dma((1,)),
        dma((1,)),
        dma((half_blocks,)),
        dma((rows,)),
        dma((2, half_blocks)),
        dma((2, half_blocks)),
        dma((2,)),
        dma((rows,)),
        dma((5,)),
        dma((5,)),
    ]
    vectors = (
        bias_query,
        bias_value,
        bias_out,
        bias_inner,
        bias_outer,
        gain_attn,
        beta_attn,
        gain_final,
        beta_final,
    )
    layer_home, grad_home, sums_a, sums_b = pl.pallas_call(
        functools.partial(kernel, seq_size, group),
        out_shape=(
            pltpu.VMEM(tokens.shape, BF16),
            pltpu.VMEM((rows, 2, span, side), BF16),
            pltpu.VMEM((slices, 8, slice_width), F32),
            pltpu.VMEM((2, 8, LANES), F32),
        ),
        in_specs=[any_space] * 2 + [smem] * 2 + [any_space] * (6 + len(vectors)),
        out_specs=(vmem,) * 4,
        scratch_shapes=scratch,
        compiler_params=pltpu.CompilerParams(
            collective_id=0, has_side_effects=True, vmem_limit_bytes=58 * 2**20
        ),
    )(
        tokens,
        cotangent,
        doc_lengths,
        pad_counts,
        w_query,
        w_key,
        w_value,
        w_out,
        w_inner,
        w_outer,
        *[vector.reshape(1, -1) for vector in vectors],
    )
    line = jax.ShapeDtypeStruct((1, width), F32)
    results = pl.pallas_call(
        finish_kernel,
        out_shape=(
            jax.ShapeDtypeStruct(tokens.shape, BF16),
            jax.ShapeDtypeStruct(tokens.shape, F32),
            line,
            line,
            line,
            jax.ShapeDtypeStruct((1, hidden), F32),
            line,
            line,
            line,
        ),
        in_specs=[vmem] * 4,
        out_specs=(any_space,) * 9,
        scratch_shapes=[
            pltpu.VMEM(tokens.shape, F32),
            pltpu.VMEM((6, 1, width), F32),
            pltpu.VMEM((1, hidden), F32),
            dma((8 + rows,)),
        ],
        compiler_params=pltpu.CompilerParams(vmem_limit_bytes=32 * 2**20),
    )(layer_home, grad_home, sums_a, sums_b)
    return tuple(results[:2]) + tuple(vector.reshape(-1) for vector in results[2:])


def solution(mesh):
    split = P("seq", "head", None)
    placed = (split, P("seq", None), P("seq")) + (P(),) * 15 + (split,)
    return jax.shard_map(
        functools.partial(per_device, mesh.shape["seq"], mesh.shape["head"]),
        mesh=mesh,
        in_specs=placed,
        out_specs=(split, split) + (P(),) * 7,
        check_vma=False,
    )
```

```python
import functools

import jax
import jax.numpy as jnp
from jax import lax
from jax.experimental import pallas as pl
from jax.experimental.pallas import tpu as pltpu
from jax.sharding import PartitionSpec as P

HEADS = 16
LANES = 128
EPS = 1e-06
BIG = 2.0**30
FF_CHUNK = 512
FEATURE_CHUNK = 512
NORM_ROWS = 32
MESH = pl.DeviceIdType.MESH
F32 = jnp.float32
BF16 = jnp.bfloat16


def dot(left, right):
    return lax.dot_general(left, right, (((1,), (0,)), ((), ())), preferred_element_type=F32)


def dot_nt(left, right):
    return lax.dot_general(left, right, (((1,), (1,)), ((), ())), preferred_element_type=F32)


def dot_tn(left, right):
    return lax.dot_general(left, right, (((0,), (0,)), ((), ())), preferred_element_type=F32)


def normed(hidden):
    row_mean = jnp.mean(hidden, axis=-1, keepdims=True)
    centred = hidden - row_mean
    inv_std = lax.rsqrt(jnp.mean(centred * centred, axis=-1, keepdims=True) + EPS)
    return centred * inv_std, inv_std


def norm_back(gradient, norm, inv_std):
    return inv_std * (
        gradient
        - jnp.mean(gradient, axis=-1, keepdims=True)
        - norm * jnp.mean(gradient * norm, axis=-1, keepdims=True)
    )


def fold_rows(block):
    total = block[0:8]
    for start in range(8, block.shape[0], 8):
        total = total + block[start : start + 8]
    return total


def kernel(
    seq_size,
    group,
    tokens,
    cotangent,
    doc_lengths,
    pad_counts,
    w_query,
    w_key,
    w_value,
    w_out,
    w_inner,
    w_outer,
    in_bias_query,
    in_bias_value,
    in_bias_out,
    in_bias_inner,
    in_bias_outer,
    in_gain_attn,
    in_beta_attn,
    in_gain_final,
    in_beta_final,
    layer_home,
    grad_home,
    sums_a,
    sums_b,
    m_qkv,
    turned_qkv,
    m_out,
    m_inner,
    m_outer,
    vectors,
    bias_inner,
    row,
    cot,
    info,
    qs,
    ks,
    vs,
    exps,
    recip,
    mixed,
    att,
    att_far,
    norm_a,
    inv_a,
    inv_f,
    mid,
    mid_low,
    acc,
    slope,
    raw_even,
    raw_odd,
    active,
    inner_sum,
    grad_h,
    grad_low,
    grad_att,
    grad_far,
    grad_qkv,
    turned,
    lefts,
    grads_turned,
    grad_scores,
    part,
    part_out,
    part_in,
    grad_out,
    layer_out,
    vec_a,
    pool_a,
    z_a,
    pool_b,
    z_b,
    w_sem,
    in_sem,
    tok_send,
    tok_recv,
    pass_send,
    pass_recv,
    info_sem,
    cot_send,
    cot_recv,
    att_send,
    att_recv,
    gat_send,
    gat_recv,
    lay_send,
    lay_recv,
    part_send,
    part_recv,
    grad_send,
    grad_recv,
    bias_send,
    bias_recv,
):
    rows, span, width = tokens.shape
    half_blocks = group // 2
    slots = span * group
    half = slots // 2
    head_width = width // HEADS
    side = width // 2
    pairs = side // LANES
    chunks = m_inner.shape[0]
    norm_steps = half // NORM_ROWS
    score_scale = head_width**-0.5
    slices = sums_a.shape[0]
    slice_width = width // slices

    seq = lax.axis_index("seq")
    z = lax.axis_index("head")
    core = lax.rem(seq, 2)
    base = seq - core
    partner = base + 1 - core
    z_half = z // half_blocks
    far = 1 - core

    def near_at(j):
        return pl.ds(pl.multiple_of(half + j * span, span), span)

    def far_at(j):
        return pl.ds(pl.multiple_of(j * span, span), span)

    def remote(src, dst, send_sem, recv_sem, at_seq, at_head):
        return pltpu.make_async_remote_copy(
            src_ref=src,
            dst_ref=dst,
            send_sem=send_sem,
            recv_sem=recv_sem,
            device_id=(at_seq, at_head),
            device_id_type=MESH,
        )

    barrier = pltpu.get_barrier_semaphore()

    def greet_z(step, carry):
        pl.semaphore_signal(
            barrier, inc=1, device_id=(seq, lax.rem(z + step, group)), device_id_type=MESH
        )
        return carry

    def greet_seq(step, carry):
        pl.semaphore_signal(
            barrier, inc=1, device_id=(lax.rem(seq + step, seq_size), z), device_id_type=MESH
        )
        return carry

    for r in range(half_blocks):
        other = core * half_blocks + r

        @pl.when(other != z)
        def _():
            pl.semaphore_signal(barrier, inc=1, device_id=(partner, other), device_id_type=MESH)

    lax.fori_loop(1, seq_size, greet_seq, 0)
    lax.fori_loop(1, group, greet_z, 0)

    mine = pl.ds(pl.multiple_of(core * side, side), side)
    theirs = pl.ds(pl.multiple_of(far * side, side), side)
    for i, weight in enumerate((w_query, w_key, w_value)):
        pltpu.make_async_copy(
            weight.at[:, mine], m_qkv.at[:, i * side : (i + 1) * side], w_sem.at[0]
        ).start()
    for i, vector in enumerate(
        (
            in_bias_query,
            in_bias_value,
            in_bias_out,
            in_bias_outer,
            in_gain_attn,
            in_beta_attn,
            in_gain_final,
            in_beta_final,
        )
    ):
        pltpu.make_async_copy(vector, vectors.at[i], w_sem.at[4]).start()
    pltpu.make_async_copy(in_bias_inner, bias_inner, w_sem.at[5]).start()

    def loaded(target, i):
        pltpu.make_async_copy(target, target, w_sem.at[i]).wait()

    line = lax.broadcasted_iota(jnp.int32, (8, LANES), 0)
    for r in range(rows):
        first = doc_lengths[r, 0]
        second = first + doc_lengths[r, 1]
        third = second + doc_lengths[r, 2]
        ends = jnp.where(line == 0, first, jnp.where(line == 1, second, third))
        info[core, r] = jnp.where(line == 3, slots - pad_counts[r], ends)

    crossed = jnp.where(z_half == core, 0, group - 1)
    pl.semaphore_wait(barrier, crossed + seq_size - 1 + group - 1)

    early = (z >= half_blocks // 2) & (z < group - half_blocks // 2)

    def spread(index, source, target_ref, at, send_sem, recv_sem):
        r = jnp.where(core == 0, rows - 1 - index, index)
        target = core * rows + r

        @pl.when(target != z)
        def _():
            remote(
                source.at[r],
                target_ref.at[at],
                send_sem.at[r],
                recv_sem.at[z - z_half * half_blocks],
                base + z_half,
                target,
            ).start()

    def keep(source, target_ref, at, local_sem):
        @pl.when(core == z_half)
        def _():
            pltpu.make_async_copy(
                source.at[z - z_half * rows], target_ref.at[at], local_sem
            ).start()

    def spread_done(index, source, target_ref, at, send_sem, recv_sem):
        r = jnp.where(core == 0, rows - 1 - index, index)
        target = core * rows + r

        @pl.when(target != z)
        def _():
            remote(
                source.at[r],
                target_ref.at[at],
                send_sem.at[r],
                recv_sem.at[z - z_half * half_blocks],
                base + z_half,
                target,
            ).wait_send()

    def arrived(source, target_ref, at, block, send_sem, recv_sem, local_sem):
        j = block - core * half_blocks

        @pl.when(block != z)
        def _():
            remote(
                source.at[0],
                target_ref.at[at],
                send_sem.at[0],
                recv_sem.at[j],
                base + z_half,
                block,
            ).wait_recv()

        @pl.when(block == z)
        def _():
            pltpu.make_async_copy(source.at[0], target_ref.at[at], local_sem).wait()

    info_copy = remote(info.at[core], info.at[core], info_sem.at[0], info_sem.at[1], partner, z)
    info_copy.start()
    tok_at = near_at(z - z_half * half_blocks)
    cot_at = pl.ds(pl.multiple_of((z - z_half * half_blocks) * span, span), span)

    def send_tokens():
        for index in range(rows):
            spread(index, tokens, row, tok_at, tok_send, tok_recv)

    def tokens_sent():
        for index in range(rows):
            spread_done(index, tokens, row, tok_at, tok_send, tok_recv)

    def send_cotangents():
        for index in range(rows):
            spread(index, cotangent, cot, cot_at, cot_send, cot_recv)

    def cotangents_sent():
        for index in range(rows):
            spread_done(index, cotangent, cot, cot_at, cot_send, cot_recv)

    send_tokens()
    keep(tokens, row, tok_at, in_sem.at[0])
    keep(cotangent, cot, cot_at, in_sem.at[1])

    @pl.when(early)
    def _():
        send_cotangents()

    pltpu.make_async_copy(w_out.at[mine], m_out.at[0:side], w_sem.at[1]).start()
    pltpu.make_async_copy(w_out.at[theirs], m_out.at[side:width], w_sem.at[1]).start()
    for f in range(chunks):
        columns = slice(f * FF_CHUNK, (f + 1) * FF_CHUNK)
        pltpu.make_async_copy(w_inner.at[:, columns], m_inner.at[f], w_sem.at[2]).start()
    pltpu.make_async_copy(w_outer, m_outer, w_sem.at[3]).start()

    info_copy.wait_send()
    remote(info.at[far], info.at[far], info_sem.at[0], info_sem.at[1], partner, z).wait_recv()
    loaded(m_qkv, 0)
    loaded(vectors, 4)
    loaded(bias_inner, 5)
    bias_query = vectors[0, :, mine]
    bias_value = vectors[1, :, mine]

    lane = lax.broadcasted_iota(jnp.int32, (slots, LANES), 1)
    place = lax.broadcasted_iota(jnp.int32, (slots, LANES), 0)
    slot = jnp.where(place < half, far * half + place, core * half + place - half)
    ends = info[z_half, z - z_half * rows]
    doc = (slot >= ends[0:1]).astype(jnp.int32)
    for i in range(1, 4):
        doc = doc + (slot >= ends[i : i + 1]).astype(jnp.int32)
    doc_query = jnp.where(doc == lane, BIG, 0.0).astype(BF16)
    doc_key = jnp.where((doc != lane) & (lane < 5), -1.0, 0.0).astype(BF16)
    ones = jnp.ones((slots, LANES), BF16)

    def pass_on(j):
        return remote(
            row.at[near_at(j)], row.at[far_at(j)], pass_send.at[j], pass_recv.at[j], partner, z
        )

    def taken(which, step):
        local = lax.rem(z - z_half * half_blocks + step, half_blocks)
        beyond = jnp.where(z_half == 0, half_blocks - 1 - step, step)
        return jnp.where(which == z_half, local, beyond)

    def project(at):
        x = row[at, :]
        q = (dot(x, m_qkv[:, 0:side]) + bias_query) * score_scale
        k = dot(x, m_qkv[:, side : 2 * side])
        v = dot(x, m_qkv[:, 2 * side : 3 * side]) + bias_value
        for p in range(pairs):
            cut = slice(p * LANES, (p + 1) * LANES)
            qs[p, at, :] = q[:, cut].astype(BF16)
            if span % LANES == 0:
                turned[p, :, at] = q[:, cut].astype(BF16).T
            ks[p, at, :] = k[:, cut].astype(BF16)
            vs[p, at, :] = v[:, cut].astype(BF16)


    def project_step(i, carry):
        in_turn = core == z_half
        own = jnp.where(in_turn, i < half_blocks, lax.rem(i, 2) == 1)
        step = jnp.where(in_turn, lax.rem(i, half_blocks), i // 2)
        j = taken(jnp.where(own, core, far), step)

        @pl.when(own)
        def _():
            block = core * half_blocks + j

            @pl.when((i == group - 1) & jnp.logical_not(early))
            def _():
                send_cotangents()

            arrived(tokens, row, near_at(j), block, tok_send, tok_recv, in_sem.at[0])
            pass_on(j).start()

        @pl.when(jnp.logical_not(own))
        def _():
            pass_on(j).wait_recv()

            @pl.when(in_turn & (i == half_blocks) & jnp.logical_not(early))
            def _():
                send_cotangents()

        project(pl.ds(pl.multiple_of(jnp.where(own, half, 0) + j * span, span), span))
        return carry

    for i in range(0, 3 * side, 2 * LANES):
        turned_qkv[i : i + 2 * LANES, :] = m_qkv[:, i : i + 2 * LANES].T

    lax.fori_loop(0, group, project_step, 0)

    for i, target in enumerate((m_out, m_inner, m_outer)):
        loaded(target, 1 + i)

    lane_row = lax.broadcasted_iota(jnp.int32, (1, LANES), 1)
    head_mask = [
        (lane_row < head_width).astype(F32),
        (lane_row >= head_width).astype(F32),
    ]
    low_mask = [mask.astype(BF16) for mask in head_mask]
    near_rows = slice(half, slots)
    far_rows = slice(0, half)

    def score(unit, spot):
        head, at = unit
        p = head // 2
        left = jnp.concatenate([qs[p, at, :] * low_mask[head % 2], doc_query[at, :]], axis=1)
        keys = jnp.concatenate([ks[p], doc_key], axis=1)
        slope[spot, 0:half, :] = dot_nt(left, keys)

    def soften(unit, spot):
        head, at = unit
        scores = slope[spot, 0:half, :]
        exponent = jnp.exp(scores - jnp.max(scores, axis=-1, keepdims=True))
        exps[head, at, :] = exponent.astype(BF16)

    def mix(unit):
        head, at = unit
        both = dot(exps[head, at, :], jnp.concatenate([vs[head // 2], ones], axis=1))
        share = 1.0 / both[:, LANES:]
        return both[:, :LANES] * share * head_mask[head % 2], share * head_mask[head % 2]

    units = [(head, at) for at in (far_rows, near_rows) for head in range(2 * pairs)]
    spots = slope.shape[0]
    score(units[0], 0)
    for i in range(len(units) + 1):
        if i + 1 < len(units):
            score(units[i + 1], (i + 1) % spots)
        if i > 0:
            head, at = units[i - 1]
            if head % 2 == 0:
                held = mix(units[i - 1])
            else:
                total, shares = (a + b for a, b in zip(held, mix(units[i - 1])))
                p = head // 2
                mixed[p, at, :] = total
                recip[p, at, :] = shares
                att[p, at, :] = total.astype(BF16)
        if i < len(units):
            soften(units[i], i % spots)
        if i == 2 * pairs:
            att_copy = remote(
                att.at[:, far_rows], att_far, att_send.at[0], att_recv.at[0], partner, z
            )
            att_copy.start()

    def whole(source, target, send_sem, recv_sem):
        return remote(source, target, send_sem, recv_sem, partner, z)

    att_copy.wait()
    left = jnp.concatenate(
        [att[p, near_rows, :] for p in range(pairs)] + [att_far[p] for p in range(pairs)], axis=1
    )
    acc[...] = dot(left, m_out[...])
    def lines_of(step):
        return pl.ds(pl.multiple_of(step * NORM_ROWS, NORM_ROWS), NORM_ROWS)

    def norm_first(step, carry):
        at = lines_of(step)
        near = pl.ds(pl.multiple_of(half + step * NORM_ROWS, NORM_ROWS), NORM_ROWS)
        hidden = row[near, :].astype(F32) + acc[at, :] + vectors[2]
        norm, inv_std = normed(hidden)
        norm_a[at, :] = norm
        inv_a[at, :] = jnp.broadcast_to(inv_std, (NORM_ROWS, LANES))
        middle = norm * vectors[4] + vectors[5]
        mid[at, :] = middle
        mid_low[at, :] = middle.astype(BF16)
        return carry

    lax.fori_loop(0, norm_steps, norm_first, 0, unroll=True)

    def slope_at(f):
        return f // 2, slice(f % 2 * half, (f % 2 + 1) * half)

    def activate(f):
        columns = slice(f * FF_CHUNK, (f + 1) * FF_CHUNK)
        inner = raw[f % 2][...] + bias_inner[:, columns]
        cdf = 0.5 * (1.0 + lax.erf(inner * 0.7071067811865476))
        which, lines = slope_at(f)
        slope[which, lines, :] = cdf + inner * jnp.exp(-0.5 * inner * inner) * 0.3989422804014327
        active[:, columns] = (inner * cdf).astype(BF16)

    raw = (raw_even, raw_odd)
    raw_even[...] = dot(mid_low[...], m_inner[0])
    for f in range(chunks):
        if f + 1 < chunks:
            raw[(f + 1) % 2][...] = dot(mid_low[...], m_inner[f + 1])
        activate(f)
    for n in range(0, width, FEATURE_CHUNK):
        acc[:, n : n + FEATURE_CHUNK] = dot(active[...], m_outer[:, n : n + FEATURE_CHUNK])

    live_end = ends[3:4, 0:1]

    def live_at(step):
        place = lax.broadcasted_iota(jnp.int32, (NORM_ROWS, 1), 0) + core * half + step * NORM_ROWS
        return (place < live_end).astype(F32)

    def norm_last(step, carry):
        at = lines_of(step)
        norm, inv_std = normed(mid[at, :] + acc[at, :] + vectors[3])
        acc[at, :] = norm
        inv_f[at, :] = jnp.broadcast_to(inv_std, (NORM_ROWS, LANES))
        layer_out[at, :] = (live_at(step) * (norm * vectors[6] + vectors[7])).astype(BF16)
        return carry

    lax.fori_loop(0, norm_steps, norm_last, 0, unroll=True)

    def home_block(block, source, target_ref, send_sem, recv_sem, local_sem):
        j = block - core * half_blocks
        src = source.at[pl.ds(pl.multiple_of(j * span, span), span)]
        line_at = z - z_half * rows

        @pl.when(block != z)
        def _():
            remote(
                src,
                target_ref.at[line_at],
                send_sem.at[j],
                recv_sem.at[line_at],
                base + z_half,
                block,
            ).start()

        @pl.when(block == z)
        def _():
            pltpu.make_async_copy(src, target_ref.at[line_at], local_sem).start()

    def home_done(source, target_ref, send_sem, recv_sem, local_sem):
        for j in range(half_blocks):
            block = core * half_blocks + j
            src = source.at[j * span : (j + 1) * span]
            line_at = z - z_half * rows

            @pl.when(block != z)
            def _():
                remote(
                    src,
                    target_ref.at[line_at],
                    send_sem.at[j],
                    recv_sem.at[line_at],
                    base + z_half,
                    block,
                ).wait_send()

            @pl.when(block == z)
            def _():
                pltpu.make_async_copy(src, target_ref.at[line_at], local_sem).wait()

        for r in range(rows):
            target = core * rows + r

            @pl.when(target != z)
            def _():
                remote(
                    source.at[0:span],
                    target_ref.at[r],
                    send_sem.at[0],
                    recv_sem.at[r],
                    base + z_half,
                    target,
                ).wait_recv()

    for j in range(half_blocks):
        home_block(
            core * half_blocks + j, layer_out, layer_home, lay_send, lay_recv, in_sem.at[2]
        )
    if span % LANES != 0:
        for p in range(pairs):
            turned[p] = qs[p].T

    def cot_wait(j, carry):
        at = pl.ds(pl.multiple_of(j * span, span), span)
        arrived(cotangent, cot, at, core * half_blocks + j, cot_send, cot_recv, in_sem.at[1])
        return carry

    lax.fori_loop(0, half_blocks, cot_wait, 0)

    zero_sum = jnp.zeros((8, width), F32)

    def norm_last_back(step, carry):
        beta_sum, outer_sum = carry
        at = lines_of(step)
        grad_final = live_at(step) * cot[at, :].astype(F32)
        grad_hidden = norm_back(grad_final * vectors[6], acc[at, :], inv_f[at, 0:1])
        grad_h[at, :] = grad_hidden
        grad_low[at, :] = grad_hidden.astype(BF16)
        return beta_sum + fold_rows(grad_final), outer_sum + fold_rows(grad_hidden)

    sums = lax.fori_loop(0, norm_steps, norm_last_back, (zero_sum, zero_sum), unroll=True)
    beta_final_sum, outer_sum = sums

    for f in range(chunks):
        which, lines = slope_at(f)
        columns = slice(f * FF_CHUNK, (f + 1) * FF_CHUNK)
        grad_active = dot_nt(grad_low[...], m_outer[columns, :])
        grad_inner = (grad_active * slope[which, lines, :]).astype(BF16)
        active[:, columns] = grad_inner
        inner_sum[f] = fold_rows(grad_inner.astype(F32))
    for n in range(0, width, FEATURE_CHUNK):
        total = None
        for f in range(chunks):
            term = dot_nt(
                active[:, f * FF_CHUNK : (f + 1) * FF_CHUNK], m_inner[f, n : n + FEATURE_CHUNK, :]
            )
            total = term if total is None else total + term
        acc[:, n : n + FEATURE_CHUNK] = total
    def norm_first_back(step, carry):
        beta_sum, out_sum = carry
        at = lines_of(step)
        grad_middle = grad_h[at, :] + acc[at, :]
        grad_hidden = norm_back(grad_middle * vectors[4], norm_a[at, :], inv_a[at, 0:1])
        grad_h[at, :] = grad_hidden
        grad_low[at, :] = grad_hidden.astype(BF16)
        return beta_sum + fold_rows(grad_middle), out_sum + fold_rows(grad_hidden)

    beta_attn_sum, out_sum = lax.fori_loop(
        0, norm_steps, norm_first_back, (zero_sum, zero_sum), unroll=True
    )

    def sum_up():
        per_line = width // FF_CHUNK
        for f in range(chunks):
            line_at = 4 + f // per_line
            column = f % per_line * FF_CHUNK
            vec_a[line_at : line_at + 1, column : column + FF_CHUNK] = jnp.sum(
                inner_sum[f], axis=0, keepdims=True
            )
        for i, lines in enumerate((out_sum, outer_sum, beta_attn_sum, beta_final_sum)):
            vec_a[i : i + 1, :] = jnp.sum(lines, axis=0, keepdims=True)
        pool_a[seq] = vec_a[:, pl.ds(pl.multiple_of(own_slice * slice_width, LANES), slice_width)]

    def send_all(start, size, here, make):
        def go(step, carry):
            make(start + lax.rem(here - start + step, size)).start()
            return carry

        lax.fori_loop(1, size, go, 0)

    def wait_all(pool, size, make):
        everything = pool.at[pl.ds(0, size - 1)]
        copy = make(everything, everything)
        copy.wait()

    def bias_copy(i, peer_seq, peer_z):
        return lambda source, target: remote(
            source, target, bias_send.at[i], bias_recv.at[i], peer_seq, peer_z
        )

    def plane_a(peer):
        piece = pl.ds(pl.multiple_of(lax.rem(peer, slices) * slice_width, LANES), slice_width)
        return bias_copy(0, peer, z)(vec_a.at[:, piece], pool_a.at[seq])

    def column_a(peer):
        return bias_copy(1, seq, peer)(z_a.at[z], z_a.at[z])

    own_slice = lax.rem(seq, slices)

    def gather_a(peer):
        return bias_copy(2, peer, z)(sums_a.at[own_slice], sums_a.at[own_slice])

    def column_b(peer):
        return bias_copy(3, seq, peer)(z_b.at[z], z_b.at[z])

    def plane_b(peer):
        return bias_copy(4, peer, z)(pool_b.at[seq], pool_b.at[seq])

    def total_of(pool, places):
        total = pool[places[0]]
        for place in places[1:]:
            total = total + pool[place]
        return total

    def gat_copy(p):
        return remote(
            grad_far.at[p], grad_att.at[p, far_rows], gat_send.at[0], gat_recv.at[0], partner, z
        )

    lines = dot_nt(grad_low[...], m_out[side:width, :])
    for p in range(pairs):
        grad_far[p] = lines[:, p * LANES : (p + 1) * LANES].astype(BF16)
        gat_copy(p).start()
    sum_up()
    send_all(0, seq_size, seq, plane_a)
    lines = dot_nt(grad_low[...], m_out[0:side, :])
    for p in range(pairs):
        grad_att[p, near_rows, :] = lines[:, p * LANES : (p + 1) * LANES].astype(BF16)

    def prepare(p, at):
        scaled = (grad_att[p, at, :].astype(F32) * recip[p, at, :]).astype(BF16)
        product = scaled.astype(F32) * mixed[p, at, :]
        half_lane = lane[at, :]
        for i in range(2):
            delta = jnp.sum(product * head_mask[i], axis=-1, keepdims=True)
            high = delta.astype(BF16).astype(F32)
            extra = jnp.where(half_lane == 0, -high, jnp.where(half_lane == 1, high - delta, 0.0))
            grads = scaled * low_mask[i]
            lefts[2 * p + i, at, :] = jnp.concatenate([grads, extra.astype(BF16)], axis=1)
        grads_turned[p, :, at] = scaled.T

    def score_grads(head, at):
        values = jnp.concatenate([vs[head // 2], ones], axis=1)
        grads = exps[head, at, :].astype(F32) * dot_nt(lefts[head, at, :], values)
        grad_scores[head, at, :] = grads.astype(BF16)
        return fold_rows(grads)

    quarter = slots // 4

    def half_of(turn):
        return 1 - z_half if turn < 2 else z_half

    def start_of(turn):
        return jnp.where(core == half_of(turn), half, 0) + turn % 2 * quarter

    def attend_back(p, turn):
        part_of = pl.ds(pl.multiple_of(start_of(turn), quarter), quarter)
        dq = None
        dk = []
        dv = []
        for i in range(2):
            cut = slice(i * head_width, (i + 1) * head_width)
            head = 2 * p + i
            term = dot(grad_scores[head, part_of, :], ks[p] * low_mask[i])
            dq = term if dq is None else dq + term
            dk.append(dot(turned[p, cut, :], grad_scores[head, :, part_of]))
            dv.append(dot(grads_turned[p, cut, :], exps[head, :, part_of]))
        dq = (dq * score_scale).astype(BF16)
        dk = jnp.concatenate(dk, axis=0).astype(BF16).T
        dv = jnp.concatenate(dv, axis=0).astype(BF16).T
        for i, block in enumerate((dq, dk, dv)):
            grad_qkv[turn, :, i * side + p * LANES : i * side + (p + 1) * LANES] = block

    def score_grads_of(at):
        sums = []
        prepare(0, at)
        for p in range(pairs):
            if p + 1 < pairs:
                prepare(p + 1, at)
            sums += [score_grads(2 * p, at), score_grads(2 * p + 1, at)]
        return sums

    near_sums = score_grads_of(near_rows)
    whole(grad_far, grad_far, gat_send.at[0], gat_recv.at[0]).wait()
    far_sums = score_grads_of(far_rows)
    for p in range(pairs):
        rows_of_pair = []
        for head in (2 * p, 2 * p + 1):
            sums = near_sums[head] + far_sums[head]
            high = sums.astype(BF16)
            rows_of_pair += [high, (sums - high.astype(F32)).astype(BF16)]
        query_sum = dot(jnp.concatenate(rows_of_pair, axis=0), ks[p])
        query_sum = query_sum[0:16] * head_mask[0] + query_sum[16:32] * head_mask[1]
        z_b[z, p : p + 1, :] = jnp.sum(query_sum, axis=0, keepdims=True) * score_scale
        z_b[z, pairs + p : pairs + p + 1, :] = jnp.sum(
            fold_rows(grad_att[p].astype(F32)), axis=0, keepdims=True
        )
    send_all(0, group, z, column_b)
    for p in range(pairs):
        attend_back(p, 0)
    wait_all(pool_a, seq_size, bias_copy(0, partner, z))
    z_a[z] = total_of(pool_a, range(seq_size))
    send_all(0, group, z, column_a)

    home_line = z - z_half * rows

    def part_copy(turn):
        return remote(
            part_out.at[turn], part_in.at[turn], part_send.at[turn], part_recv.at[turn], partner, z
        )

    def token_grad(turn, which):
        own = core == half_of(turn)
        columns = pl.ds(pl.multiple_of(which * side, side), side)
        near = slice(turn % 2 * quarter, (turn % 2 + 1) * quarter)
        term = dot(grad_qkv[turn], turned_qkv[:, columns])
        return term + jnp.where(own, 1.0, 0.0) * grad_h[near, columns]

    def finish(turn):
        part_copy(turn).wait_recv()
        at = slice(turn * quarter, (turn + 1) * quarter)
        grad_out[at, :] = (part[turn % 2] + part_in[turn].astype(F32)).astype(BF16)
        for j in range(quarter // span):
            block = half_of(turn) * half_blocks + turn % 2 * (quarter // span) + j
            source = grad_out.at[turn * quarter + j * span : turn * quarter + (j + 1) * span]
            target_ref = grad_home.at[home_line, core]
            stays = (block == z) & (core == z_half)

            @pl.when(jnp.logical_not(stays))
            def _():
                remote(
                    source,
                    target_ref,
                    grad_send.at[0],
                    grad_recv.at[home_line],
                    base + z_half,
                    block,
                ).start()

            @pl.when(stays)
            def _():
                pltpu.make_async_copy(source, target_ref, in_sem.at[3]).start()

    def grads_done():
        @pl.when(core == z_half)
        def _():
            one = grad_out.at[0:span]
            rest = grad_out.at[span:slots]
            pltpu.make_async_copy(one, one, in_sem.at[3]).wait()
            whole(rest, rest, grad_send.at[0], grad_recv.at[0]).wait_send()

        @pl.when(core != z_half)
        def _():
            whole(grad_out, grad_out, grad_send.at[0], grad_recv.at[0]).wait_send()

        for r in range(rows):
            everything = grad_home.at[r]

            @pl.when(core * rows + r != z)
            def _():
                whole(everything, everything, grad_send.at[0], grad_recv.at[r]).wait_recv()

            @pl.when(core * rows + r == z)
            def _():
                one = everything.at[0]
                whole(one, one, grad_send.at[0], grad_recv.at[r]).wait_recv()

    for turn in range(4):
        if turn > 0:
            for p in range(pairs):
                attend_back(p, turn)
            finish(turn - 1)
        part_out[turn] = token_grad(turn, far).astype(BF16)
        part_copy(turn).start()
        part[turn % 2] = token_grad(turn, core)
    finish(3)
    wait_all(z_a, group, bias_copy(1, partner, z))
    sums_a[own_slice] = total_of(z_a, range(group))
    send_all(seq - own_slice, slices, seq, gather_a)
    wait_all(z_b, group, bias_copy(3, partner, z))
    pool_b[seq] = total_of(z_b, range(group))
    send_all(0, seq_size, seq, plane_b)

    for turn in range(4):
        part_copy(turn).wait_send()
    wait_all(sums_a, slices, bias_copy(2, partner, z))
    wait_all(pool_b, seq_size, bias_copy(4, partner, z))
    for i in range(2):
        sums_b[i] = total_of(pool_b, range(i, seq_size, 2))
    tokens_sent()
    cotangents_sent()

    def pass_wait(j, carry):
        pass_on(j).wait_send()
        return carry

    lax.fori_loop(0, half_blocks, pass_wait, 0)
    home_done(layer_out, layer_home, lay_send, lay_recv, in_sem.at[2])
    grads_done()


def finish_kernel(
    layer,
    grad,
    sums_a,
    sums_b,
    layer_out,
    input_grad,
    grad_bias_query,
    grad_bias_value,
    grad_bias_out,
    grad_bias_inner,
    grad_bias_outer,
    grad_beta_attn,
    grad_beta_final,
    wide,
    lines,
    inner_line,
    sems,
):
    rows, span, width = layer.shape
    slices, _, slice_width = sums_a.shape
    copies = [pltpu.make_async_copy(layer, layer_out, sems.at[0])]
    copies[0].start()
    for r in range(rows):
        for c in range(2):
            wide[r, :, c * width // 2 : (c + 1) * width // 2] = grad[r, c].astype(F32)
        copies.append(pltpu.make_async_copy(wide.at[r], input_grad.at[r], sems.at[1 + r]))
        copies[-1].start()
    pairs = sums_b.shape[1] // 2
    for i in range(2):
        for p in range(pairs):
            column = (i * pairs + p) * LANES
            lines[0, :, column : column + LANES] = sums_b[i, p : p + 1, :]
            lines[1, :, column : column + LANES] = sums_b[i, pairs + p : pairs + p + 1, :]
    for j in range(slices):
        column = j * slice_width
        for i in range(4):
            lines[2 + i, :, column : column + slice_width] = sums_a[j, i : i + 1, :]
            inner_line[:, i * width + column : i * width + column + slice_width] = sums_a[
                j, 4 + i : 5 + i, :
            ]
    targets = (
        grad_bias_query,
        grad_bias_value,
        grad_bias_out,
        grad_bias_outer,
        grad_beta_attn,
        grad_beta_final,
    )
    for i, target in enumerate(targets):
        copies.append(pltpu.make_async_copy(lines.at[i], target, sems.at[1 + rows + i]))
        copies[-1].start()
    copies.append(pltpu.make_async_copy(inner_line, grad_bias_inner, sems.at[7 + rows]))
    copies[-1].start()
    for copy in copies:
        copy.wait()


def per_device(
    seq_size,
    group,
    tokens,
    doc_lengths,
    pad_counts,
    w_query,
    w_key,
    w_value,
    w_out,
    w_inner,
    w_outer,
    bias_query,
    bias_value,
    bias_out,
    bias_inner,
    bias_outer,
    gain_attn,
    beta_attn,
    gain_final,
    beta_final,
    cotangent,
):
    rows, span, width = tokens.shape
    hidden = w_inner.shape[1]
    slots = span * group
    half = slots // 2
    half_blocks = group // 2
    side = width // 2
    pairs = side // LANES
    chunks = hidden // FF_CHUNK
    slices = min(8, seq_size)
    quarter = slots // 4
    slice_width = width // slices
    if rows * 2 != group or pairs != 4 or hidden != 4 * width or slots != FF_CHUNK or quarter % span != 0:
        raise ValueError("unsupported sizes")

    any_space = pl.BlockSpec(memory_space=pl.ANY)
    vmem = pl.BlockSpec(memory_space=pltpu.VMEM)
    smem = pl.BlockSpec(memory_space=pltpu.SMEM)
    dma = pltpu.SemaphoreType.DMA
    scratch = [
        pltpu.VMEM((width, 3 * side), BF16),
        pltpu.VMEM((3 * side, width), BF16),
        pltpu.VMEM((width, width), BF16),
        pltpu.VMEM((chunks, width, FF_CHUNK), BF16),
        pltpu.VMEM((hidden, width), BF16),
        pltpu.VMEM((8, 1, width), F32),
        pltpu.VMEM((1, hidden), F32),
        pltpu.VMEM((slots, width), BF16),
        pltpu.VMEM((half, width), BF16),
        pltpu.VMEM((2, rows, 8, LANES), jnp.int32),
        pltpu.VMEM((pairs, slots, LANES), BF16),
        pltpu.VMEM((pairs, slots, LANES), BF16),
        pltpu.VMEM((pairs, slots, LANES), BF16),
        pltpu.VMEM((2 * pairs, slots, slots), BF16),
        pltpu.VMEM((pairs, slots, LANES), F32),
        pltpu.VMEM((pairs, slots, LANES), F32),
        pltpu.VMEM((pairs, slots, LANES), BF16),
        pltpu.VMEM((pairs, half, LANES), BF16),
        pltpu.VMEM((half, width), F32),
        pltpu.VMEM((half, LANES), F32),
        pltpu.VMEM((half, LANES), F32),
        pltpu.VMEM((half, width), F32),
        pltpu.VMEM((half, width), BF16),
        pltpu.VMEM((half, width), F32),
        pltpu.VMEM((chunks // 2, slots, slots), F32),
        pltpu.VMEM((half, FF_CHUNK), F32),
        pltpu.VMEM((half, FF_CHUNK), F32),
        pltpu.VMEM((half, hidden), BF16),
        pltpu.VMEM((chunks, 8, FF_CHUNK), F32),
        pltpu.VMEM((half, width), F32),
        pltpu.VMEM((half, width), BF16),
        pltpu.VMEM((pairs, slots, LANES), BF16),
        pltpu.VMEM((pairs, half, LANES), BF16),
        pltpu.VMEM((4, quarter, 3 * side), BF16),
        pltpu.VMEM((pairs, LANES, slots), BF16),
        pltpu.VMEM((2 * pairs, slots, 2 * LANES), BF16),
        pltpu.VMEM((pairs, LANES, slots), BF16),
        pltpu.VMEM((2 * pairs, slots, slots), BF16),
        pltpu.VMEM((2, quarter, side), F32),
        pltpu.VMEM((4, quarter, side), BF16),
        pltpu.VMEM((4, quarter, side), BF16),
        pltpu.VMEM((slots, side), BF16),
        pltpu.VMEM((half, width), BF16),
        pltpu.VMEM((8, width), F32),
        pltpu.VMEM((seq_size, 8, slice_width), F32),
        pltpu.VMEM((group, 8, slice_width), F32),
        pltpu.VMEM((seq_size, 8, LANES), F32),
        pltpu.VMEM((group, 8, LANES), F32),
        dma((6,)),
        dma((4,)),
        dma((rows,)),
        dma((half_blocks,)),
        dma((half_blocks,)),
        dma((half_blocks,)),
        dma((2,)),
        dma((rows,)),
        dma((half_blocks,)),
        dma((1,)),
        dma((1,)),
        dma((1,)),
        dma((1,)),
        dma((half_blocks,)),
        dma((rows,)),
        dma((4,)),
        dma((4,)),
        dma((1,)),
        dma((rows,)),
        dma((5,)),
        dma((5,)),
    ]
    vectors = (
        bias_query,
        bias_value,
        bias_out,
        bias_inner,
        bias_outer,
        gain_attn,
        beta_attn,
        gain_final,
        beta_final,
    )
    layer_home, grad_home, sums_a, sums_b = pl.pallas_call(
        functools.partial(kernel, seq_size, group),
        out_shape=(
            pltpu.VMEM(tokens.shape, BF16),
            pltpu.VMEM((rows, 2, span, side), BF16),
            pltpu.VMEM((slices, 8, slice_width), F32),
            pltpu.VMEM((2, 8, LANES), F32),
        ),
        in_specs=[any_space] * 2 + [smem] * 2 + [any_space] * (6 + len(vectors)),
        out_specs=(vmem,) * 4,
        scratch_shapes=scratch,
        compiler_params=pltpu.CompilerParams(
            collective_id=0, has_side_effects=True, vmem_limit_bytes=58 * 2**20
        ),
    )(
        tokens,
        cotangent,
        doc_lengths,
        pad_counts,
        w_query,
        w_key,
        w_value,
        w_out,
        w_inner,
        w_outer,
        *[vector.reshape(1, -1) for vector in vectors],
    )
    line = jax.ShapeDtypeStruct((1, width), F32)
    results = pl.pallas_call(
        finish_kernel,
        out_shape=(
            jax.ShapeDtypeStruct(tokens.shape, BF16),
            jax.ShapeDtypeStruct(tokens.shape, F32),
            line,
            line,
            line,
            jax.ShapeDtypeStruct((1, hidden), F32),
            line,
            line,
            line,
        ),
        in_specs=[vmem] * 4,
        out_specs=(any_space,) * 9,
        scratch_shapes=[
            pltpu.VMEM(tokens.shape, F32),
            pltpu.VMEM((6, 1, width), F32),
            pltpu.VMEM((1, hidden), F32),
            dma((8 + rows,)),
        ],
        compiler_params=pltpu.CompilerParams(vmem_limit_bytes=32 * 2**20),
    )(layer_home, grad_home, sums_a, sums_b)
    return tuple(results[:2]) + tuple(vector.reshape(-1) for vector in results[2:])


def solution(mesh):
    split = P("seq", "head", None)
    placed = (split, P("seq", None), P("seq")) + (P(),) * 15 + (split,)
    return jax.shard_map(
        functools.partial(per_device, mesh.shape["seq"], mesh.shape["head"]),
        mesh=mesh,
        in_specs=placed,
        out_specs=(split, split) + (P(),) * 7,
        check_vma=False,
    )
```

```python
import functools

import jax
import jax.numpy as jnp
from jax import lax
from jax.experimental import pallas as pl
from jax.experimental.pallas import tpu as pltpu
from jax.sharding import PartitionSpec as P

HEADS = 16
LANES = 128
EPS = 1e-06
BIG = 2.0**30
FF_CHUNK = 512
FEATURE_CHUNK = 512
NORM_ROWS = 32
MESH = pl.DeviceIdType.MESH
F32 = jnp.float32
BF16 = jnp.bfloat16


def dot(left, right):
    return lax.dot_general(left, right, (((1,), (0,)), ((), ())), preferred_element_type=F32)


def dot_nt(left, right):
    return lax.dot_general(left, right, (((1,), (1,)), ((), ())), preferred_element_type=F32)


def dot_tn(left, right):
    return lax.dot_general(left, right, (((0,), (0,)), ((), ())), preferred_element_type=F32)


def normed(hidden):
    row_mean = jnp.mean(hidden, axis=-1, keepdims=True)
    centred = hidden - row_mean
    inv_std = lax.rsqrt(jnp.mean(centred * centred, axis=-1, keepdims=True) + EPS)
    return centred * inv_std, inv_std


def norm_back(gradient, norm, inv_std):
    return inv_std * (
        gradient
        - jnp.mean(gradient, axis=-1, keepdims=True)
        - norm * jnp.mean(gradient * norm, axis=-1, keepdims=True)
    )


def fold_rows(block):
    total = block[0:8]
    for start in range(8, block.shape[0], 8):
        total = total + block[start : start + 8]
    return total


def kernel(
    seq_size,
    group,
    tokens,
    cotangent,
    doc_lengths,
    pad_counts,
    w_query,
    w_key,
    w_value,
    w_out,
    w_inner,
    w_outer,
    in_bias_query,
    in_bias_value,
    in_bias_out,
    in_bias_inner,
    in_bias_outer,
    in_gain_attn,
    in_beta_attn,
    in_gain_final,
    in_beta_final,
    layer_home,
    grad_home,
    sums_a,
    sums_b,
    m_qkv,
    turned_qkv,
    m_out,
    m_inner,
    m_outer,
    vectors,
    bias_inner,
    row,
    cot,
    info,
    qs,
    ks,
    vs,
    exps,
    recip,
    mixed,
    att,
    att_far,
    norm_a,
    inv_a,
    inv_f,
    mid,
    mid_low,
    acc,
    slope,
    raw_even,
    raw_odd,
    active,
    inner_sum,
    grad_h,
    grad_low,
    grad_att,
    grad_far,
    grad_qkv,
    turned,
    lefts,
    grads_turned,
    grad_scores,
    part,
    part_out,
    part_in,
    grad_out,
    layer_out,
    vec_a,
    pool_a,
    z_a,
    pool_b,
    z_b,
    w_sem,
    in_sem,
    tok_send,
    tok_recv,
    pass_send,
    pass_recv,
    info_sem,
    cot_send,
    cot_recv,
    att_send,
    att_recv,
    gat_send,
    gat_recv,
    lay_send,
    lay_recv,
    part_send,
    part_recv,
    grad_send,
    grad_recv,
    bias_send,
    bias_recv,
):
    rows, span, width = tokens.shape
    half_blocks = group // 2
    slots = span * group
    half = slots // 2
    head_width = width // HEADS
    side = width // 2
    pairs = side // LANES
    chunks = m_inner.shape[0]
    norm_steps = half // NORM_ROWS
    score_scale = head_width**-0.5
    slices = sums_a.shape[0]
    slice_width = width // slices

    seq = lax.axis_index("seq")
    z = lax.axis_index("head")
    core = lax.rem(seq, 2)
    base = seq - core
    partner = base + 1 - core
    z_half = z // half_blocks
    far = 1 - core

    def near_at(j):
        return pl.ds(pl.multiple_of(half + j * span, span), span)

    def far_at(j):
        return pl.ds(pl.multiple_of(j * span, span), span)

    def remote(src, dst, send_sem, recv_sem, at_seq, at_head):
        return pltpu.make_async_remote_copy(
            src_ref=src,
            dst_ref=dst,
            send_sem=send_sem,
            recv_sem=recv_sem,
            device_id=(at_seq, at_head),
            device_id_type=MESH,
        )

    barrier = pltpu.get_barrier_semaphore()

    def greet_z(step, carry):
        pl.semaphore_signal(
            barrier, inc=1, device_id=(seq, lax.rem(z + step, group)), device_id_type=MESH
        )
        return carry

    def greet_seq(step, carry):
        pl.semaphore_signal(
            barrier, inc=1, device_id=(lax.rem(seq + step, seq_size), z), device_id_type=MESH
        )
        return carry

    for step in range(group - 1, 0, -1):
        greet_z(step, 0)

    for r in range(half_blocks):
        other = core * half_blocks + r

        @pl.when(other != z)
        def _():
            pl.semaphore_signal(barrier, inc=1, device_id=(partner, other), device_id_type=MESH)

    lax.fori_loop(1, seq_size, greet_seq, 0)

    mine = pl.ds(pl.multiple_of(core * side, side), side)
    theirs = pl.ds(pl.multiple_of(far * side, side), side)
    for i, weight in enumerate((w_query, w_key, w_value)):
        pltpu.make_async_copy(
            weight.at[:, mine], m_qkv.at[:, i * side : (i + 1) * side], w_sem.at[0]
        ).start()
    for i, vector in enumerate(
        (
            in_bias_query,
            in_bias_value,
            in_bias_out,
            in_bias_outer,
            in_gain_attn,
            in_beta_attn,
            in_gain_final,
            in_beta_final,
        )
    ):
        pltpu.make_async_copy(vector, vectors.at[i], w_sem.at[4]).start()
    pltpu.make_async_copy(in_bias_inner, bias_inner, w_sem.at[5]).start()

    def loaded(target, i):
        pltpu.make_async_copy(target, target, w_sem.at[i]).wait()

    line = lax.broadcasted_iota(jnp.int32, (8, LANES), 0)
    for r in range(rows):
        first = doc_lengths[r, 0]
        second = first + doc_lengths[r, 1]
        third = second + doc_lengths[r, 2]
        ends = jnp.where(line == 0, first, jnp.where(line == 1, second, third))
        info[core, r] = jnp.where(line == 3, slots - pad_counts[r], ends)

    crossed = jnp.where(z_half == core, 0, group - 1)
    pl.semaphore_wait(barrier, crossed + seq_size - 1 + group - 1)

    early = (z >= half_blocks // 2) & (z < group - half_blocks // 2)

    def spread(index, source, target_ref, at, send_sem, recv_sem):
        r = jnp.where(core == 0, rows - 1 - index, index)
        target = core * rows + r

        @pl.when(target != z)
        def _():
            remote(
                source.at[r],
                target_ref.at[at],
                send_sem.at[r],
                recv_sem.at[z - z_half * half_blocks],
                base + z_half,
                target,
            ).start()

    def keep(source, target_ref, at, local_sem):
        @pl.when(core == z_half)
        def _():
            pltpu.make_async_copy(
                source.at[z - z_half * rows], target_ref.at[at], local_sem
            ).start()

    def spread_done(index, source, target_ref, at, send_sem, recv_sem):
        r = jnp.where(core == 0, rows - 1 - index, index)
        target = core * rows + r

        @pl.when(target != z)
        def _():
            remote(
                source.at[r],
                target_ref.at[at],
                send_sem.at[r],
                recv_sem.at[z - z_half * half_blocks],
                base + z_half,
                target,
            ).wait_send()

    def arrived(source, target_ref, at, block, send_sem, recv_sem, local_sem):
        j = block - core * half_blocks

        @pl.when(block != z)
        def _():
            remote(
                source.at[0],
                target_ref.at[at],
                send_sem.at[0],
                recv_sem.at[j],
                base + z_half,
                block,
            ).wait_recv()

        @pl.when(block == z)
        def _():
            pltpu.make_async_copy(source.at[0], target_ref.at[at], local_sem).wait()

    info_copy = remote(info.at[core], info.at[core], info_sem.at[0], info_sem.at[1], partner, z)
    info_copy.start()
    tok_at = near_at(z - z_half * half_blocks)
    cot_at = pl.ds(pl.multiple_of((z - z_half * half_blocks) * span, span), span)

    def send_tokens():
        for index in range(rows):
            spread(index, tokens, row, tok_at, tok_send, tok_recv)

    def tokens_sent():
        for index in range(rows):
            spread_done(index, tokens, row, tok_at, tok_send, tok_recv)

    def send_cotangents():
        for index in range(rows):
            spread(index, cotangent, cot, cot_at, cot_send, cot_recv)

    def cotangents_sent():
        for index in range(rows):
            spread_done(index, cotangent, cot, cot_at, cot_send, cot_recv)

    send_tokens()
    keep(tokens, row, tok_at, in_sem.at[0])
    keep(cotangent, cot, cot_at, in_sem.at[1])

    @pl.when(early)
    def _():
        send_cotangents()

    pltpu.make_async_copy(w_out.at[mine], m_out.at[0:side], w_sem.at[1]).start()
    pltpu.make_async_copy(w_out.at[theirs], m_out.at[side:width], w_sem.at[1]).start()
    for f in range(chunks):
        columns = slice(f * FF_CHUNK, (f + 1) * FF_CHUNK)
        pltpu.make_async_copy(w_inner.at[:, columns], m_inner.at[f], w_sem.at[2]).start()
    pltpu.make_async_copy(w_outer, m_outer, w_sem.at[3]).start()

    info_copy.wait_send()
    remote(info.at[far], info.at[far], info_sem.at[0], info_sem.at[1], partner, z).wait_recv()
    loaded(m_qkv, 0)
    loaded(vectors, 4)
    loaded(bias_inner, 5)
    bias_query = vectors[0, :, mine]
    bias_value = vectors[1, :, mine]

    lane = lax.broadcasted_iota(jnp.int32, (slots, LANES), 1)
    place = lax.broadcasted_iota(jnp.int32, (slots, LANES), 0)
    slot = jnp.where(place < half, far * half + place, core * half + place - half)
    ends = info[z_half, z - z_half * rows]
    doc = (slot >= ends[0:1]).astype(jnp.int32)
    for i in range(1, 4):
        doc = doc + (slot >= ends[i : i + 1]).astype(jnp.int32)
    doc_query = jnp.where(doc == lane, BIG, 0.0).astype(BF16)
    doc_key = jnp.where((doc != lane) & (lane < 5), -1.0, 0.0).astype(BF16)
    ones = jnp.ones((slots, LANES), BF16)

    def pass_on(j):
        return remote(
            row.at[near_at(j)], row.at[far_at(j)], pass_send.at[j], pass_recv.at[j], partner, z
        )

    def taken(which, step):
        local = lax.rem(z - z_half * half_blocks + step, half_blocks)
        beyond = jnp.where(z_half == 0, half_blocks - 1 - step, step)
        return jnp.where(which == z_half, local, beyond)

    def project(at):
        x = row[at, :]
        q = (dot(x, m_qkv[:, 0:side]) + bias_query) * score_scale
        k = dot(x, m_qkv[:, side : 2 * side])
        v = dot(x, m_qkv[:, 2 * side : 3 * side]) + bias_value
        for p in range(pairs):
            cut = slice(p * LANES, (p + 1) * LANES)
            qs[p, at, :] = q[:, cut].astype(BF16)
            if span % LANES == 0:
                turned[p, :, at] = q[:, cut].astype(BF16).T
            ks[p, at, :] = k[:, cut].astype(BF16)
            vs[p, at, :] = v[:, cut].astype(BF16)


    def project_step(i, carry):
        in_turn = core == z_half
        own = jnp.where(in_turn, i < half_blocks, (i >= 1) & (i <= half_blocks))
        passed = jnp.where(i == 0, 0, i - half_blocks)
        step = jnp.where(in_turn, lax.rem(i, half_blocks), jnp.where(own, i - 1, passed))
        j = taken(jnp.where(own, core, far), step)

        @pl.when(own)
        def _():
            block = core * half_blocks + j

            @pl.when((i == half_blocks) & jnp.logical_not(early))
            def _():
                send_cotangents()

            arrived(tokens, row, near_at(j), block, tok_send, tok_recv, in_sem.at[0])
            pass_on(j).start()

        @pl.when(jnp.logical_not(own))
        def _():
            pass_on(j).wait_recv()

            @pl.when(in_turn & (i == half_blocks) & jnp.logical_not(early))
            def _():
                send_cotangents()

        project(pl.ds(pl.multiple_of(jnp.where(own, half, 0) + j * span, span), span))
        return carry

    for i in range(0, 3 * side, 2 * LANES):
        turned_qkv[i : i + 2 * LANES, :] = m_qkv[:, i : i + 2 * LANES].T

    lax.fori_loop(0, group, project_step, 0)

    for i, target in enumerate((m_out, m_inner, m_outer)):
        loaded(target, 1 + i)

    lane_row = lax.broadcasted_iota(jnp.int32, (1, LANES), 1)
    head_mask = [
        (lane_row < head_width).astype(F32),
        (lane_row >= head_width).astype(F32),
    ]
    low_mask = [mask.astype(BF16) for mask in head_mask]
    near_rows = slice(half, slots)
    far_rows = slice(0, half)

    def score(unit, spot):
        head, at = unit
        p = head // 2
        left = jnp.concatenate([qs[p, at, :] * low_mask[head % 2], doc_query[at, :]], axis=1)
        keys = jnp.concatenate([ks[p], doc_key], axis=1)
        slope[spot, 0:half, :] = dot_nt(left, keys)

    def soften(unit, spot):
        head, at = unit
        scores = slope[spot, 0:half, :]
        exponent = jnp.exp(scores - jnp.max(scores, axis=-1, keepdims=True))
        exps[head, at, :] = exponent.astype(BF16)

    def mix(unit):
        head, at = unit
        both = dot(exps[head, at, :], jnp.concatenate([vs[head // 2], ones], axis=1))
        share = 1.0 / both[:, LANES:]
        return both[:, :LANES] * share * head_mask[head % 2], share * head_mask[head % 2]

    units = [(head, at) for at in (far_rows, near_rows) for head in range(2 * pairs)]
    spots = slope.shape[0]
    score(units[0], 0)
    for i in range(len(units) + 1):
        if i + 1 < len(units):
            score(units[i + 1], (i + 1) % spots)
        if i > 0:
            head, at = units[i - 1]
            if head % 2 == 0:
                held = mix(units[i - 1])
            else:
                total, shares = (a + b for a, b in zip(held, mix(units[i - 1])))
                p = head // 2
                mixed[p, at, :] = total
                recip[p, at, :] = shares
                att[p, at, :] = total.astype(BF16)
        if i < len(units):
            soften(units[i], i % spots)
        if i == 2 * pairs:
            att_copy = remote(
                att.at[:, far_rows], att_far, att_send.at[0], att_recv.at[0], partner, z
            )
            att_copy.start()

    def whole(source, target, send_sem, recv_sem):
        return remote(source, target, send_sem, recv_sem, partner, z)

    att_copy.wait()
    left = jnp.concatenate(
        [att[p, near_rows, :] for p in range(pairs)] + [att_far[p] for p in range(pairs)], axis=1
    )
    acc[...] = dot(left, m_out[...])
    def lines_of(step):
        return pl.ds(pl.multiple_of(step * NORM_ROWS, NORM_ROWS), NORM_ROWS)

    def norm_first(step, carry):
        at = lines_of(step)
        near = pl.ds(pl.multiple_of(half + step * NORM_ROWS, NORM_ROWS), NORM_ROWS)
        hidden = row[near, :].astype(F32) + acc[at, :] + vectors[2]
        norm, inv_std = normed(hidden)
        norm_a[at, :] = norm
        inv_a[at, :] = jnp.broadcast_to(inv_std, (NORM_ROWS, LANES))
        middle = norm * vectors[4] + vectors[5]
        mid[at, :] = middle
        mid_low[at, :] = middle.astype(BF16)
        return carry

    lax.fori_loop(0, norm_steps, norm_first, 0, unroll=True)

    def slope_at(f):
        return f // 2, slice(f % 2 * half, (f % 2 + 1) * half)

    def activate(f):
        columns = slice(f * FF_CHUNK, (f + 1) * FF_CHUNK)
        inner = raw[f % 2][...] + bias_inner[:, columns]
        scaled = inner * 0.7071067811865476
        cdf = 0.5 + 0.5 * lax.erf(scaled)
        which, lines = slope_at(f)
        slope[which, lines, :] = cdf + scaled * 0.5641895835477563 * jnp.exp2(
            scaled * scaled * -1.4426950408889634
        )
        active[:, columns] = (inner * cdf).astype(BF16)

    raw = (raw_even, raw_odd)
    raw_even[...] = dot(mid_low[...], m_inner[0])
    for f in range(chunks):
        if f + 1 < chunks:
            raw[(f + 1) % 2][...] = dot(mid_low[...], m_inner[f + 1])
        activate(f)
    for n in range(0, width, FEATURE_CHUNK):
        acc[:, n : n + FEATURE_CHUNK] = dot(active[...], m_outer[:, n : n + FEATURE_CHUNK])

    live_end = ends[3:4, 0:1]

    def live_at(step):
        place = lax.broadcasted_iota(jnp.int32, (NORM_ROWS, 1), 0) + core * half + step * NORM_ROWS
        return (place < live_end).astype(F32)

    def norm_last(step, carry):
        at = lines_of(step)
        norm, inv_std = normed(mid[at, :] + acc[at, :] + vectors[3])
        acc[at, :] = norm
        inv_f[at, :] = jnp.broadcast_to(inv_std, (NORM_ROWS, LANES))
        layer_out[at, :] = (live_at(step) * (norm * vectors[6] + vectors[7])).astype(BF16)
        return carry

    lax.fori_loop(0, norm_steps, norm_last, 0, unroll=True)

    def home_block(block, source, target_ref, send_sem, recv_sem, local_sem):
        j = block - core * half_blocks
        src = source.at[pl.ds(pl.multiple_of(j * span, span), span)]
        line_at = z - z_half * rows

        @pl.when(block != z)
        def _():
            remote(
                src,
                target_ref.at[line_at],
                send_sem.at[j],
                recv_sem.at[line_at],
                base + z_half,
                block,
            ).start()

        @pl.when(block == z)
        def _():
            pltpu.make_async_copy(src, target_ref.at[line_at], local_sem).start()

    def home_done(source, target_ref, send_sem, recv_sem, local_sem):
        for j in range(half_blocks):
            block = core * half_blocks + j
            src = source.at[j * span : (j + 1) * span]
            line_at = z - z_half * rows

            @pl.when(block != z)
            def _():
                remote(
                    src,
                    target_ref.at[line_at],
                    send_sem.at[j],
                    recv_sem.at[line_at],
                    base + z_half,
                    block,
                ).wait_send()

            @pl.when(block == z)
            def _():
                pltpu.make_async_copy(src, target_ref.at[line_at], local_sem).wait()

        for r in range(rows):
            target = core * rows + r

            @pl.when(target != z)
            def _():
                remote(
                    source.at[0:span],
                    target_ref.at[r],
                    send_sem.at[0],
                    recv_sem.at[r],
                    base + z_half,
                    target,
                ).wait_recv()

    for j in range(half_blocks):
        home_block(
            core * half_blocks + j, layer_out, layer_home, lay_send, lay_recv, in_sem.at[2]
        )
    if span % LANES != 0:
        for p in range(pairs):
            turned[p] = qs[p].T

    def cot_wait(j, carry):
        at = pl.ds(pl.multiple_of(j * span, span), span)
        arrived(cotangent, cot, at, core * half_blocks + j, cot_send, cot_recv, in_sem.at[1])
        return carry

    lax.fori_loop(0, half_blocks, cot_wait, 0)

    zero_sum = jnp.zeros((8, width), F32)

    def norm_last_back(step, carry):
        beta_sum, outer_sum = carry
        at = lines_of(step)
        grad_final = live_at(step) * cot[at, :].astype(F32)
        grad_hidden = norm_back(grad_final * vectors[6], acc[at, :], inv_f[at, 0:1])
        grad_h[at, :] = grad_hidden
        grad_low[at, :] = grad_hidden.astype(BF16)
        return beta_sum + fold_rows(grad_final), outer_sum + fold_rows(grad_hidden)

    sums = lax.fori_loop(0, norm_steps, norm_last_back, (zero_sum, zero_sum), unroll=True)
    beta_final_sum, outer_sum = sums

    for f in range(chunks):
        which, lines = slope_at(f)
        columns = slice(f * FF_CHUNK, (f + 1) * FF_CHUNK)
        grad_active = dot_nt(grad_low[...], m_outer[columns, :])
        grad_inner = (grad_active * slope[which, lines, :]).astype(BF16)
        active[:, columns] = grad_inner
        inner_sum[f] = fold_rows(grad_inner.astype(F32))
    for n in range(0, width, FEATURE_CHUNK):
        total = None
        for f in range(chunks):
            term = dot_nt(
                active[:, f * FF_CHUNK : (f + 1) * FF_CHUNK], m_inner[f, n : n + FEATURE_CHUNK, :]
            )
            total = term if total is None else total + term
        acc[:, n : n + FEATURE_CHUNK] = total
    def norm_first_back(step, carry):
        beta_sum, out_sum = carry
        at = lines_of(step)
        grad_middle = grad_h[at, :] + acc[at, :]
        grad_hidden = norm_back(grad_middle * vectors[4], norm_a[at, :], inv_a[at, 0:1])
        grad_h[at, :] = grad_hidden
        grad_low[at, :] = grad_hidden.astype(BF16)
        return beta_sum + fold_rows(grad_middle), out_sum + fold_rows(grad_hidden)

    beta_attn_sum, out_sum = lax.fori_loop(
        0, norm_steps, norm_first_back, (zero_sum, zero_sum), unroll=True
    )

    def sum_up():
        per_line = width // FF_CHUNK
        for f in range(chunks):
            line_at = 4 + f // per_line
            column = f % per_line * FF_CHUNK
            vec_a[line_at : line_at + 1, column : column + FF_CHUNK] = jnp.sum(
                inner_sum[f], axis=0, keepdims=True
            )
        for i, lines in enumerate((out_sum, outer_sum, beta_attn_sum, beta_final_sum)):
            vec_a[i : i + 1, :] = jnp.sum(lines, axis=0, keepdims=True)
        pool_a[seq] = vec_a[:, pl.ds(pl.multiple_of(own_slice * slice_width, LANES), slice_width)]

    def send_all(start, size, here, make):
        def go(step, carry):
            make(start + lax.rem(here - start + step, size)).start()
            return carry

        lax.fori_loop(1, size, go, 0)

    def wait_all(pool, size, make):
        everything = pool.at[pl.ds(0, size - 1)]
        copy = make(everything, everything)
        copy.wait()

    def bias_copy(i, peer_seq, peer_z):
        return lambda source, target: remote(
            source, target, bias_send.at[i], bias_recv.at[i], peer_seq, peer_z
        )

    def plane_a(peer):
        piece = pl.ds(pl.multiple_of(lax.rem(peer, slices) * slice_width, LANES), slice_width)
        return bias_copy(0, peer, z)(vec_a.at[:, piece], pool_a.at[seq])

    def column_a(peer):
        return bias_copy(1, seq, peer)(z_a.at[z], z_a.at[z])

    own_slice = lax.rem(seq, slices)

    def gather_a(peer):
        return bias_copy(2, peer, z)(sums_a.at[own_slice], sums_a.at[own_slice])

    def column_b(peer):
        return bias_copy(3, seq, peer)(z_b.at[z], z_b.at[z])

    def plane_b(peer):
        return bias_copy(4, peer, z)(pool_b.at[seq], pool_b.at[seq])

    def total_of(pool, places):
        total = pool[places[0]]
        for place in places[1:]:
            total = total + pool[place]
        return total

    def gat_copy(p):
        return remote(
            grad_far.at[p], grad_att.at[p, far_rows], gat_send.at[0], gat_recv.at[0], partner, z
        )

    lines = dot_nt(grad_low[...], m_out[side:width, :])
    for p in range(pairs):
        grad_far[p] = lines[:, p * LANES : (p + 1) * LANES].astype(BF16)
        gat_copy(p).start()
    sum_up()
    send_all(0, seq_size, seq, plane_a)
    lines = dot_nt(grad_low[...], m_out[0:side, :])
    for p in range(pairs):
        grad_att[p, near_rows, :] = lines[:, p * LANES : (p + 1) * LANES].astype(BF16)

    def prepare(p, at):
        scaled = (grad_att[p, at, :].astype(F32) * recip[p, at, :]).astype(BF16)
        product = scaled.astype(F32) * mixed[p, at, :]
        half_lane = lane[at, :]
        for i in range(2):
            delta = jnp.sum(product * head_mask[i], axis=-1, keepdims=True)
            high = delta.astype(BF16).astype(F32)
            extra = jnp.where(half_lane == 0, -high, jnp.where(half_lane == 1, high - delta, 0.0))
            grads = scaled * low_mask[i]
            lefts[2 * p + i, at, :] = jnp.concatenate([grads, extra.astype(BF16)], axis=1)
        grads_turned[p, :, at] = scaled.T

    def score_grads(head, at):
        values = jnp.concatenate([vs[head // 2], ones], axis=1)
        grads = exps[head, at, :].astype(F32) * dot_nt(lefts[head, at, :], values)
        grad_scores[head, at, :] = grads.astype(BF16)
        return fold_rows(grads)

    quarter = slots // 4

    def half_of(turn):
        return 1 - z_half if turn < 2 else z_half

    def start_of(turn):
        return jnp.where(core == half_of(turn), half, 0) + turn % 2 * quarter

    def attend_back(p, turn):
        part_of = pl.ds(pl.multiple_of(start_of(turn), quarter), quarter)
        dq = None
        dk = []
        dv = []
        for i in range(2):
            cut = slice(i * head_width, (i + 1) * head_width)
            head = 2 * p + i
            term = dot(grad_scores[head, part_of, :], ks[p] * low_mask[i])
            dq = term if dq is None else dq + term
            dk.append(dot(turned[p, cut, :], grad_scores[head, :, part_of]))
            dv.append(dot(grads_turned[p, cut, :], exps[head, :, part_of]))
        dq = (dq * score_scale).astype(BF16)
        dk = jnp.concatenate(dk, axis=0).astype(BF16).T
        dv = jnp.concatenate(dv, axis=0).astype(BF16).T
        for i, block in enumerate((dq, dk, dv)):
            grad_qkv[turn, :, i * side + p * LANES : i * side + (p + 1) * LANES] = block

    def score_grads_of(at):
        sums = []
        prepare(0, at)
        for p in range(pairs):
            if p + 1 < pairs:
                prepare(p + 1, at)
            sums += [score_grads(2 * p, at), score_grads(2 * p + 1, at)]
        return sums

    near_sums = score_grads_of(near_rows)
    whole(grad_far, grad_far, gat_send.at[0], gat_recv.at[0]).wait()
    far_sums = score_grads_of(far_rows)
    for p in range(pairs):
        rows_of_pair = []
        for head in (2 * p, 2 * p + 1):
            sums = near_sums[head] + far_sums[head]
            high = sums.astype(BF16)
            rows_of_pair += [high, (sums - high.astype(F32)).astype(BF16)]
        query_sum = dot(jnp.concatenate(rows_of_pair, axis=0), ks[p])
        query_sum = query_sum[0:16] * head_mask[0] + query_sum[16:32] * head_mask[1]
        z_b[z, p : p + 1, :] = jnp.sum(query_sum, axis=0, keepdims=True) * score_scale
        z_b[z, pairs + p : pairs + p + 1, :] = jnp.sum(
            fold_rows(grad_att[p].astype(F32)), axis=0, keepdims=True
        )
    send_all(0, group, z, column_b)
    for p in range(pairs):
        attend_back(p, 0)

    home_line = z - z_half * rows

    def part_copy(turn):
        return remote(
            part_out.at[turn], part_in.at[turn], part_send.at[turn], part_recv.at[turn], partner, z
        )

    def token_grad(turn, which):
        own = core == half_of(turn)
        columns = pl.ds(pl.multiple_of(which * side, side), side)
        near = slice(turn % 2 * quarter, (turn % 2 + 1) * quarter)
        term = dot(grad_qkv[turn], turned_qkv[:, columns])
        return term + jnp.where(own, 1.0, 0.0) * grad_h[near, columns]

    def finish(turn):
        part_copy(turn).wait_recv()
        at = slice(turn * quarter, (turn + 1) * quarter)
        grad_out[at, :] = (part[turn % 2] + part_in[turn].astype(F32)).astype(BF16)
        for j in range(quarter // span):
            block = half_of(turn) * half_blocks + turn % 2 * (quarter // span) + j
            source = grad_out.at[turn * quarter + j * span : turn * quarter + (j + 1) * span]
            target_ref = grad_home.at[home_line, core]
            stays = (block == z) & (core == z_half)

            @pl.when(jnp.logical_not(stays))
            def _():
                remote(
                    source,
                    target_ref,
                    grad_send.at[0],
                    grad_recv.at[home_line],
                    base + z_half,
                    block,
                ).start()

            @pl.when(stays)
            def _():
                pltpu.make_async_copy(source, target_ref, in_sem.at[3]).start()

    def grads_done():
        @pl.when(core == z_half)
        def _():
            one = grad_out.at[0:span]
            rest = grad_out.at[span:slots]
            pltpu.make_async_copy(one, one, in_sem.at[3]).wait()
            whole(rest, rest, grad_send.at[0], grad_recv.at[0]).wait_send()

        @pl.when(core != z_half)
        def _():
            whole(grad_out, grad_out, grad_send.at[0], grad_recv.at[0]).wait_send()

        for r in range(rows):
            everything = grad_home.at[r]

            @pl.when(core * rows + r != z)
            def _():
                whole(everything, everything, grad_send.at[0], grad_recv.at[r]).wait_recv()

            @pl.when(core * rows + r == z)
            def _():
                one = everything.at[0]
                whole(one, one, grad_send.at[0], grad_recv.at[r]).wait_recv()

    for turn in range(4):
        if turn > 0:
            for p in range(pairs):
                attend_back(p, turn)
            finish(turn - 1)
        part_out[turn] = token_grad(turn, far).astype(BF16)
        part_copy(turn).start()
        part[turn % 2] = token_grad(turn, core)
        if turn == 0:
            wait_all(pool_a, seq_size, bias_copy(0, partner, z))
            z_a[z] = total_of(pool_a, range(seq_size))
            send_all(0, group, z, column_a)
    finish(3)
    wait_all(z_a, group, bias_copy(1, partner, z))
    sums_a[own_slice] = total_of(z_a, range(group))
    send_all(seq - own_slice, slices, seq, gather_a)
    wait_all(z_b, group, bias_copy(3, partner, z))
    pool_b[seq] = total_of(z_b, range(group))
    send_all(0, seq_size, seq, plane_b)

    for turn in range(4):
        part_copy(turn).wait_send()
    wait_all(sums_a, slices, bias_copy(2, partner, z))
    wait_all(pool_b, seq_size, bias_copy(4, partner, z))
    for i in range(2):
        sums_b[i] = total_of(pool_b, range(i, seq_size, 2))
    tokens_sent()
    cotangents_sent()

    def pass_wait(j, carry):
        pass_on(j).wait_send()
        return carry

    lax.fori_loop(0, half_blocks, pass_wait, 0)
    home_done(layer_out, layer_home, lay_send, lay_recv, in_sem.at[2])
    grads_done()


def finish_kernel(
    layer,
    grad,
    sums_a,
    sums_b,
    layer_out,
    input_grad,
    grad_bias_query,
    grad_bias_value,
    grad_bias_out,
    grad_bias_inner,
    grad_bias_outer,
    grad_beta_attn,
    grad_beta_final,
    wide,
    lines,
    inner_line,
    sems,
):
    rows, span, width = layer.shape
    slices, _, slice_width = sums_a.shape
    copies = [pltpu.make_async_copy(layer, layer_out, sems.at[0])]
    copies[0].start()
    for r in range(rows):
        for c in range(2):
            wide[r, :, c * width // 2 : (c + 1) * width // 2] = grad[r, c].astype(F32)
        copies.append(pltpu.make_async_copy(wide.at[r], input_grad.at[r], sems.at[1 + r]))
        copies[-1].start()
    pairs = sums_b.shape[1] // 2
    for i in range(2):
        for p in range(pairs):
            column = (i * pairs + p) * LANES
            lines[0, :, column : column + LANES] = sums_b[i, p : p + 1, :]
            lines[1, :, column : column + LANES] = sums_b[i, pairs + p : pairs + p + 1, :]
    for j in range(slices):
        column = j * slice_width
        for i in range(4):
            lines[2 + i, :, column : column + slice_width] = sums_a[j, i : i + 1, :]
            inner_line[:, i * width + column : i * width + column + slice_width] = sums_a[
                j, 4 + i : 5 + i, :
            ]
    targets = (
        grad_bias_query,
        grad_bias_value,
        grad_bias_out,
        grad_bias_outer,
        grad_beta_attn,
        grad_beta_final,
    )
    for i, target in enumerate(targets):
        copies.append(pltpu.make_async_copy(lines.at[i], target, sems.at[1 + rows + i]))
        copies[-1].start()
    copies.append(pltpu.make_async_copy(inner_line, grad_bias_inner, sems.at[7 + rows]))
    copies[-1].start()
    for copy in copies:
        copy.wait()


def per_device(
    seq_size,
    group,
    tokens,
    doc_lengths,
    pad_counts,
    w_query,
    w_key,
    w_value,
    w_out,
    w_inner,
    w_outer,
    bias_query,
    bias_value,
    bias_out,
    bias_inner,
    bias_outer,
    gain_attn,
    beta_attn,
    gain_final,
    beta_final,
    cotangent,
):
    rows, span, width = tokens.shape
    hidden = w_inner.shape[1]
    slots = span * group
    half = slots // 2
    half_blocks = group // 2
    side = width // 2
    pairs = side // LANES
    chunks = hidden // FF_CHUNK
    slices = min(8, seq_size)
    quarter = slots // 4
    slice_width = width // slices
    if rows * 2 != group or pairs != 4 or hidden != 4 * width or slots != FF_CHUNK or quarter % span != 0:
        raise ValueError("unsupported sizes")

    any_space = pl.BlockSpec(memory_space=pl.ANY)
    vmem = pl.BlockSpec(memory_space=pltpu.VMEM)
    smem = pl.BlockSpec(memory_space=pltpu.SMEM)
    dma = pltpu.SemaphoreType.DMA
    scratch = [
        pltpu.VMEM((width, 3 * side), BF16),
        pltpu.VMEM((3 * side, width), BF16),
        pltpu.VMEM((width, width), BF16),
        pltpu.VMEM((chunks, width, FF_CHUNK), BF16),
        pltpu.VMEM((hidden, width), BF16),
        pltpu.VMEM((8, 1, width), F32),
        pltpu.VMEM((1, hidden), F32),
        pltpu.VMEM((slots, width), BF16),
        pltpu.VMEM((half, width), BF16),
        pltpu.VMEM((2, rows, 8, LANES), jnp.int32),
        pltpu.VMEM((pairs, slots, LANES), BF16),
        pltpu.VMEM((pairs, slots, LANES), BF16),
        pltpu.VMEM((pairs, slots, LANES), BF16),
        pltpu.VMEM((2 * pairs, slots, slots), BF16),
        pltpu.VMEM((pairs, slots, LANES), F32),
        pltpu.VMEM((pairs, slots, LANES), F32),
        pltpu.VMEM((pairs, slots, LANES), BF16),
        pltpu.VMEM((pairs, half, LANES), BF16),
        pltpu.VMEM((half, width), F32),
        pltpu.VMEM((half, LANES), F32),
        pltpu.VMEM((half, LANES), F32),
        pltpu.VMEM((half, width), F32),
        pltpu.VMEM((half, width), BF16),
        pltpu.VMEM((half, width), F32),
        pltpu.VMEM((chunks // 2, slots, slots), F32),
        pltpu.VMEM((half, FF_CHUNK), F32),
        pltpu.VMEM((half, FF_CHUNK), F32),
        pltpu.VMEM((half, hidden), BF16),
        pltpu.VMEM((chunks, 8, FF_CHUNK), F32),
        pltpu.VMEM((half, width), F32),
        pltpu.VMEM((half, width), BF16),
        pltpu.VMEM((pairs, slots, LANES), BF16),
        pltpu.VMEM((pairs, half, LANES), BF16),
        pltpu.VMEM((4, quarter, 3 * side), BF16),
        pltpu.VMEM((pairs, LANES, slots), BF16),
        pltpu.VMEM((2 * pairs, slots, 2 * LANES), BF16),
        pltpu.VMEM((pairs, LANES, slots), BF16),
        pltpu.VMEM((2 * pairs, slots, slots), BF16),
        pltpu.VMEM((2, quarter, side), F32),
        pltpu.VMEM((4, quarter, side), BF16),
        pltpu.VMEM((4, quarter, side), BF16),
        pltpu.VMEM((slots, side), BF16),
        pltpu.VMEM((half, width), BF16),
        pltpu.VMEM((8, width), F32),
        pltpu.VMEM((seq_size, 8, slice_width), F32),
        pltpu.VMEM((group, 8, slice_width), F32),
        pltpu.VMEM((seq_size, 8, LANES), F32),
        pltpu.VMEM((group, 8, LANES), F32),
        dma((6,)),
        dma((4,)),
        dma((rows,)),
        dma((half_blocks,)),
        dma((half_blocks,)),
        dma((half_blocks,)),
        dma((2,)),
        dma((rows,)),
        dma((half_blocks,)),
        dma((1,)),
        dma((1,)),
        dma((1,)),
        dma((1,)),
        dma((half_blocks,)),
        dma((rows,)),
        dma((4,)),
        dma((4,)),
        dma((1,)),
        dma((rows,)),
        dma((5,)),
        dma((5,)),
    ]
    vectors = (
        bias_query,
        bias_value,
        bias_out,
        bias_inner,
        bias_outer,
        gain_attn,
        beta_attn,
        gain_final,
        beta_final,
    )
    layer_home, grad_home, sums_a, sums_b = pl.pallas_call(
        functools.partial(kernel, seq_size, group),
        out_shape=(
            pltpu.VMEM(tokens.shape, BF16),
            pltpu.VMEM((rows, 2, span, side), BF16),
            pltpu.VMEM((slices, 8, slice_width), F32),
            pltpu.VMEM((2, 8, LANES), F32),
        ),
        in_specs=[any_space] * 2 + [smem] * 2 + [any_space] * (6 + len(vectors)),
        out_specs=(vmem,) * 4,
        scratch_shapes=scratch,
        compiler_params=pltpu.CompilerParams(
            collective_id=0, has_side_effects=True, vmem_limit_bytes=58 * 2**20
        ),
    )(
        tokens,
        cotangent,
        doc_lengths,
        pad_counts,
        w_query,
        w_key,
        w_value,
        w_out,
        w_inner,
        w_outer,
        *[vector.reshape(1, -1) for vector in vectors],
    )
    line = jax.ShapeDtypeStruct((1, width), F32)
    results = pl.pallas_call(
        finish_kernel,
        out_shape=(
            jax.ShapeDtypeStruct(tokens.shape, BF16),
            jax.ShapeDtypeStruct(tokens.shape, F32),
            line,
            line,
            line,
            jax.ShapeDtypeStruct((1, hidden), F32),
            line,
            line,
            line,
        ),
        in_specs=[vmem] * 4,
        out_specs=(any_space,) * 9,
        scratch_shapes=[
            pltpu.VMEM(tokens.shape, F32),
            pltpu.VMEM((6, 1, width), F32),
            pltpu.VMEM((1, hidden), F32),
            dma((8 + rows,)),
        ],
        compiler_params=pltpu.CompilerParams(vmem_limit_bytes=32 * 2**20),
    )(layer_home, grad_home, sums_a, sums_b)
    return tuple(results[:2]) + tuple(vector.reshape(-1) for vector in results[2:])


def solution(mesh):
    split = P("seq", "head", None)
    placed = (split, P("seq", None), P("seq")) + (P(),) * 15 + (split,)
    return jax.shard_map(
        functools.partial(per_device, mesh.shape["seq"], mesh.shape["head"]),
        mesh=mesh,
        in_specs=placed,
        out_specs=(split, split) + (P(),) * 7,
        check_vma=False,
    )
```

```python
import functools

import jax
import jax.numpy as jnp
from jax import lax
from jax.experimental import pallas as pl
from jax.experimental.pallas import tpu as pltpu
from jax.sharding import PartitionSpec as P

HEADS = 16
LANES = 128
EPS = 1e-06
BIG = 2.0**30
FF_CHUNK = 512
FEATURE_CHUNK = 512
NORM_ROWS = 32
MESH = pl.DeviceIdType.MESH
F32 = jnp.float32
BF16 = jnp.bfloat16


def dot(left, right):
    return lax.dot_general(left, right, (((1,), (0,)), ((), ())), preferred_element_type=F32)


def dot_nt(left, right):
    return lax.dot_general(left, right, (((1,), (1,)), ((), ())), preferred_element_type=F32)


def dot_tn(left, right):
    return lax.dot_general(left, right, (((0,), (0,)), ((), ())), preferred_element_type=F32)


def normed(hidden):
    row_mean = jnp.mean(hidden, axis=-1, keepdims=True)
    centred = hidden - row_mean
    inv_std = lax.rsqrt(jnp.mean(centred * centred, axis=-1, keepdims=True) + EPS)
    return centred * inv_std, inv_std


def norm_back(gradient, norm, inv_std):
    return inv_std * (
        gradient
        - jnp.mean(gradient, axis=-1, keepdims=True)
        - norm * jnp.mean(gradient * norm, axis=-1, keepdims=True)
    )


def fold_rows(block):
    total = block[0:8]
    for start in range(8, block.shape[0], 8):
        total = total + block[start : start + 8]
    return total


def kernel(
    seq_size,
    group,
    tokens,
    cotangent,
    doc_lengths,
    pad_counts,
    w_query,
    w_key,
    w_value,
    w_out,
    w_inner,
    w_outer,
    in_bias_query,
    in_bias_value,
    in_bias_out,
    in_bias_inner,
    in_bias_outer,
    in_gain_attn,
    in_beta_attn,
    in_gain_final,
    in_beta_final,
    layer_home,
    grad_home,
    sums_a,
    sums_b,
    m_qkv,
    turned_qkv,
    m_out,
    m_inner,
    m_outer,
    vectors,
    bias_inner,
    row,
    cot,
    info,
    qs,
    ks,
    vs,
    exps,
    recip,
    mixed,
    att,
    att_far,
    norm_a,
    inv_a,
    inv_f,
    mid,
    mid_low,
    acc,
    slope,
    raw_even,
    raw_odd,
    active,
    inner_sum,
    grad_h,
    grad_low,
    grad_att,
    grad_far,
    grad_qkv,
    turned,
    lefts,
    grads_turned,
    grad_scores,
    score_sums,
    part,
    part_out,
    part_in,
    grad_out,
    layer_out,
    vec_a,
    pool_a,
    z_a,
    pool_b,
    z_b,
    w_sem,
    in_sem,
    tok_send,
    tok_recv,
    pass_send,
    pass_recv,
    info_sem,
    cot_send,
    cot_recv,
    att_send,
    att_recv,
    gat_send,
    gat_recv,
    lay_send,
    lay_recv,
    part_send,
    part_recv,
    grad_send,
    grad_recv,
    bias_send,
    bias_recv,
):
    rows, span, width = tokens.shape
    half_blocks = group // 2
    slots = span * group
    half = slots // 2
    head_width = width // HEADS
    side = width // 2
    pairs = side // LANES
    chunks = m_inner.shape[0]
    norm_steps = half // NORM_ROWS
    score_scale = head_width**-0.5
    slices = sums_a.shape[0]
    slice_width = width // slices

    seq = lax.axis_index("seq")
    z = lax.axis_index("head")
    core = lax.rem(seq, 2)
    base = seq - core
    partner = base + 1 - core
    z_half = z // half_blocks
    far = 1 - core

    def near_at(j):
        return pl.ds(pl.multiple_of(half + j * span, span), span)

    def far_at(j):
        return pl.ds(pl.multiple_of(j * span, span), span)

    def remote(src, dst, send_sem, recv_sem, at_seq, at_head):
        return pltpu.make_async_remote_copy(
            src_ref=src,
            dst_ref=dst,
            send_sem=send_sem,
            recv_sem=recv_sem,
            device_id=(at_seq, at_head),
            device_id_type=MESH,
        )

    barrier = pltpu.get_barrier_semaphore()

    def greet_z(step, carry):
        pl.semaphore_signal(
            barrier, inc=1, device_id=(seq, lax.rem(z + step, group)), device_id_type=MESH
        )
        return carry

    def greet_seq(step, carry):
        pl.semaphore_signal(
            barrier, inc=1, device_id=(lax.rem(seq + step, seq_size), z), device_id_type=MESH
        )
        return carry

    for step in range(group - 1, 0, -1):
        greet_z(step, 0)

    for r in range(half_blocks):
        other = core * half_blocks + r

        @pl.when(other != z)
        def _():
            pl.semaphore_signal(barrier, inc=1, device_id=(partner, other), device_id_type=MESH)

    lax.fori_loop(1, seq_size, greet_seq, 0)

    mine = pl.ds(pl.multiple_of(core * side, side), side)
    theirs = pl.ds(pl.multiple_of(far * side, side), side)
    for i, weight in enumerate((w_query, w_key, w_value)):
        pltpu.make_async_copy(
            weight.at[:, mine], m_qkv.at[:, i * side : (i + 1) * side], w_sem.at[0]
        ).start()
    for i, vector in enumerate(
        (
            in_bias_query,
            in_bias_value,
            in_bias_out,
            in_bias_outer,
            in_gain_attn,
            in_beta_attn,
            in_gain_final,
            in_beta_final,
        )
    ):
        pltpu.make_async_copy(vector, vectors.at[i], w_sem.at[4]).start()
    pltpu.make_async_copy(in_bias_inner, bias_inner, w_sem.at[5]).start()

    def loaded(target, i):
        pltpu.make_async_copy(target, target, w_sem.at[i]).wait()

    line = lax.broadcasted_iota(jnp.int32, (8, LANES), 0)
    for r in range(rows):
        first = doc_lengths[r, 0]
        second = first + doc_lengths[r, 1]
        third = second + doc_lengths[r, 2]
        ends = jnp.where(line == 0, first, jnp.where(line == 1, second, third))
        info[core, r] = jnp.where(line == 3, slots - pad_counts[r], ends)

    crossed = jnp.where(z_half == core, 0, group - 1)
    pl.semaphore_wait(barrier, crossed + seq_size - 1 + group - 1)

    early = (z >= half_blocks // 2) & (z < group - half_blocks // 2)

    def spread(index, source, target_ref, at, send_sem, recv_sem):
        r = jnp.where(core == 0, rows - 1 - index, index)
        target = core * rows + r

        @pl.when(target != z)
        def _():
            remote(
                source.at[r],
                target_ref.at[at],
                send_sem.at[r],
                recv_sem.at[z - z_half * half_blocks],
                base + z_half,
                target,
            ).start()

    def keep(source, target_ref, at, local_sem):
        @pl.when(core == z_half)
        def _():
            pltpu.make_async_copy(
                source.at[z - z_half * rows], target_ref.at[at], local_sem
            ).start()

    def spread_done(index, source, target_ref, at, send_sem, recv_sem):
        r = jnp.where(core == 0, rows - 1 - index, index)
        target = core * rows + r

        @pl.when(target != z)
        def _():
            remote(
                source.at[r],
                target_ref.at[at],
                send_sem.at[r],
                recv_sem.at[z - z_half * half_blocks],
                base + z_half,
                target,
            ).wait_send()

    def arrived(source, target_ref, at, block, send_sem, recv_sem, local_sem):
        j = block - core * half_blocks

        @pl.when(block != z)
        def _():
            remote(
                source.at[0],
                target_ref.at[at],
                send_sem.at[0],
                recv_sem.at[j],
                base + z_half,
                block,
            ).wait_recv()

        @pl.when(block == z)
        def _():
            pltpu.make_async_copy(source.at[0], target_ref.at[at], local_sem).wait()

    info_copy = remote(info.at[core], info.at[core], info_sem.at[0], info_sem.at[1], partner, z)
    info_copy.start()
    tok_at = near_at(z - z_half * half_blocks)
    cot_at = pl.ds(pl.multiple_of((z - z_half * half_blocks) * span, span), span)

    gives_way = jnp.logical_not(early) & (core == z_half)
    goes_far = jnp.logical_not(early) & (core != z_half)

    def send_tokens():
        for index in range(rows):
            spread(index, tokens, row, tok_at, tok_send, tok_recv)

    def tokens_sent():
        for index in range(rows):
            spread_done(index, tokens, row, tok_at, tok_send, tok_recv)

    def send_cotangents():
        for index in range(rows):
            spread(index, cotangent, cot, cot_at, cot_send, cot_recv)

    def cotangents_sent():
        for index in range(rows):
            spread_done(index, cotangent, cot, cot_at, cot_send, cot_recv)

    @pl.when(jnp.logical_not(goes_far))
    def _():
        send_tokens()

    keep(tokens, row, tok_at, in_sem.at[0])
    keep(cotangent, cot, cot_at, in_sem.at[1])

    @pl.when(early)
    def _():
        send_cotangents()

    pltpu.make_async_copy(w_out.at[mine], m_out.at[0:side], w_sem.at[1]).start()
    pltpu.make_async_copy(w_out.at[theirs], m_out.at[side:width], w_sem.at[1]).start()
    for f in range(chunks):
        columns = slice(f * FF_CHUNK, (f + 1) * FF_CHUNK)
        pltpu.make_async_copy(w_inner.at[:, columns], m_inner.at[f], w_sem.at[2]).start()
    pltpu.make_async_copy(w_outer, m_outer, w_sem.at[3]).start()

    info_copy.wait_send()
    remote(info.at[far], info.at[far], info_sem.at[0], info_sem.at[1], partner, z).wait_recv()
    loaded(m_qkv, 0)
    loaded(vectors, 4)
    loaded(bias_inner, 5)
    bias_query = vectors[0, :, mine]
    bias_value = vectors[1, :, mine]

    lane = lax.broadcasted_iota(jnp.int32, (slots, LANES), 1)
    place = lax.broadcasted_iota(jnp.int32, (slots, LANES), 0)
    slot = jnp.where(place < half, far * half + place, core * half + place - half)
    ends = info[z_half, z - z_half * rows]
    doc = (slot >= ends[0:1]).astype(jnp.int32)
    for i in range(1, 4):
        doc = doc + (slot >= ends[i : i + 1]).astype(jnp.int32)
    doc_query = jnp.where(doc == lane, BIG, 0.0).astype(BF16)
    doc_key = jnp.where((doc != lane) & (lane < 5), -1.0, 0.0).astype(BF16)
    ones = jnp.ones((slots, LANES), BF16)

    def pass_on(j):
        return remote(
            row.at[near_at(j)], row.at[far_at(j)], pass_send.at[j], pass_recv.at[j], partner, z
        )

    def taken(which, step):
        local = lax.rem(z - z_half * half_blocks + step, half_blocks)
        beyond = jnp.where(z_half == 0, half_blocks - 1 - step, step)
        return jnp.where(which == z_half, local, beyond)

    def project(at):
        x = row[at, :]
        q = (dot(x, m_qkv[:, 0:side]) + bias_query) * score_scale
        k = dot(x, m_qkv[:, side : 2 * side])
        v = dot(x, m_qkv[:, 2 * side : 3 * side]) + bias_value
        for p in range(pairs):
            cut = slice(p * LANES, (p + 1) * LANES)
            qs[p, at, :] = q[:, cut].astype(BF16)
            if span % LANES == 0:
                turned[p, :, at] = q[:, cut].astype(BF16).T
            ks[p, at, :] = k[:, cut].astype(BF16)
            vs[p, at, :] = v[:, cut].astype(BF16)


    def project_step(i, carry):
        in_turn = core == z_half
        own = jnp.where(in_turn, i < half_blocks, (i >= 1) & (i <= half_blocks))
        passed = jnp.where(i == 0, 0, i - half_blocks)
        step = jnp.where(in_turn, lax.rem(i, half_blocks), jnp.where(own, i - 1, passed))
        j = taken(jnp.where(own, core, far), step)

        @pl.when(own)
        def _():
            block = core * half_blocks + j

            @pl.when((i == half_blocks) & jnp.logical_not(early))
            def _():
                send_cotangents()

            arrived(tokens, row, near_at(j), block, tok_send, tok_recv, in_sem.at[0])
            pass_on(j).start()

        @pl.when(jnp.logical_not(own))
        def _():
            pass_on(j).wait_recv()

            @pl.when(in_turn & (i == half_blocks) & jnp.logical_not(early))
            def _():
                send_cotangents()

        project(pl.ds(pl.multiple_of(jnp.where(own, half, 0) + j * span, span), span))
        return carry

    for i in range(0, 3 * side, 2 * LANES):
        turned_qkv[i : i + 2 * LANES, :] = m_qkv[:, i : i + 2 * LANES].T

    @pl.when(goes_far)
    def _():
        send_tokens()

    lax.fori_loop(0, group, project_step, 0)

    for i, target in enumerate((m_out, m_inner, m_outer)):
        loaded(target, 1 + i)

    lane_row = lax.broadcasted_iota(jnp.int32, (1, LANES), 1)
    head_mask = [
        (lane_row < head_width).astype(F32),
        (lane_row >= head_width).astype(F32),
    ]
    low_mask = [mask.astype(BF16) for mask in head_mask]
    near_rows = slice(half, slots)
    far_rows = slice(0, half)

    def score(unit, spot):
        head, at = unit
        p = head // 2
        left = jnp.concatenate([qs[p, at, :] * low_mask[head % 2], doc_query[at, :]], axis=1)
        keys = jnp.concatenate([ks[p], doc_key], axis=1)
        slope[spot, 0:half, :] = dot_nt(left, keys)

    def soften(unit, spot):
        head, at = unit
        scores = slope[spot, 0:half, :]
        exponent = jnp.exp(scores - jnp.max(scores, axis=-1, keepdims=True))
        exps[head, at, :] = exponent.astype(BF16)

    def mix(unit):
        head, at = unit
        both = dot(exps[head, at, :], jnp.concatenate([vs[head // 2], ones], axis=1))
        share = 1.0 / both[:, LANES:]
        return both[:, :LANES] * share * head_mask[head % 2], share * head_mask[head % 2]

    units = [(head, at) for at in (far_rows, near_rows) for head in range(2 * pairs)]
    spots = slope.shape[0]
    score(units[0], 0)
    for i in range(len(units) + 1):
        if i + 1 < len(units):
            score(units[i + 1], (i + 1) % spots)
        if i > 0:
            head, at = units[i - 1]
            if head % 2 == 0:
                held = mix(units[i - 1])
            else:
                total, shares = (a + b for a, b in zip(held, mix(units[i - 1])))
                p = head // 2
                mixed[p, at, :] = total
                recip[p, at, :] = shares
                att[p, at, :] = total.astype(BF16)
        if i < len(units):
            soften(units[i], i % spots)
        if i == 2 * pairs:
            att_copy = remote(
                att.at[:, far_rows], att_far, att_send.at[0], att_recv.at[0], partner, z
            )
            att_copy.start()

    def whole(source, target, send_sem, recv_sem):
        return remote(source, target, send_sem, recv_sem, partner, z)

    att_copy.wait()
    left = jnp.concatenate(
        [att[p, near_rows, :] for p in range(pairs)] + [att_far[p] for p in range(pairs)], axis=1
    )
    acc[...] = dot(left, m_out[...])
    def lines_of(step):
        return pl.ds(pl.multiple_of(step * NORM_ROWS, NORM_ROWS), NORM_ROWS)

    def norm_first(step, carry):
        at = lines_of(step)
        near = pl.ds(pl.multiple_of(half + step * NORM_ROWS, NORM_ROWS), NORM_ROWS)
        hidden = row[near, :].astype(F32) + acc[at, :] + vectors[2]
        norm, inv_std = normed(hidden)
        norm_a[at, :] = norm
        inv_a[at, :] = jnp.broadcast_to(inv_std, (NORM_ROWS, LANES))
        middle = norm * vectors[4] + vectors[5]
        mid[at, :] = middle
        mid_low[at, :] = middle.astype(BF16)
        return carry

    lax.fori_loop(0, norm_steps, norm_first, 0, unroll=True)

    def slope_at(f):
        return f // 2, slice(f % 2 * half, (f % 2 + 1) * half)

    def activate(f):
        columns = slice(f * FF_CHUNK, (f + 1) * FF_CHUNK)
        inner = raw[f % 2][...] + bias_inner[:, columns]
        scaled = inner * 0.7071067811865476
        cdf = 0.5 + 0.5 * lax.erf(scaled)
        which, lines = slope_at(f)
        slope[which, lines, :] = cdf + scaled * 0.5641895835477563 * jnp.exp2(
            scaled * scaled * -1.4426950408889634
        )
        active[:, columns] = (inner * cdf).astype(BF16)

    raw = (raw_even, raw_odd)
    raw_even[...] = dot(mid_low[...], m_inner[0])
    for f in range(chunks):
        if f + 1 < chunks:
            raw[(f + 1) % 2][...] = dot(mid_low[...], m_inner[f + 1])
        activate(f)
    for n in range(0, width, FEATURE_CHUNK):
        acc[:, n : n + FEATURE_CHUNK] = dot(active[...], m_outer[:, n : n + FEATURE_CHUNK])

    live_end = ends[3:4, 0:1]

    def live_at(step):
        place = lax.broadcasted_iota(jnp.int32, (NORM_ROWS, 1), 0) + core * half + step * NORM_ROWS
        return (place < live_end).astype(F32)

    def norm_last(step, carry):
        at = lines_of(step)
        norm, inv_std = normed(mid[at, :] + acc[at, :] + vectors[3])
        acc[at, :] = norm
        inv_f[at, :] = jnp.broadcast_to(inv_std, (NORM_ROWS, LANES))
        layer_out[at, :] = (live_at(step) * (norm * vectors[6] + vectors[7])).astype(BF16)
        return carry

    lax.fori_loop(0, norm_steps, norm_last, 0, unroll=True)

    def home_block(block, source, target_ref, send_sem, recv_sem, local_sem):
        j = block - core * half_blocks
        src = source.at[pl.ds(pl.multiple_of(j * span, span), span)]
        line_at = z - z_half * rows

        @pl.when(block != z)
        def _():
            remote(
                src,
                target_ref.at[line_at],
                send_sem.at[j],
                recv_sem.at[line_at],
                base + z_half,
                block,
            ).start()

        @pl.when(block == z)
        def _():
            pltpu.make_async_copy(src, target_ref.at[line_at], local_sem).start()

    def home_done(source, target_ref, send_sem, recv_sem, local_sem):
        for j in range(half_blocks):
            block = core * half_blocks + j
            src = source.at[j * span : (j + 1) * span]
            line_at = z - z_half * rows

            @pl.when(block != z)
            def _():
                remote(
                    src,
                    target_ref.at[line_at],
                    send_sem.at[j],
                    recv_sem.at[line_at],
                    base + z_half,
                    block,
                ).wait_send()

            @pl.when(block == z)
            def _():
                pltpu.make_async_copy(src, target_ref.at[line_at], local_sem).wait()

        for r in range(rows):
            target = core * rows + r

            @pl.when(target != z)
            def _():
                remote(
                    source.at[0:span],
                    target_ref.at[r],
                    send_sem.at[0],
                    recv_sem.at[r],
                    base + z_half,
                    target,
                ).wait_recv()

    def send_layer_out():
        for j in range(half_blocks):
            home_block(
                core * half_blocks + j, layer_out, layer_home, lay_send, lay_recv, in_sem.at[2]
            )

    @pl.when(jnp.logical_not(gives_way))
    def _():
        send_layer_out()

    def cot_wait(j, carry):
        at = pl.ds(pl.multiple_of(j * span, span), span)
        arrived(cotangent, cot, at, core * half_blocks + j, cot_send, cot_recv, in_sem.at[1])
        return carry

    lax.fori_loop(0, half_blocks, cot_wait, 0)

    zero_sum = jnp.zeros((8, width), F32)

    def norm_last_back(step, carry):
        beta_sum, outer_sum = carry
        at = lines_of(step)
        grad_final = live_at(step) * cot[at, :].astype(F32)
        grad_hidden = norm_back(grad_final * vectors[6], acc[at, :], inv_f[at, 0:1])
        grad_h[at, :] = grad_hidden
        grad_low[at, :] = grad_hidden.astype(BF16)
        return beta_sum + fold_rows(grad_final), outer_sum + fold_rows(grad_hidden)

    sums = lax.fori_loop(0, norm_steps, norm_last_back, (zero_sum, zero_sum), unroll=True)
    beta_final_sum, outer_sum = sums

    for f in range(chunks):
        which, lines = slope_at(f)
        columns = slice(f * FF_CHUNK, (f + 1) * FF_CHUNK)
        grad_active = dot_nt(grad_low[...], m_outer[columns, :])
        grad_inner = (grad_active * slope[which, lines, :]).astype(BF16)
        active[:, columns] = grad_inner
        inner_sum[f] = fold_rows(grad_inner.astype(F32))
    for n in range(0, width, FEATURE_CHUNK):
        total = None
        for f in range(chunks):
            term = dot_nt(
                active[:, f * FF_CHUNK : (f + 1) * FF_CHUNK], m_inner[f, n : n + FEATURE_CHUNK, :]
            )
            total = term if total is None else total + term
        acc[:, n : n + FEATURE_CHUNK] = total
    @pl.when(gives_way)
    def _():
        send_layer_out()

    def norm_first_back(step, carry):
        beta_sum, out_sum = carry
        at = lines_of(step)
        grad_middle = grad_h[at, :] + acc[at, :]
        grad_hidden = norm_back(grad_middle * vectors[4], norm_a[at, :], inv_a[at, 0:1])
        grad_h[at, :] = grad_hidden
        grad_low[at, :] = grad_hidden.astype(BF16)
        return beta_sum + fold_rows(grad_middle), out_sum + fold_rows(grad_hidden)

    beta_attn_sum, out_sum = lax.fori_loop(
        0, norm_steps, norm_first_back, (zero_sum, zero_sum), unroll=True
    )

    def sum_up():
        per_line = width // FF_CHUNK
        for f in range(chunks):
            line_at = 4 + f // per_line
            column = f % per_line * FF_CHUNK
            vec_a[line_at : line_at + 1, column : column + FF_CHUNK] = jnp.sum(
                inner_sum[f], axis=0, keepdims=True
            )
        for i, lines in enumerate((out_sum, outer_sum, beta_attn_sum, beta_final_sum)):
            vec_a[i : i + 1, :] = jnp.sum(lines, axis=0, keepdims=True)
        pool_a[seq] = vec_a[:, pl.ds(pl.multiple_of(own_slice * slice_width, LANES), slice_width)]

    def send_all(start, size, here, make):
        def go(step, carry):
            make(start + lax.rem(here - start + step, size)).start()
            return carry

        lax.fori_loop(1, size, go, 0)

    def wait_all(pool, size, make):
        everything = pool.at[pl.ds(0, size - 1)]
        copy = make(everything, everything)
        copy.wait()

    def bias_copy(i, peer_seq, peer_z):
        return lambda source, target: remote(
            source, target, bias_send.at[i], bias_recv.at[i], peer_seq, peer_z
        )

    def plane_a(peer):
        piece = pl.ds(pl.multiple_of(lax.rem(peer, slices) * slice_width, LANES), slice_width)
        return bias_copy(0, peer, z)(vec_a.at[:, piece], pool_a.at[seq])

    def column_a(peer):
        return bias_copy(1, seq, peer)(z_a.at[z], z_a.at[z])

    own_slice = lax.rem(seq, slices)

    def gather_a(peer):
        return bias_copy(2, peer, z)(sums_a.at[own_slice], sums_a.at[own_slice])

    def column_b(peer):
        return bias_copy(3, seq, peer)(z_b.at[z], z_b.at[z])

    def plane_b(peer):
        return bias_copy(4, peer, z)(pool_b.at[seq], pool_b.at[seq])

    def total_of(pool, places):
        total = pool[places[0]]
        for place in places[1:]:
            total = total + pool[place]
        return total

    def gat_copy(p):
        return remote(
            grad_far.at[p], grad_att.at[p, far_rows], gat_send.at[0], gat_recv.at[0], partner, z
        )

    lines = dot_nt(grad_low[...], m_out[side:width, :])
    for p in range(pairs):
        grad_far[p] = lines[:, p * LANES : (p + 1) * LANES].astype(BF16)
        gat_copy(p).start()
    sum_up()
    send_all(0, seq_size, seq, plane_a)
    lines = dot_nt(grad_low[...], m_out[0:side, :])
    for p in range(pairs):
        grad_att[p, near_rows, :] = lines[:, p * LANES : (p + 1) * LANES].astype(BF16)

    def prepare(p, at):
        scaled = (grad_att[p, at, :].astype(F32) * recip[p, at, :]).astype(BF16)
        product = scaled.astype(F32) * mixed[p, at, :]
        half_lane = lane[at, :]
        for i in range(2):
            delta = jnp.sum(product * head_mask[i], axis=-1, keepdims=True)
            high = delta.astype(BF16).astype(F32)
            extra = jnp.where(half_lane == 0, -high, jnp.where(half_lane == 1, high - delta, 0.0))
            grads = scaled * low_mask[i]
            lefts[2 * p + i, at, :] = jnp.concatenate([grads, extra.astype(BF16)], axis=1)
        grads_turned[p, :, at] = scaled.T

    def score_grads(head, at):
        values = jnp.concatenate([vs[head // 2], ones], axis=1)
        grads = exps[head, at, :].astype(F32) * dot_nt(lefts[head, at, :], values)
        grad_scores[head, at, :] = grads.astype(BF16)
        return fold_rows(grads)

    quarter = slots // 4

    def half_of(turn):
        return 1 - z_half if turn < 2 else z_half

    home_quarter = (z - z_half * half_blocks) * span // quarter

    def quarter_of(turn):
        if turn < 2:
            return turn
        return 1 - home_quarter if turn == 2 else home_quarter

    def start_of(turn):
        return jnp.where(core == half_of(turn), half, 0) + quarter_of(turn) * quarter

    def attend_back(p, turn):
        part_of = pl.ds(pl.multiple_of(start_of(turn), quarter), quarter)
        dq = None
        dk = []
        dv = []
        for i in range(2):
            cut = slice(i * head_width, (i + 1) * head_width)
            head = 2 * p + i
            term = dot(grad_scores[head, part_of, :], ks[p] * low_mask[i])
            dq = term if dq is None else dq + term
            dk.append(dot(turned[p, cut, :], grad_scores[head, :, part_of]))
            dv.append(dot(grads_turned[p, cut, :], exps[head, :, part_of]))
        dq = (dq * score_scale).astype(BF16)
        dk = jnp.concatenate(dk, axis=0).astype(BF16).T
        dv = jnp.concatenate(dv, axis=0).astype(BF16).T
        for i, block in enumerate((dq, dk, dv)):
            grad_qkv[turn, :, i * side + p * LANES : i * side + (p + 1) * LANES] = block

    def score_grads_of(at):
        prepare(0, at)
        for p in range(pairs):
            if p + 1 < pairs:
                prepare(p + 1, at)
            for head in (2 * p, 2 * p + 1):
                sums = score_grads(head, at)
                score_sums[head] = sums if at == near_rows else score_sums[head] + sums

    def sum_up_heads():
        for p in range(pairs):
            rows_of_pair = []
            for head in (2 * p, 2 * p + 1):
                sums = score_sums[head]
                high = sums.astype(BF16)
                rows_of_pair += [high, (sums - high.astype(F32)).astype(BF16)]
            query_sum = dot(jnp.concatenate(rows_of_pair, axis=0), ks[p])
            query_sum = query_sum[0:16] * head_mask[0] + query_sum[16:32] * head_mask[1]
            z_b[z, p : p + 1, :] = jnp.sum(query_sum, axis=0, keepdims=True) * score_scale
            z_b[z, pairs + p : pairs + p + 1, :] = jnp.sum(
                fold_rows(grad_att[p].astype(F32)), axis=0, keepdims=True
            )

    score_grads_of(near_rows)
    whole(grad_far, grad_far, gat_send.at[0], gat_recv.at[0]).wait()
    score_grads_of(far_rows)
    for p in range(pairs):
        attend_back(p, 0)

    home_line = z - z_half * rows

    def part_copy(turn):
        return remote(
            part_out.at[turn], part_in.at[turn], part_send.at[turn], part_recv.at[turn], partner, z
        )

    def token_grad(turn, which):
        own = core == half_of(turn)
        columns = pl.ds(pl.multiple_of(which * side, side), side)
        near = pl.ds(pl.multiple_of(quarter_of(turn) * quarter, quarter), quarter)
        term = dot(grad_qkv[turn], turned_qkv[:, columns])
        return term + jnp.where(own, 1.0, 0.0) * grad_h[near, columns]

    def finish(turn):
        part_copy(turn).wait_recv()
        at = slice(turn * quarter, (turn + 1) * quarter)
        grad_out[at, :] = (part[turn % 2] + part_in[turn].astype(F32)).astype(BF16)
        for j in range(quarter // span):
            block = half_of(turn) * half_blocks + quarter_of(turn) * (quarter // span) + j
            source = grad_out.at[turn * quarter + j * span : turn * quarter + (j + 1) * span]
            target_ref = grad_home.at[home_line, core]
            stays = (block == z) & (core == z_half)

            @pl.when(jnp.logical_not(stays))
            def _():
                remote(
                    source,
                    target_ref,
                    grad_send.at[0],
                    grad_recv.at[home_line],
                    base + z_half,
                    block,
                ).start()

            @pl.when(stays)
            def _():
                pltpu.make_async_copy(source, target_ref, in_sem.at[3]).start()

    def grads_done():
        @pl.when(core == z_half)
        def _():
            one = grad_out.at[0:span]
            rest = grad_out.at[span:slots]
            pltpu.make_async_copy(one, one, in_sem.at[3]).wait()
            whole(rest, rest, grad_send.at[0], grad_recv.at[0]).wait_send()

        @pl.when(core != z_half)
        def _():
            whole(grad_out, grad_out, grad_send.at[0], grad_recv.at[0]).wait_send()

        for r in range(rows):
            everything = grad_home.at[r]

            @pl.when(core * rows + r != z)
            def _():
                whole(everything, everything, grad_send.at[0], grad_recv.at[r]).wait_recv()

            @pl.when(core * rows + r == z)
            def _():
                one = everything.at[0]
                whole(one, one, grad_send.at[0], grad_recv.at[r]).wait_recv()

    for turn in range(4):
        if turn > 0:
            for p in range(pairs):
                attend_back(p, turn)
        if turn > 1:
            finish(turn - 1)
        part_out[turn] = token_grad(turn, far).astype(BF16)
        part_copy(turn).start()
        part[turn % 2] = token_grad(turn, core)
        if turn == 0:
            sum_up_heads()
            send_all(0, group, z, column_b)
            wait_all(pool_a, seq_size, bias_copy(0, partner, z))
            z_a[z] = total_of(pool_a, range(seq_size))
            send_all(0, group, z, column_a)
            finish(0)
    finish(3)
    wait_all(z_a, group, bias_copy(1, partner, z))
    sums_a[own_slice] = total_of(z_a, range(group))
    send_all(seq - own_slice, slices, seq, gather_a)
    wait_all(z_b, group, bias_copy(3, partner, z))
    pool_b[seq] = total_of(z_b, range(group))
    send_all(0, seq_size, seq, plane_b)

    for turn in range(4):
        part_copy(turn).wait_send()
    wait_all(sums_a, slices, bias_copy(2, partner, z))
    wait_all(pool_b, seq_size, bias_copy(4, partner, z))
    for i in range(2):
        sums_b[i] = total_of(pool_b, range(i, seq_size, 2))
    tokens_sent()
    cotangents_sent()

    def pass_wait(j, carry):
        pass_on(j).wait_send()
        return carry

    lax.fori_loop(0, half_blocks, pass_wait, 0)
    home_done(layer_out, layer_home, lay_send, lay_recv, in_sem.at[2])
    grads_done()


def finish_kernel(
    layer,
    grad,
    sums_a,
    sums_b,
    layer_out,
    input_grad,
    grad_bias_query,
    grad_bias_value,
    grad_bias_out,
    grad_bias_inner,
    grad_bias_outer,
    grad_beta_attn,
    grad_beta_final,
    wide,
    lines,
    inner_line,
    sems,
):
    rows, span, width = layer.shape
    slices, _, slice_width = sums_a.shape
    copies = [pltpu.make_async_copy(layer, layer_out, sems.at[0])]
    copies[0].start()
    for r in range(rows):
        for c in range(2):
            wide[r, :, c * width // 2 : (c + 1) * width // 2] = grad[r, c].astype(F32)
        copies.append(pltpu.make_async_copy(wide.at[r], input_grad.at[r], sems.at[1 + r]))
        copies[-1].start()
    pairs = sums_b.shape[1] // 2
    for i in range(2):
        for p in range(pairs):
            column = (i * pairs + p) * LANES
            lines[0, :, column : column + LANES] = sums_b[i, p : p + 1, :]
            lines[1, :, column : column + LANES] = sums_b[i, pairs + p : pairs + p + 1, :]
    for j in range(slices):
        column = j * slice_width
        for i in range(4):
            lines[2 + i, :, column : column + slice_width] = sums_a[j, i : i + 1, :]
            inner_line[:, i * width + column : i * width + column + slice_width] = sums_a[
                j, 4 + i : 5 + i, :
            ]
    targets = (
        grad_bias_query,
        grad_bias_value,
        grad_bias_out,
        grad_bias_outer,
        grad_beta_attn,
        grad_beta_final,
    )
    for i, target in enumerate(targets):
        copies.append(pltpu.make_async_copy(lines.at[i], target, sems.at[1 + rows + i]))
        copies[-1].start()
    copies.append(pltpu.make_async_copy(inner_line, grad_bias_inner, sems.at[7 + rows]))
    copies[-1].start()
    for copy in copies:
        copy.wait()


def per_device(
    seq_size,
    group,
    tokens,
    doc_lengths,
    pad_counts,
    w_query,
    w_key,
    w_value,
    w_out,
    w_inner,
    w_outer,
    bias_query,
    bias_value,
    bias_out,
    bias_inner,
    bias_outer,
    gain_attn,
    beta_attn,
    gain_final,
    beta_final,
    cotangent,
):
    rows, span, width = tokens.shape
    hidden = w_inner.shape[1]
    slots = span * group
    half = slots // 2
    half_blocks = group // 2
    side = width // 2
    pairs = side // LANES
    chunks = hidden // FF_CHUNK
    slices = min(8, seq_size)
    quarter = slots // 4
    slice_width = width // slices
    if rows * 2 != group or pairs != 4 or hidden != 4 * width or slots != FF_CHUNK or quarter % span != 0:
        raise ValueError("unsupported sizes")

    any_space = pl.BlockSpec(memory_space=pl.ANY)
    vmem = pl.BlockSpec(memory_space=pltpu.VMEM)
    smem = pl.BlockSpec(memory_space=pltpu.SMEM)
    dma = pltpu.SemaphoreType.DMA
    scratch = [
        pltpu.VMEM((width, 3 * side), BF16),
        pltpu.VMEM((3 * side, width), BF16),
        pltpu.VMEM((width, width), BF16),
        pltpu.VMEM((chunks, width, FF_CHUNK), BF16),
        pltpu.VMEM((hidden, width), BF16),
        pltpu.VMEM((8, 1, width), F32),
        pltpu.VMEM((1, hidden), F32),
        pltpu.VMEM((slots, width), BF16),
        pltpu.VMEM((half, width), BF16),
        pltpu.VMEM((2, rows, 8, LANES), jnp.int32),
        pltpu.VMEM((pairs, slots, LANES), BF16),
        pltpu.VMEM((pairs, slots, LANES), BF16),
        pltpu.VMEM((pairs, slots, LANES), BF16),
        pltpu.VMEM((2 * pairs, slots, slots), BF16),
        pltpu.VMEM((pairs, slots, LANES), F32),
        pltpu.VMEM((pairs, slots, LANES), F32),
        pltpu.VMEM((pairs, slots, LANES), BF16),
        pltpu.VMEM((pairs, half, LANES), BF16),
        pltpu.VMEM((half, width), F32),
        pltpu.VMEM((half, LANES), F32),
        pltpu.VMEM((half, LANES), F32),
        pltpu.VMEM((half, width), F32),
        pltpu.VMEM((half, width), BF16),
        pltpu.VMEM((half, width), F32),
        pltpu.VMEM((chunks // 2, slots, slots), F32),
        pltpu.VMEM((half, FF_CHUNK), F32),
        pltpu.VMEM((half, FF_CHUNK), F32),
        pltpu.VMEM((half, hidden), BF16),
        pltpu.VMEM((chunks, 8, FF_CHUNK), F32),
        pltpu.VMEM((half, width), F32),
        pltpu.VMEM((half, width), BF16),
        pltpu.VMEM((pairs, slots, LANES), BF16),
        pltpu.VMEM((pairs, half, LANES), BF16),
        pltpu.VMEM((4, quarter, 3 * side), BF16),
        pltpu.VMEM((pairs, LANES, slots), BF16),
        pltpu.VMEM((2 * pairs, slots, 2 * LANES), BF16),
        pltpu.VMEM((pairs, LANES, slots), BF16),
        pltpu.VMEM((2 * pairs, slots, slots), BF16),
        pltpu.VMEM((2 * pairs, 8, slots), F32),
        pltpu.VMEM((2, quarter, side), F32),
        pltpu.VMEM((4, quarter, side), BF16),
        pltpu.VMEM((4, quarter, side), BF16),
        pltpu.VMEM((slots, side), BF16),
        pltpu.VMEM((half, width), BF16),
        pltpu.VMEM((8, width), F32),
        pltpu.VMEM((seq_size, 8, slice_width), F32),
        pltpu.VMEM((group, 8, slice_width), F32),
        pltpu.VMEM((seq_size, 8, LANES), F32),
        pltpu.VMEM((group, 8, LANES), F32),
        dma((6,)),
        dma((4,)),
        dma((rows,)),
        dma((half_blocks,)),
        dma((half_blocks,)),
        dma((half_blocks,)),
        dma((2,)),
        dma((rows,)),
        dma((half_blocks,)),
        dma((1,)),
        dma((1,)),
        dma((1,)),
        dma((1,)),
        dma((half_blocks,)),
        dma((rows,)),
        dma((4,)),
        dma((4,)),
        dma((1,)),
        dma((rows,)),
        dma((5,)),
        dma((5,)),
    ]
    vectors = (
        bias_query,
        bias_value,
        bias_out,
        bias_inner,
        bias_outer,
        gain_attn,
        beta_attn,
        gain_final,
        beta_final,
    )
    layer_home, grad_home, sums_a, sums_b = pl.pallas_call(
        functools.partial(kernel, seq_size, group),
        out_shape=(
            pltpu.VMEM(tokens.shape, BF16),
            pltpu.VMEM((rows, 2, span, side), BF16),
            pltpu.VMEM((slices, 8, slice_width), F32),
            pltpu.VMEM((2, 8, LANES), F32),
        ),
        in_specs=[any_space] * 2 + [smem] * 2 + [any_space] * (6 + len(vectors)),
        out_specs=(vmem,) * 4,
        scratch_shapes=scratch,
        compiler_params=pltpu.CompilerParams(
            collective_id=0, has_side_effects=True, vmem_limit_bytes=58 * 2**20
        ),
    )(
        tokens,
        cotangent,
        doc_lengths,
        pad_counts,
        w_query,
        w_key,
        w_value,
        w_out,
        w_inner,
        w_outer,
        *[vector.reshape(1, -1) for vector in vectors],
    )
    line = jax.ShapeDtypeStruct((1, width), F32)
    results = pl.pallas_call(
        finish_kernel,
        out_shape=(
            jax.ShapeDtypeStruct(tokens.shape, BF16),
            jax.ShapeDtypeStruct(tokens.shape, F32),
            line,
            line,
            line,
            jax.ShapeDtypeStruct((1, hidden), F32),
            line,
            line,
            line,
        ),
        in_specs=[vmem] * 4,
        out_specs=(any_space,) * 9,
        scratch_shapes=[
            pltpu.VMEM(tokens.shape, F32),
            pltpu.VMEM((6, 1, width), F32),
            pltpu.VMEM((1, hidden), F32),
            dma((8 + rows,)),
        ],
        compiler_params=pltpu.CompilerParams(vmem_limit_bytes=32 * 2**20),
    )(layer_home, grad_home, sums_a, sums_b)
    return tuple(results[:2]) + tuple(vector.reshape(-1) for vector in results[2:])


def solution(mesh):
    split = P("seq", "head", None)
    placed = (split, P("seq", None), P("seq")) + (P(),) * 15 + (split,)
    return jax.shard_map(
        functools.partial(per_device, mesh.shape["seq"], mesh.shape["head"]),
        mesh=mesh,
        in_specs=placed,
        out_specs=(split, split) + (P(),) * 7,
        check_vma=False,
    )
```
